32 devices in a mesh: factor: 4 (over y, core), load: 8 (over z, x).
Axes of the slice: x: 2, y: 2, z: 4, core: 2. Of those that a mesh axis runs over, the one named last changes fastest.
Arguments:
- b_panel: bfloat16 [2048, 2048], P('factor', 'load'), may hold values from -6 to 6
- b_update: bfloat16 [8192, 2048], P('factor', 'load'), may hold values from -6 to 6
- panel_inverse: bfloat16 [2048, 2048], P('factor'), as said below
- update_factor: bfloat16 [8192, 2048], P('factor'), may hold values from -0.125 to 0.125
- update_solution: bfloat16 [8192, 2048], P(('factor', 'load')), may hold values from -3 to 3
- axle_weights: bfloat16 [3072, 2048], P('load'), may hold values from -0.125 to 0.125
Outputs:
- update_rhs: bfloat16 [8192, 2048], P('factor', 'load')
- panel_solution: bfloat16 [2048, 2048], P('factor', 'load')
- config_response: float32 [3072, 2048], P('load', 'factor')
The draws below stay inside these ranges and needn't reach their ends.
Inputs may be any that keep to these rules, and one draw needn't show every extreme that they name: panel_inverse is zero above the diagonal and its diagonal lies between 1 and 2.
All inputs are finite; a program needn't handle non-finite values.
Results may differ from the reference program's by a relative error of at most 0.0052.
Values may be sent and summed in bfloat16 or wider, within the bound.
No kernel may reach another device: no remote copies, remote signals or barrier semaphores. Data moves between devices by JAX's collectives and lax.ppermute only.
A program may use at most 64 MiB of HBM per device.

```python
import jax
import jax.numpy as jnp
from jax import lax

PANEL = 2048
UPD = 8192
CONFIGS = 3072
COLUMNS = 2048


def draw_panel_inverse(key, part):
    first, second = jax.random.split(jax.random.fold_in(key, 11))
    lower = jax.random.normal(first, (PANEL, PANEL), jnp.float32)
    lower = lower * (1.5 / PANEL ** 0.5)
    diagonal = jax.random.uniform(second, (PANEL,), jnp.float32, 1.0, 2.0)
    rows = jnp.arange(PANEL)[:, None]
    cols = jnp.arange(PANEL)[None, :]
    whole = jnp.where(rows > cols, lower, 0.0) + jnp.where(rows == cols, diagonal[None, :], 0.0)
    return whole.astype(jnp.bfloat16)


def level_of(key, shape, cuts, least, top_value):
    def one(axis_at, blocks):
        draws = jax.random.uniform(jax.random.fold_in(jax.random.fold_in(key, 6), axis_at), (blocks,), jnp.float32, least / len(cuts), top_value / len(cuts))
        return jnp.repeat(jnp.exp(draws), shape[axis_at] // blocks).reshape((-1,) + (1,) * (len(shape) - axis_at - 1))

    factor_of = one(*cuts[0])
    for cut in cuts[1:]:
        factor_of = factor_of * one(*cut)
    return factor_of


def gaussian(rng, extent, spread, reach, cuts=(), kind=jnp.bfloat16):
    values = jax.random.normal(rng, extent, jnp.float32) * spread
    if len(cuts) > 0:
        values = level_of(rng, extent, cuts, -0.22, 0.18) * values
    return jnp.clip(values, min=-reach, max=reach).astype(kind)


def setup_inputs(seed: int = 0) -> dict:
    splits = jax.random.split(jax.random.key(seed), 7)
    return {
        "b_panel": gaussian(splits[0], (PANEL, COLUMNS), 1.0, 6.0, ((0, 4), (1, 8))),
        "b_update": gaussian(splits[1], (UPD, COLUMNS), 1.0, 6.0, ((0, 4), (1, 8))),
        "panel_inverse": draw_panel_inverse(jax.random.fold_in(splits[6], 71), 0),
        "update_factor": gaussian(splits[3], (UPD, PANEL), PANEL ** -0.5, 0.125, ((0, 4),)),
        "update_solution": gaussian(splits[4], (UPD, COLUMNS), 0.5, 3.0, ((0, 32),)),
        "axle_weights": gaussian(splits[5], (CONFIGS, COLUMNS), COLUMNS ** -0.5, 0.125, ((0, 8),)),
    }


def reference(b_panel, b_update, panel_inverse, update_factor, update_solution, axle_weights):
    forward = jnp.dot(panel_inverse, b_panel, preferred_element_type=jnp.float32).astype(jnp.bfloat16)
    lowered = jnp.dot(update_factor, forward, preferred_element_type=jnp.float32)
    update_rhs = (b_update.astype(jnp.float32) - lowered).astype(jnp.bfloat16)
    coupled = lax.dot_general(update_factor, update_solution, (((0,), (0,)), ((), ())), preferred_element_type=jnp.float32)
    reduced = (forward.astype(jnp.float32) - coupled).astype(jnp.bfloat16)
    panel_solution = lax.dot_general(panel_inverse, reduced, (((0,), (0,)), ((), ())), preferred_element_type=jnp.float32).astype(jnp.bfloat16)
    config_response = lax.dot_general(axle_weights, panel_solution, (((1,), (1,)), ((), ())), preferred_element_type=jnp.float32)
    return (update_rhs, panel_solution, config_response)
```

```python
import jax
import jax.numpy as jnp
from jax import lax
from jax.experimental import pallas as pl
from jax.experimental.pallas import tpu as pltpu
from jax.sharding import PartitionSpec as P

BF16 = jnp.bfloat16
F32 = jnp.float32


def config_kernel(at_ref, axle_ref, *refs):
    shards, out_ref = refs[:-1], refs[-1]
    cols = shards[0].shape[0]
    total = None
    for j, shard in enumerate(shards):
        block = axle_ref[:, pl.ds(pl.multiple_of(at_ref[j] * cols, cols), cols)]
        term = jnp.dot(block, shard[...], preferred_element_type=F32)
        total = term if total is None else total + term
    out_ref[...] = total


def config_of(at, axle, shards):
    configs, rows = axle.shape[0], shards[0].shape[1]
    columns = axle.shape[1]
    vmem = pl.BlockSpec(memory_space=pltpu.VMEM)
    return pl.pallas_call(
        config_kernel,
        out_shape=jax.ShapeDtypeStruct((configs, rows), F32),
        in_specs=[pl.BlockSpec(memory_space=pltpu.SMEM), vmem] + [vmem] * len(shards),
        out_specs=vmem,
        compiler_params=pltpu.CompilerParams(vmem_limit_bytes=24 * 2**20),
        cost_estimate=pl.CostEstimate(
            flops=2 * configs * rows * columns,
            bytes_accessed=2 * (configs + rows) * columns + 4 * configs * rows,
            transcendentals=0,
        ),
    )(at, axle, *shards)


def by_xor(value, axis, size, bits):
    return lax.ppermute(value, axis, [(i, i ^ bits) for i in range(size)])


def small_slice(b_panel, b_update, panel_inverse, update_factor, update_solution, axle_weights):
    factors, loads = 4, 8
    rows = panel_inverse.shape[0]
    cols = b_panel.shape[1]
    f, at_load = lax.axis_index("factor"), lax.axis_index("load")
    y, core = f // 2, f % 2

    regrouped = lax.all_to_all(update_solution, "load", split_axis=1, concat_axis=0, tiled=True)

    other_cols = lax.dynamic_slice_in_dim(panel_inverse, 0, 2 * rows, axis=1)
    inverse_other = lax.ppermute(other_cols, "factor", [(2, 0), (3, 1)])
    inverse_own = lax.dynamic_slice_in_dim(panel_inverse, y * 2 * rows, 2 * rows, axis=1)

    b_all = lax.all_gather(b_panel, "factor", axis=0, tiled=True)
    forward = jnp.dot(panel_inverse, b_all, preferred_element_type=F32).astype(BF16)
    forward_all = lax.all_gather(forward, "factor", axis=0, tiled=True)
    lowered = jnp.dot(update_factor, forward_all, preferred_element_type=F32)
    update_rhs = (b_update.astype(F32) - lowered).astype(BF16)

    coupled = lax.dot_general(
        regrouped, update_factor, (((0,), (0,)), ((), ())), preferred_element_type=F32
    ).reshape(cols, factors, rows)

    def block(b):
        return lax.dynamic_index_in_dim(coupled, b, axis=1, keepdims=False)

    send = jnp.stack([block(f ^ 1), block(f ^ 3)]).astype(BF16)
    both = by_xor(send, "factor", factors, 1).astype(F32) + jnp.stack([block(f), block(f ^ 2)])
    send = both[::-1].astype(BF16)
    both = by_xor(send, "factor", factors, 2).astype(F32) + both

    def forward_block(b):
        return lax.dynamic_slice_in_dim(forward_all, b * rows, rows, axis=0).T.astype(F32)

    reduced_own = (forward.T.astype(F32) - both[0]).astype(BF16)
    reduced_other = (forward_block(f ^ 2) - both[1]).astype(BF16)
    solved = jnp.dot(reduced_own, inverse_own, preferred_element_type=F32) + jnp.dot(
        reduced_other, inverse_other, preferred_element_type=F32
    )
    solved = solved.reshape(cols, 2, rows)
    send = lax.dynamic_index_in_dim(solved, 1 - core, axis=1, keepdims=False).astype(BF16)
    keep = lax.dynamic_index_in_dim(solved, core, axis=1, keepdims=False)
    solution_t = (keep + by_xor(send, "factor", factors, 1).astype(F32)).astype(BF16)
    panel_solution = solution_t.T

    along_z = [solution_t] + [by_xor(solution_t, "load", loads, 2 * k) for k in (1, 2, 3)]
    shards = []
    for value in along_z:
        shards += [value, by_xor(value, "load", loads, 1)]
    at = at_load ^ jnp.arange(loads, dtype=jnp.int32)
    config_response = config_of(at, axle_weights, shards)
    return (update_rhs, panel_solution, config_response)


def any_slice(b_panel, b_update, panel_inverse, update_factor, update_solution, axle_weights):
    b_all = lax.all_gather(b_panel, "factor", axis=0, tiled=True)
    forward = jnp.dot(panel_inverse, b_all, preferred_element_type=F32).astype(BF16)
    forward_all = lax.all_gather(forward, "factor", axis=0, tiled=True)
    lowered = jnp.dot(update_factor, forward_all, preferred_element_type=F32)
    update_rhs = (b_update.astype(F32) - lowered).astype(BF16)
    regrouped = lax.all_to_all(update_solution, "load", split_axis=1, concat_axis=0, tiled=True)
    over_rows = (((0,), (0,)), ((), ()))
    coupled = lax.psum_scatter(
        lax.dot_general(update_factor, regrouped, over_rows, preferred_element_type=F32),
        "factor",
        scatter_dimension=0,
        tiled=True,
    )
    reduced = (forward.astype(F32) - coupled).astype(BF16)
    panel_solution = lax.psum_scatter(
        lax.dot_general(panel_inverse, reduced, over_rows, preferred_element_type=F32),
        "factor",
        scatter_dimension=0,
        tiled=True,
    ).astype(BF16)
    config_response = lax.dot_general(
        axle_weights,
        lax.all_gather(panel_solution, "load", axis=1, tiled=True),
        (((1,), (1,)), ((), ())),
        preferred_element_type=F32,
    )
    return (update_rhs, panel_solution, config_response)


def solution(mesh):
    in_specs = (
        P("factor", "load"),
        P("factor", "load"),
        P("factor", None),
        P("factor", None),
        P(("factor", "load"), None),
        P("load", None),
    )
    out_specs = (P("factor", "load"), P("factor", "load"), P("load", "factor"))
    small = mesh.shape["factor"] == 4 and mesh.shape["load"] == 8
    local = small_slice if small else any_slice
    return jax.shard_map(local, mesh=mesh, in_specs=in_specs, out_specs=out_specs, check_vma=False)
```

```python
import jax
import jax.numpy as jnp
from jax import lax
from jax.experimental import pallas as pl
from jax.experimental.pallas import tpu as pltpu
from jax.sharding import PartitionSpec as P

BF16 = jnp.bfloat16
F32 = jnp.float32


VMEM = pl.BlockSpec(memory_space=pltpu.VMEM)
SMEM = pl.BlockSpec(memory_space=pltpu.SMEM)


def call(kernel, at, operands, outs, flops):
    shapes = [jax.ShapeDtypeStruct(shape, kind) for shape, kind in outs]
    moved = sum(v.size * v.dtype.itemsize for v in list(operands) + shapes)
    return pl.pallas_call(
        kernel,
        out_shape=shapes,
        in_specs=[SMEM] + [VMEM] * len(operands),
        out_specs=[VMEM] * len(shapes),
        compiler_params=pltpu.CompilerParams(vmem_limit_bytes=32 * 2**20),
        cost_estimate=pl.CostEstimate(flops=flops, bytes_accessed=moved, transcendentals=0),
    )(at, *operands)


def part(index, size):
    return pl.ds(pl.multiple_of(index * size, size), size)


def dot(a, b):
    return jnp.dot(a, b, preferred_element_type=F32)


def forward_kernel(at_ref, inverse_ref, *refs):
    blocks, out_ref = refs[:-1], refs[-1]
    rows = out_ref.shape[0]
    total = None
    for j, block in enumerate(blocks):
        term = dot(inverse_ref[:, part(at_ref[j], rows)], block[...])
        total = term if total is None else total + term
    out_ref[...] = total.astype(out_ref.dtype)


def update_kernel(at_ref, factor_ref, rhs_ref, *refs):
    blocks, (out_ref, turned_ref) = refs[:-2], refs[-2:]
    rows = blocks[0].shape[0]
    turned_ref[0] = blocks[0][...].T
    turned_ref[1] = blocks[2][...].T

    @pl.loop(0, out_ref.shape[0] // rows)
    def _(i):
        here = part(i, rows)
        total = rhs_ref[here, :].astype(F32)
        for j, block in enumerate(blocks):
            total = total - dot(factor_ref[here, part(at_ref[j], rows)], block[...])
        out_ref[here, :] = total.astype(out_ref.dtype)


def coupled_kernel(at_ref, factor_ref, solved_ref, out_ref):
    pieces, _, depth = solved_ref.shape
    width = out_ref.shape[2]
    for j in range(out_ref.shape[0]):
        cols = part(at_ref[j], width)
        total = None
        for k in range(pieces):
            term = dot(solved_ref[k], factor_ref[k * depth : (k + 1) * depth, cols])
            total = term if total is None else total + term
        out_ref[j] = total.astype(out_ref.dtype)


def reduce_kernel(at_ref, turned_ref, kept_ref, core_ref, across_ref, own_ref, other_ref, reduced_ref, send_ref):
    rows = send_ref.shape[1]
    for j in range(2):
        coupled = kept_ref[j] + core_ref[j].astype(F32) + across_ref[1 - j].astype(F32)
        reduced_ref[j] = (turned_ref[j].astype(F32) - coupled).astype(reduced_ref.dtype)
    solved = dot(reduced_ref[0], own_ref[:, part(at_ref[0], rows)]) + dot(
        reduced_ref[1], other_ref[:, part(at_ref[1], rows)]
    )
    send_ref[...] = solved.astype(send_ref.dtype)


def solve_kernel(at_ref, reduced_ref, own_ref, other_ref, keep_ref):
    rows = keep_ref.shape[1]
    keep_ref[...] = dot(reduced_ref[0], own_ref[:, part(at_ref[0], rows)]) + dot(
        reduced_ref[1], other_ref[:, part(at_ref[1], rows)]
    )


def config_kernel(at_ref, axle_ref, *refs):
    shards, out_ref = refs[:-1], refs[-1]
    cols = shards[0].shape[0]
    total = None
    for j, shard in enumerate(shards):
        term = dot(axle_ref[:, part(at_ref[j], cols)], shard[...])
        total = term if total is None else total + term
    out_ref[...] = total


def by_xor(value, axis, size, bits):
    return lax.ppermute(value, axis, [(i, i ^ bits) for i in range(size)])


def small_slice(b_panel, b_update, panel_inverse, update_factor, update_solution, axle_weights):
    factors, loads = 4, 8
    rows = panel_inverse.shape[0]
    updates, panel = update_factor.shape
    cols = b_panel.shape[1]
    f, at_load = lax.axis_index("factor"), lax.axis_index("load")
    core = f & 1
    at_factor = f ^ jnp.arange(factors, dtype=jnp.int32)

    turned = update_solution.T.reshape(loads, cols, update_solution.shape[0])
    regrouped = lax.all_to_all(turned, "load", split_axis=0, concat_axis=0, tiled=True)

    up, down = [(0, 2), (1, 3)], [(2, 0), (3, 1)]
    b_core = by_xor(b_panel, "factor", factors, 1)
    b_across = lax.ppermute(b_panel, "factor", up)
    b_far = lax.ppermute(b_across, "factor", [(2, 3), (3, 2)])
    inverse_other = lax.ppermute(panel_inverse[:, : 2 * rows], "factor", down)
    (forward,) = call(
        forward_kernel,
        at_factor,
        [panel_inverse, b_panel, b_core, b_across, b_far],
        [((rows, cols), BF16)],
        2 * rows * panel * cols,
    )
    forward_core = by_xor(forward, "factor", factors, 1)
    forward_across = by_xor(forward, "factor", factors, 2)
    forward_far = by_xor(forward_across, "factor", factors, 1)
    regrouped, inverse_other, forward_core, forward_across, forward_far = lax.optimization_barrier(
        (regrouped, inverse_other, forward_core, forward_across, forward_far)
    )
    update_rhs, forward_t = call(
        update_kernel,
        at_factor,
        [update_factor, b_update, forward, forward_core, forward_across, forward_far],
        [((updates, cols), BF16), ((2, cols, rows), BF16)],
        2 * updates * panel * cols,
    )

    pair = (2, cols, rows)
    half = updates * panel * cols
    (send,) = call(coupled_kernel, at_factor[1::2], [update_factor, regrouped], [(pair, BF16)], half)
    from_core = by_xor(send, "factor", factors, 1)
    (kept,) = call(coupled_kernel, at_factor[0::2], [update_factor, regrouped], [(pair, F32)], half)
    send = (kept + from_core.astype(F32)).astype(BF16)
    from_across = by_xor(send, "factor", factors, 2)

    work = 4 * cols * rows * rows
    reduced, send = call(
        reduce_kernel,
        jnp.stack([f ^ 1, core ^ 1]),
        [forward_t, kept, from_core, from_across, panel_inverse, inverse_other],
        [(pair, BF16), ((cols, rows), BF16)],
        work,
    )
    from_core = by_xor(send, "factor", factors, 1)
    (keep,) = call(
        solve_kernel,
        jnp.stack([f, core]),
        [reduced, panel_inverse, inverse_other],
        [((cols, rows), F32)],
        work,
    )
    solution_t = (keep + from_core.astype(F32)).astype(BF16)
    panel_solution = solution_t.T

    along_z = [solution_t] + [by_xor(solution_t, "load", loads, 2 * k) for k in (1, 2, 3)]
    shards = []
    for value in along_z:
        shards += [value, by_xor(value, "load", loads, 1)]
    (config_response,) = call(
        config_kernel,
        at_load ^ jnp.arange(loads, dtype=jnp.int32),
        [axle_weights] + shards,
        [((axle_weights.shape[0], rows), F32)],
        2 * axle_weights.size * rows,
    )
    return (update_rhs, panel_solution, config_response)


def any_slice(b_panel, b_update, panel_inverse, update_factor, update_solution, axle_weights):
    b_all = lax.all_gather(b_panel, "factor", axis=0, tiled=True)
    forward = jnp.dot(panel_inverse, b_all, preferred_element_type=F32).astype(BF16)
    forward_all = lax.all_gather(forward, "factor", axis=0, tiled=True)
    lowered = jnp.dot(update_factor, forward_all, preferred_element_type=F32)
    update_rhs = (b_update.astype(F32) - lowered).astype(BF16)
    regrouped = lax.all_to_all(update_solution, "load", split_axis=1, concat_axis=0, tiled=True)
    over_rows = (((0,), (0,)), ((), ()))
    coupled = lax.psum_scatter(
        lax.dot_general(update_factor, regrouped, over_rows, preferred_element_type=F32),
        "factor",
        scatter_dimension=0,
        tiled=True,
    )
    reduced = (forward.astype(F32) - coupled).astype(BF16)
    panel_solution = lax.psum_scatter(
        lax.dot_general(panel_inverse, reduced, over_rows, preferred_element_type=F32),
        "factor",
        scatter_dimension=0,
        tiled=True,
    ).astype(BF16)
    config_response = lax.dot_general(
        axle_weights,
        lax.all_gather(panel_solution, "load", axis=1, tiled=True),
        (((1,), (1,)), ((), ())),
        preferred_element_type=F32,
    )
    return (update_rhs, panel_solution, config_response)


def solution(mesh):
    in_specs = (
        P("factor", "load"),
        P("factor", "load"),
        P("factor", None),
        P("factor", None),
        P(("factor", "load"), None),
        P("load", None),
    )
    out_specs = (P("factor", "load"), P("factor", "load"), P("load", "factor"))
    small = mesh.shape["factor"] == 4 and mesh.shape["load"] == 8
    local = small_slice if small else any_slice
    return jax.shard_map(local, mesh=mesh, in_specs=in_specs, out_specs=out_specs, check_vma=False)
```

```python
import functools

import jax
import jax.numpy as jnp
from jax import lax
from jax.experimental import pallas as pl
from jax.experimental.pallas import tpu as pltpu
from jax.sharding import PartitionSpec as P

BF16 = jnp.bfloat16
F32 = jnp.float32


VMEM = pl.BlockSpec(memory_space=pltpu.VMEM)
SMEM = pl.BlockSpec(memory_space=pltpu.SMEM)


def call(kernel, at, operands, outs, flops):
    shapes = [jax.ShapeDtypeStruct(shape, kind) for shape, kind in outs]
    moved = sum(v.size * v.dtype.itemsize for v in list(operands) + shapes)
    return pl.pallas_call(
        kernel,
        out_shape=shapes,
        in_specs=[SMEM] + [VMEM] * len(operands),
        out_specs=[VMEM] * len(shapes),
        compiler_params=pltpu.CompilerParams(vmem_limit_bytes=16 * 2**20),
        cost_estimate=pl.CostEstimate(flops=flops, bytes_accessed=moved, transcendentals=0),
    )(at, *operands)


def part(index, size):
    return pl.ds(pl.multiple_of(index * size, size), size)


def dot(a, b):
    return jnp.dot(a, b, preferred_element_type=F32)


def forward_kernel(at_ref, inverse_ref, *refs):
    blocks, out_ref = refs[:-1], refs[-1]
    rows = out_ref.shape[0]
    total = None
    for j, block in enumerate(blocks):
        term = dot(inverse_ref[:, part(at_ref[j], rows)], block[...])
        total = term if total is None else total + term
    out_ref[...] = total.astype(out_ref.dtype)


def update_kernel(at_ref, factor_ref, rhs_ref, *refs):
    blocks, (out_ref, turned_ref) = refs[:-2], refs[-2:]
    rows = blocks[0].shape[0]
    turned_ref[0] = blocks[0][...].T
    turned_ref[1] = blocks[2][...].T

    @pl.loop(0, out_ref.shape[0] // rows)
    def _(i):
        here = part(i, rows)
        total = rhs_ref[here, :].astype(F32)
        for j, block in enumerate(blocks):
            total = total - dot(factor_ref[here, part(at_ref[j], rows)], block[...])
        out_ref[here, :] = total.astype(out_ref.dtype)


def split_kernel(at_ref, solved_ref, *outs):
    cols = outs[0].shape[0]
    for j, out_ref in enumerate(outs):
        out_ref[...] = solved_ref[:, part(at_ref[j], cols)].T


def hold_kernel(factor_ref, out_ref, sem):
    copy = pltpu.make_async_copy(factor_ref, out_ref, sem)
    copy.start()
    copy.wait()


def coupled_kernel(panel_blocks, row_blocks, first, at_ref, factor_ref, *refs):
    pieces, out_ref = refs[-1 - len(row_blocks) : -1], refs[-1]
    depth, width = pieces[0].shape[1], out_ref.shape[2]
    for j, b in enumerate(panel_blocks):
        cols = part(at_ref[b], width)
        total = None if first is None else refs[0][first[j]]
        for k, piece in zip(row_blocks, pieces):
            term = dot(piece[...], factor_ref[part(at_ref[k], depth), cols])
            total = term if total is None else total + term
        out_ref[j] = total.astype(out_ref.dtype)


def reduce_kernel(at_ref, turned_ref, kept_ref, core_ref, across_ref, own_ref, other_ref, reduced_ref, send_ref):
    rows = send_ref.shape[1]
    for j in range(2):
        coupled = kept_ref[j] + core_ref[j].astype(F32) + across_ref[1 - j].astype(F32)
        reduced_ref[j] = (turned_ref[j].astype(F32) - coupled).astype(reduced_ref.dtype)
    solved = dot(reduced_ref[0], own_ref[:, part(at_ref[0], rows)]) + dot(
        reduced_ref[1], other_ref[:, part(at_ref[1], rows)]
    )
    send_ref[...] = solved.astype(send_ref.dtype)


def solve_kernel(at_ref, reduced_ref, own_ref, other_ref, keep_ref):
    rows = keep_ref.shape[1]
    keep_ref[...] = dot(reduced_ref[0], own_ref[:, part(at_ref[0], rows)]) + dot(
        reduced_ref[1], other_ref[:, part(at_ref[1], rows)]
    )


def config_near_kernel(at_ref, axle_ref, *refs):
    shards, out_ref = refs[:-1], refs[-1]
    cols = shards[0].shape[0]
    total = None
    for j, shard in enumerate(shards):
        term = dot(axle_ref[:, part(at_ref[j], cols)], shard[...])
        total = term if total is None else total + term
    out_ref[...] = total


def config_far_kernel(at_ref, axle_ref, near_ref, c_ref, cx_ref, b_ref, bx_ref, e_ref, ex_ref, out_ref):
    cols = c_ref.shape[0]
    middle = at_ref[8] == 1
    total = near_ref[...]
    shards = [
        c_ref[...],
        cx_ref[...],
        jnp.where(middle, b_ref[...], e_ref[...]),
        jnp.where(middle, bx_ref[...], ex_ref[...]),
    ]
    for j, shard in enumerate(shards):
        total = total + dot(axle_ref[:, part(at_ref[4 + j], cols)], shard)
    out_ref[...] = total


def by_xor(value, axis, size, bits):
    return lax.ppermute(value, axis, [(i, i ^ bits) for i in range(size)])


def small_slice(b_panel, b_update, panel_inverse, update_factor, update_solution, axle_weights):
    factors, loads = 4, 8
    rows = panel_inverse.shape[0]
    updates, panel = update_factor.shape
    cols = b_panel.shape[1]
    f, at_load = lax.axis_index("factor"), lax.axis_index("load")
    core = f & 1
    at_factor = f ^ jnp.arange(factors, dtype=jnp.int32)

    spread = at_load ^ jnp.arange(loads, dtype=jnp.int32)

    depth = update_solution.shape[0]
    pieces = call(split_kernel, spread, [update_solution], [((cols, depth), BF16)] * loads, 0)
    near = [pieces[0]] + [by_xor(pieces[k], "load", loads, k) for k in (1, 2, 3)]
    far = [by_xor(pieces[k], "load", loads, k) for k in (4, 5, 6, 7)]
    held = pl.pallas_call(
        hold_kernel,
        out_shape=jax.ShapeDtypeStruct((updates, panel), BF16),
        in_specs=[pl.BlockSpec(memory_space=pltpu.MemorySpace.HBM)],
        out_specs=VMEM,
        scratch_shapes=[pltpu.SemaphoreType.DMA],
        compiler_params=pltpu.CompilerParams(vmem_limit_bytes=16 * 2**20),
        cost_estimate=pl.CostEstimate(flops=0, bytes_accessed=2 * updates * panel, transcendentals=0),
    )(update_factor)

    up, down = [(0, 2), (1, 3)], [(2, 0), (3, 1)]
    b_core = by_xor(b_panel, "factor", factors, 1)
    b_across = lax.ppermute(b_panel, "factor", up)
    b_far = lax.ppermute(b_across, "factor", [(2, 3), (3, 2)])
    inverse_other = lax.ppermute(panel_inverse[:, : 2 * rows], "factor", down)
    (forward,) = call(
        forward_kernel,
        at_factor,
        [panel_inverse, b_panel, b_core, b_across, b_far],
        [((rows, cols), BF16)],
        2 * rows * panel * cols,
    )
    forward_core = by_xor(forward, "factor", factors, 1)
    forward_across = by_xor(forward, "factor", factors, 2)
    forward_far = by_xor(forward_across, "factor", factors, 1)
    far[3], inverse_other, forward_core, forward_across, forward_far = lax.optimization_barrier(
        (far[3], inverse_other, forward_core, forward_across, forward_far)
    )
    update_rhs, forward_t = call(
        update_kernel,
        at_factor,
        [held, b_update, forward, forward_core, forward_across, forward_far],
        [((updates, cols), BF16), ((2, cols, rows), BF16)],
        2 * updates * panel * cols,
    )

    pair = (2, cols, rows)
    at_coupled = jnp.concatenate([at_factor, spread])

    def coupled(panel_blocks, row_blocks, first, before, blocks, kind):
        shape = (len(panel_blocks), cols, rows)
        (out,) = call(
            functools.partial(coupled_kernel, panel_blocks, row_blocks, first),
            at_coupled,
            [held] + before + blocks,
            [(shape, kind)],
            2 * cols * rows * depth * len(panel_blocks) * len(row_blocks),
        )
        return out

    begun = coupled((1, 3, 0, 2), (4, 5, 6, 7), None, [], near, F32)
    send = coupled((1, 3), (8, 9, 10, 11), (0, 1), [begun], far, BF16)
    from_core = by_xor(send, "factor", factors, 1)
    kept = coupled((0, 2), (8, 9, 10, 11), (2, 3), [begun], far, F32)
    send = (kept + from_core.astype(F32)).astype(BF16)
    from_across = by_xor(send, "factor", factors, 2)

    work = 4 * cols * rows * rows
    reduced, send = call(
        reduce_kernel,
        jnp.stack([f ^ 1, core ^ 1]),
        [forward_t, kept, from_core, from_across, panel_inverse, inverse_other],
        [(pair, BF16), ((cols, rows), BF16)],
        work,
    )
    from_core = by_xor(send, "factor", factors, 1)
    (keep,) = call(
        solve_kernel,
        jnp.stack([f, core]),
        [reduced, panel_inverse, inverse_other],
        [((cols, rows), F32)],
        work,
    )
    solution_t = (keep + from_core.astype(F32)).astype(BF16)
    panel_solution = solution_t.T

    middle, ends = (2, 3, 4, 5), (0, 1, 6, 7)

    def hop(value, places, bits):
        return lax.ppermute(value, "load", [(i, i ^ bits) for i in places])

    everyone = middle + ends
    own = solution_t
    a = hop(own, everyone, 2)
    b = hop(own, middle, 6)
    own_x = hop(own, everyone, 1)
    c = hop(a, middle, 6)
    a_x = hop(a, everyone, 1)
    d = hop(b, middle, 2)
    b_x = hop(b, middle, 1)
    e = hop(c, middle, 2)
    in_middle = (at_load >= 2) & (at_load < 6)
    c = jnp.where(in_middle, c, d)
    c_x = hop(c, everyone, 1)
    e_x = hop(e, ends, 1)

    axle_at = jnp.concatenate([spread, in_middle.astype(jnp.int32)[None]])
    response = [((axle_weights.shape[0], rows), F32)]
    work = axle_weights.size * rows
    (begun,) = call(config_near_kernel, axle_at, [axle_weights, own, own_x, a, a_x], response, work)
    (config_response,) = call(
        config_far_kernel, axle_at, [axle_weights, begun, c, c_x, b, b_x, e, e_x], response, work
    )
    return (update_rhs, panel_solution, config_response)


def any_slice(b_panel, b_update, panel_inverse, update_factor, update_solution, axle_weights):
    b_all = lax.all_gather(b_panel, "factor", axis=0, tiled=True)
    forward = jnp.dot(panel_inverse, b_all, preferred_element_type=F32).astype(BF16)
    forward_all = lax.all_gather(forward, "factor", axis=0, tiled=True)
    lowered = jnp.dot(update_factor, forward_all, preferred_element_type=F32)
    update_rhs = (b_update.astype(F32) - lowered).astype(BF16)
    regrouped = lax.all_to_all(update_solution, "load", split_axis=1, concat_axis=0, tiled=True)
    over_rows = (((0,), (0,)), ((), ()))
    coupled = lax.psum_scatter(
        lax.dot_general(update_factor, regrouped, over_rows, preferred_element_type=F32),
        "factor",
        scatter_dimension=0,
        tiled=True,
    )
    reduced = (forward.astype(F32) - coupled).astype(BF16)
    panel_solution = lax.psum_scatter(
        lax.dot_general(panel_inverse, reduced, over_rows, preferred_element_type=F32),
        "factor",
        scatter_dimension=0,
        tiled=True,
    ).astype(BF16)
    config_response = lax.dot_general(
        axle_weights,
        lax.all_gather(panel_solution, "load", axis=1, tiled=True),
        (((1,), (1,)), ((), ())),
        preferred_element_type=F32,
    )
    return (update_rhs, panel_solution, config_response)


def solution(mesh):
    in_specs = (
        P("factor", "load"),
        P("factor", "load"),
        P("factor", None),
        P("factor", None),
        P(("factor", "load"), None),
        P("load", None),
    )
    out_specs = (P("factor", "load"), P("factor", "load"), P("load", "factor"))
    small = mesh.shape["factor"] == 4 and mesh.shape["load"] == 8
    local = small_slice if small else any_slice
    return jax.shard_map(local, mesh=mesh, in_specs=in_specs, out_specs=out_specs, check_vma=False)
```

```python
import functools

import jax
import jax.numpy as jnp
from jax import lax
from jax.experimental import pallas as pl
from jax.experimental.pallas import tpu as pltpu
from jax.sharding import PartitionSpec as P

BF16 = jnp.bfloat16
F32 = jnp.float32


VMEM = pl.BlockSpec(memory_space=pltpu.VMEM)
SMEM = pl.BlockSpec(memory_space=pltpu.SMEM)


def call(kernel, at, operands, outs, flops):
    at = [] if at is None else [at]
    shapes = [jax.ShapeDtypeStruct(shape, kind) for shape, kind in outs]
    moved = sum(v.size * v.dtype.itemsize for v in list(operands) + shapes)
    return pl.pallas_call(
        kernel,
        out_shape=shapes,
        in_specs=[SMEM] * len(at) + [VMEM] * len(operands),
        out_specs=[VMEM] * len(shapes),
        compiler_params=pltpu.CompilerParams(vmem_limit_bytes=16 * 2**20),
        cost_estimate=pl.CostEstimate(flops=flops, bytes_accessed=moved, transcendentals=0),
    )(*at, *operands)


def part(index, size):
    return pl.ds(pl.multiple_of(index * size, size), size)


def dot(a, b):
    return jnp.dot(a, b, preferred_element_type=F32)


def forward_kernel(inverse_ref, b_ref, out_ref):
    out_ref[...] = dot(inverse_ref[...], b_ref[...]).astype(out_ref.dtype)


def update_kernel(factor_ref, rhs_ref, forward_ref, out_ref):
    rows = 512

    @pl.loop(0, out_ref.shape[0] // rows)
    def _(i):
        here = part(i, rows)
        total = rhs_ref[here, :].astype(F32) - dot(factor_ref[here, :], forward_ref[...])
        out_ref[here, :] = total.astype(out_ref.dtype)


def split_kernel(at_ref, solved_ref, *outs):
    cols = outs[0].shape[0]
    for j, out_ref in enumerate(outs):
        out_ref[...] = solved_ref[:, part(at_ref[j], cols)].T


def hold_kernel(factor_ref, out_ref, sem):
    copy = pltpu.make_async_copy(factor_ref, out_ref, sem)
    copy.start()
    copy.wait()


def coupled_kernel(panel_blocks, row_blocks, first, at_ref, factor_ref, *refs):
    pieces, out_ref = refs[-1 - len(row_blocks) : -1], refs[-1]
    depth, width = pieces[0].shape[1], out_ref.shape[2]
    for j, b in enumerate(panel_blocks):
        cols = part(at_ref[b], width)
        total = None if first is None else refs[0][first[j]]
        for k, piece in zip(row_blocks, pieces):
            term = dot(piece[...], factor_ref[part(at_ref[k], depth), cols])
            total = term if total is None else total + term
        out_ref[j] = total.astype(out_ref.dtype)


def reduce_kernel(at_ref, forward_ref, kept_ref, core_ref, across_ref, inverse_ref, reduced_ref, send_ref):
    rows = reduced_ref.shape[1]
    coupled = kept_ref[0] + core_ref[0].astype(F32) + across_ref[...].astype(F32)
    reduced_ref[...] = (forward_ref[...].astype(F32).T - coupled).astype(reduced_ref.dtype)
    for j, b in enumerate((1, 3)):
        send_ref[j] = dot(reduced_ref[...], inverse_ref[:, part(at_ref[b], rows)]).astype(send_ref.dtype)


def solve_kernel(at_ref, reduced_ref, inverse_ref, kept_ref):
    rows = kept_ref.shape[2]
    for j, b in enumerate((0, 2)):
        kept_ref[j] = dot(reduced_ref[...], inverse_ref[:, part(at_ref[b], rows)])


def config_kernel(first, at_ref, axle_ref, *refs):
    out_ref = refs[-1]
    total, shards = (None, refs[:-1]) if first == 0 else (refs[0][...], refs[1:-1])
    cols = shards[0].shape[0]
    for j, shard in enumerate(shards):
        term = dot(axle_ref[:, part(at_ref[first + j], cols)], shard[...])
        total = term if total is None else total + term
    out_ref[...] = total


def by_xor(value, axis, size, bits):
    return lax.ppermute(value, axis, [(i, i ^ bits) for i in range(size)])


def small_slice(b_panel, b_update, panel_inverse, update_factor, update_solution, axle_weights):
    factors, loads = 4, 8
    rows = panel_inverse.shape[0]
    updates, panel = update_factor.shape
    cols = b_panel.shape[1]
    f, at_load = lax.axis_index("factor"), lax.axis_index("load")
    at_factor = f ^ jnp.arange(factors, dtype=jnp.int32)

    spread = at_load ^ jnp.arange(loads, dtype=jnp.int32)

    depth = update_solution.shape[0]
    pieces = call(split_kernel, spread, [update_solution], [((cols, depth), BF16)] * loads, 0)
    early = [pieces[0]] + [by_xor(pieces[k], "load", loads, k) for k in (4, 5, 6)]
    late = [by_xor(pieces[k], "load", loads, k) for k in (7, 1, 2, 3)]
    held = pl.pallas_call(
        hold_kernel,
        out_shape=jax.ShapeDtypeStruct((updates, panel), BF16),
        in_specs=[pl.BlockSpec(memory_space=pltpu.MemorySpace.HBM)],
        out_specs=VMEM,
        scratch_shapes=[pltpu.SemaphoreType.DMA],
        compiler_params=pltpu.CompilerParams(vmem_limit_bytes=16 * 2**20),
        cost_estimate=pl.CostEstimate(flops=0, bytes_accessed=2 * updates * panel, transcendentals=0),
    )(update_factor)

    (forward,) = call(
        forward_kernel,
        None,
        [panel_inverse, lax.all_gather(b_panel, "factor", axis=0, tiled=True)],
        [((rows, cols), BF16)],
        2 * rows * panel * cols,
    )
    late[0], forward = lax.optimization_barrier((late[0], forward))
    forward_all = lax.all_gather(forward, "factor", axis=0, tiled=True)

    pair = (2, cols, rows)
    at_coupled = jnp.concatenate([at_factor, spread])

    def coupled(panel_blocks, row_blocks, first, before, blocks, kind):
        shape = (len(panel_blocks), cols, rows)
        (out,) = call(
            functools.partial(coupled_kernel, panel_blocks, row_blocks, first),
            at_coupled,
            [held] + before + blocks,
            [(shape, kind)],
            2 * cols * rows * depth * len(panel_blocks) * len(row_blocks),
        )
        return out

    begun = coupled((1, 3, 0, 2), (4, 8, 9, 10), None, [], early, F32)
    send = coupled((1, 3), (11, 5, 6, 7), (0, 1), [begun], late, BF16)
    from_core = by_xor(send, "factor", factors, 1)
    kept = coupled((0, 2), (11, 5, 6, 7), (2, 3), [begun], late, F32)
    send = (kept[1] + from_core[1].astype(F32)).astype(BF16)
    from_across = by_xor(send, "factor", factors, 2)
    from_across, forward_all = lax.optimization_barrier((from_across, forward_all))

    reduced, send = call(
        reduce_kernel,
        at_factor,
        [forward, kept, from_core, from_across, panel_inverse],
        [((cols, rows), BF16), (pair, BF16)],
        4 * cols * rows * rows,
    )
    from_core = by_xor(send, "factor", factors, 1)
    (kept,) = call(
        solve_kernel, at_factor, [reduced, panel_inverse], [(pair, F32)], 4 * cols * rows * rows
    )
    send = (kept[1] + from_core[1].astype(F32)).astype(BF16)
    from_across = lax.ppermute(send, "factor", [(2, 0), (3, 1)])
    (update_rhs,) = call(
        update_kernel,
        None,
        [held, b_update, forward_all],
        [((updates, cols), BF16)],
        2 * updates * panel * cols,
    )
    from_across, update_rhs = lax.optimization_barrier((from_across, update_rhs))
    solution_t = (kept[0] + from_core[0].astype(F32) + from_across.astype(F32)).astype(BF16)
    panel_solution = solution_t.T

    middle = (2, 3, 4, 5)
    own = solution_t
    own_x = by_xor(own, "load", loads, 1)
    a = by_xor(own, "load", loads, 2)
    b = by_xor(own, "load", loads, 6)
    own_x, a = lax.optimization_barrier((own_x, a))
    a_x = by_xor(a, "load", loads, 1)
    c = lax.ppermute(a, "load", [(i, i ^ 6) for i in middle])
    d = lax.ppermute(b, "load", [(i, i ^ 2) for i in middle])
    b_x = by_xor(b, "load", loads, 1)
    c = jnp.where((at_load >= 2) & (at_load < 6), c, d)
    c_x = by_xor(c, "load", loads, 1)

    axle_at = at_load ^ jnp.array([0, 1, 2, 3, 6, 7, 4, 5], jnp.int32)
    response = [((axle_weights.shape[0], rows), F32)]
    work = axle_weights.size * rows
    (begun,) = call(
        functools.partial(config_kernel, 0),
        axle_at,
        [axle_weights, own, own_x, a, a_x, b, b_x],
        response,
        3 * work // 2,
    )
    (config_response,) = call(
        functools.partial(config_kernel, 6), axle_at, [axle_weights, begun, c, c_x], response, work // 2
    )
    return (update_rhs, panel_solution, config_response)


def any_slice(b_panel, b_update, panel_inverse, update_factor, update_solution, axle_weights):
    b_all = lax.all_gather(b_panel, "factor", axis=0, tiled=True)
    forward = jnp.dot(panel_inverse, b_all, preferred_element_type=F32).astype(BF16)
    forward_all = lax.all_gather(forward, "factor", axis=0, tiled=True)
    lowered = jnp.dot(update_factor, forward_all, preferred_element_type=F32)
    update_rhs = (b_update.astype(F32) - lowered).astype(BF16)
    regrouped = lax.all_to_all(update_solution, "load", split_axis=1, concat_axis=0, tiled=True)
    over_rows = (((0,), (0,)), ((), ()))
    coupled = lax.psum_scatter(
        lax.dot_general(update_factor, regrouped, over_rows, preferred_element_type=F32),
        "factor",
        scatter_dimension=0,
        tiled=True,
    )
    reduced = (forward.astype(F32) - coupled).astype(BF16)
    panel_solution = lax.psum_scatter(
        lax.dot_general(panel_inverse, reduced, over_rows, preferred_element_type=F32),
        "factor",
        scatter_dimension=0,
        tiled=True,
    ).astype(BF16)
    config_response = lax.dot_general(
        axle_weights,
        lax.all_gather(panel_solution, "load", axis=1, tiled=True),
        (((1,), (1,)), ((), ())),
        preferred_element_type=F32,
    )
    return (update_rhs, panel_solution, config_response)


def solution(mesh):
    in_specs = (
        P("factor", "load"),
        P("factor", "load"),
        P("factor", None),
        P("factor", None),
        P(("factor", "load"), None),
        P("load", None),
    )
    out_specs = (P("factor", "load"), P("factor", "load"), P("load", "factor"))
    small = mesh.shape["factor"] == 4 and mesh.shape["load"] == 8
    local = small_slice if small else any_slice
    return jax.shard_map(local, mesh=mesh, in_specs=in_specs, out_specs=out_specs, check_vma=False)
```

```python
import functools

import jax
import jax.numpy as jnp
from jax import lax
from jax.experimental import pallas as pl
from jax.experimental.pallas import tpu as pltpu
from jax.sharding import PartitionSpec as P

BF16 = jnp.bfloat16
F32 = jnp.float32


VMEM = pl.BlockSpec(memory_space=pltpu.VMEM)
SMEM = pl.BlockSpec(memory_space=pltpu.SMEM)


def call(kernel, at, operands, outs, flops):
    at = [] if at is None else [at]
    shapes = [jax.ShapeDtypeStruct(shape, kind) for shape, kind in outs]
    moved = sum(v.size * v.dtype.itemsize for v in list(operands) + shapes)
    return pl.pallas_call(
        kernel,
        out_shape=shapes,
        in_specs=[SMEM] * len(at) + [VMEM] * len(operands),
        out_specs=[VMEM] * len(shapes),
        compiler_params=pltpu.CompilerParams(vmem_limit_bytes=16 * 2**20),
        cost_estimate=pl.CostEstimate(flops=flops, bytes_accessed=moved, transcendentals=0),
    )(*at, *operands)


def part(index, size):
    return pl.ds(pl.multiple_of(index * size, size), size)


def dot(a, b):
    return jnp.dot(a, b, preferred_element_type=F32)


def forward_kernel(at_ref, inverse_ref, *refs):
    blocks, out_ref = refs[:-1], refs[-1]
    rows = out_ref.shape[0]
    total = None
    for j, block in enumerate(blocks):
        term = dot(inverse_ref[:, part(at_ref[j], rows)], block[...])
        total = term if total is None else total + term
    out_ref[...] = total.astype(out_ref.dtype)


def update_kernel(at_ref, factor_ref, rhs_ref, *refs):
    blocks, out_ref = refs[:-1], refs[-1]
    rows = blocks[0].shape[0]

    @pl.loop(0, out_ref.shape[0] // rows)
    def _(i):
        here = part(i, rows)
        total = rhs_ref[here, :].astype(F32)
        for j, block in enumerate(blocks):
            total = total - dot(factor_ref[here, part(at_ref[j], rows)], block[...])
        out_ref[here, :] = total.astype(out_ref.dtype)


def split_kernel(at_ref, solved_ref, *outs):
    cols = outs[0].shape[0]
    for j, out_ref in enumerate(outs):
        out_ref[...] = solved_ref[:, part(at_ref[j], cols)].T


def hold_kernel(factor_ref, out_ref, sem):
    copy = pltpu.make_async_copy(factor_ref, out_ref, sem)
    copy.start()
    copy.wait()


def coupled_kernel(panel_blocks, row_blocks, first, at_ref, factor_ref, *refs):
    pieces, out_ref = refs[-1 - len(row_blocks) : -1], refs[-1]
    depth, width = pieces[0].shape[1], out_ref.shape[2]
    for j, b in enumerate(panel_blocks):
        cols = part(at_ref[b], width)
        total = None if first is None else refs[0][first[j]]
        for k, piece in zip(row_blocks, pieces):
            term = dot(piece[...], factor_ref[part(at_ref[k], depth), cols])
            total = term if total is None else total + term
        out_ref[j] = total.astype(out_ref.dtype)


def reduce_kernel(at_ref, forward_ref, kept_ref, core_ref, across_ref, inverse_ref, reduced_ref, send_ref):
    rows = reduced_ref.shape[1]
    coupled = kept_ref[0] + core_ref[0].astype(F32) + across_ref[...].astype(F32)
    reduced_ref[...] = (forward_ref[...].astype(F32).T - coupled).astype(reduced_ref.dtype)
    for j, b in enumerate((1, 3)):
        send_ref[j] = dot(reduced_ref[...], inverse_ref[:, part(at_ref[b], rows)]).astype(send_ref.dtype)


def solve_kernel(at_ref, reduced_ref, inverse_ref, kept_ref):
    rows = kept_ref.shape[2]
    for j, b in enumerate((0, 2)):
        kept_ref[j] = dot(reduced_ref[...], inverse_ref[:, part(at_ref[b], rows)])


def config_kernel(first, at_ref, axle_ref, *refs):
    out_ref = refs[-1]
    total, shards = (None, refs[:-1]) if first == 0 else (refs[0][...], refs[1:-1])
    cols = shards[0].shape[0]
    for j, shard in enumerate(shards):
        term = dot(axle_ref[:, part(at_ref[first + j], cols)], shard[...])
        total = term if total is None else total + term
    out_ref[...] = total


def by_xor(value, axis, size, bits):
    return lax.ppermute(value, axis, [(i, i ^ bits) for i in range(size)])


def small_slice(b_panel, b_update, panel_inverse, update_factor, update_solution, axle_weights):
    factors, loads = 4, 8
    rows = panel_inverse.shape[0]
    updates, panel = update_factor.shape
    cols = b_panel.shape[1]
    f, at_load = lax.axis_index("factor"), lax.axis_index("load")
    at_factor = f ^ jnp.arange(factors, dtype=jnp.int32)

    spread = at_load ^ jnp.arange(loads, dtype=jnp.int32)

    depth = update_solution.shape[0]
    pieces = call(split_kernel, spread, [update_solution], [((cols, depth), BF16)] * loads, 0)
    early, late = [pieces[0]], [by_xor(pieces[7], "load", loads, 7)]
    for k in (4, 5, 6):
        block, piece = lax.optimization_barrier((by_xor(pieces[k], "load", loads, k), pieces[k - 3]))
        early.append(block)
        late.append(by_xor(piece, "load", loads, k - 3))
    held = pl.pallas_call(
        hold_kernel,
        out_shape=jax.ShapeDtypeStruct((updates, panel), BF16),
        in_specs=[pl.BlockSpec(memory_space=pltpu.MemorySpace.HBM)],
        out_specs=VMEM,
        scratch_shapes=[pltpu.SemaphoreType.DMA],
        compiler_params=pltpu.CompilerParams(vmem_limit_bytes=16 * 2**20),
        cost_estimate=pl.CostEstimate(flops=0, bytes_accessed=2 * updates * panel, transcendentals=0),
    )(update_factor)

    b_across = lax.ppermute(b_panel, "factor", [(0, 2), (1, 3)])
    b_core = by_xor(b_panel, "factor", factors, 1)
    b_far = lax.ppermute(b_across, "factor", [(2, 3), (3, 2)])
    (forward,) = call(
        forward_kernel,
        at_factor,
        [panel_inverse, b_panel, b_core, b_across, b_far],
        [((rows, cols), BF16)],
        2 * rows * panel * cols,
    )
    late[3], forward = lax.optimization_barrier((late[3], forward))

    pair = (2, cols, rows)
    at_coupled = jnp.concatenate([at_factor, spread])

    def coupled(panel_blocks, row_blocks, first, before, blocks, kind):
        shape = (len(panel_blocks), cols, rows)
        (out,) = call(
            functools.partial(coupled_kernel, panel_blocks, row_blocks, first),
            at_coupled,
            [held] + before + blocks,
            [(shape, kind)],
            2 * cols * rows * depth * len(panel_blocks) * len(row_blocks),
        )
        return out

    begun = coupled((1, 3, 0, 2), (4, 8, 9, 10), None, [], early, F32)
    send = coupled((1, 3), (11, 5, 6, 7), (0, 1), [begun], late, BF16)
    from_core = by_xor(send, "factor", factors, 1)
    kept = coupled((0, 2), (11, 5, 6, 7), (2, 3), [begun], late, F32)
    send = (kept[1] + from_core[1].astype(F32)).astype(BF16)
    from_across = by_xor(send, "factor", factors, 2)

    reduced, send = call(
        reduce_kernel,
        at_factor,
        [forward, kept, from_core, from_across, panel_inverse],
        [((cols, rows), BF16), (pair, BF16)],
        4 * cols * rows * rows,
    )
    from_core = by_xor(send, "factor", factors, 1)
    (kept,) = call(
        solve_kernel, at_factor, [reduced, panel_inverse], [(pair, F32)], 4 * cols * rows * rows
    )
    send = (kept[1] + from_core[1].astype(F32)).astype(BF16)
    send, forward = lax.optimization_barrier((send, forward))
    from_across = lax.ppermute(send, "factor", [(2, 0), (3, 1)])
    forward_across = by_xor(forward, "factor", factors, 2)
    forward_core = by_xor(forward, "factor", factors, 1)
    forward_far = by_xor(forward_across, "factor", factors, 1)
    (update_rhs,) = call(
        update_kernel,
        at_factor,
        [held, b_update, forward, forward_core, forward_across, forward_far],
        [((updates, cols), BF16)],
        2 * updates * panel * cols,
    )
    solution_t = (kept[0] + from_core[0].astype(F32) + from_across.astype(F32)).astype(BF16)
    panel_solution = solution_t.T

    middle = (2, 3, 4, 5)
    own = solution_t
    own_x = by_xor(own, "load", loads, 1)
    a = by_xor(own, "load", loads, 2)
    b = by_xor(own, "load", loads, 6)
    own_x, a = lax.optimization_barrier((own_x, a))
    a_x = by_xor(a, "load", loads, 1)
    b, a_x = lax.optimization_barrier((b, a_x))
    c = lax.ppermute(a, "load", [(i, i ^ 6) for i in middle])
    d = lax.ppermute(b, "load", [(i, i ^ 2) for i in middle])
    b_x = by_xor(b, "load", loads, 1)
    c = jnp.where((at_load >= 2) & (at_load < 6), c, d)
    c_x = by_xor(c, "load", loads, 1)

    axle_at = at_load ^ jnp.array([0, 1, 2, 3, 6, 7, 4, 5], jnp.int32)
    response = [((axle_weights.shape[0], rows), F32)]
    work = axle_weights.size * rows
    (begun,) = call(
        functools.partial(config_kernel, 0),
        axle_at,
        [axle_weights, own, own_x, a, a_x, b, b_x],
        response,
        3 * work // 2,
    )
    (config_response,) = call(
        functools.partial(config_kernel, 6), axle_at, [axle_weights, begun, c, c_x], response, work // 2
    )
    return (update_rhs, panel_solution, config_response)


def any_slice(b_panel, b_update, panel_inverse, update_factor, update_solution, axle_weights):
    b_all = lax.all_gather(b_panel, "factor", axis=0, tiled=True)
    forward = jnp.dot(panel_inverse, b_all, preferred_element_type=F32).astype(BF16)
    forward_all = lax.all_gather(forward, "factor", axis=0, tiled=True)
    lowered = jnp.dot(update_factor, forward_all, preferred_element_type=F32)
    update_rhs = (b_update.astype(F32) - lowered).astype(BF16)
    regrouped = lax.all_to_all(update_solution, "load", split_axis=1, concat_axis=0, tiled=True)
    over_rows = (((0,), (0,)), ((), ()))
    coupled = lax.psum_scatter(
        lax.dot_general(update_factor, regrouped, over_rows, preferred_element_type=F32),
        "factor",
        scatter_dimension=0,
        tiled=True,
    )
    reduced = (forward.astype(F32) - coupled).astype(BF16)
    panel_solution = lax.psum_scatter(
        lax.dot_general(panel_inverse, reduced, over_rows, preferred_element_type=F32),
        "factor",
        scatter_dimension=0,
        tiled=True,
    ).astype(BF16)
    config_response = lax.dot_general(
        axle_weights,
        lax.all_gather(panel_solution, "load", axis=1, tiled=True),
        (((1,), (1,)), ((), ())),
        preferred_element_type=F32,
    )
    return (update_rhs, panel_solution, config_response)


def solution(mesh):
    in_specs = (
        P("factor", "load"),
        P("factor", "load"),
        P("factor", None),
        P("factor", None),
        P(("factor", "load"), None),
        P("load", None),
    )
    out_specs = (P("factor", "load"), P("factor", "load"), P("load", "factor"))
    small = mesh.shape["factor"] == 4 and mesh.shape["load"] == 8
    local = small_slice if small else any_slice
    return jax.shard_map(local, mesh=mesh, in_specs=in_specs, out_specs=out_specs, check_vma=False)
```

```python
import functools

import jax
import jax.numpy as jnp
from jax import lax
from jax.experimental import pallas as pl
from jax.experimental.pallas import tpu as pltpu
from jax.sharding import PartitionSpec as P

BF16 = jnp.bfloat16
F32 = jnp.float32


VMEM = pl.BlockSpec(memory_space=pltpu.VMEM)
SMEM = pl.BlockSpec(memory_space=pltpu.SMEM)


def call(kernel, at, operands, outs, flops):
    at = [] if at is None else [at]
    shapes = [jax.ShapeDtypeStruct(shape, kind) for shape, kind in outs]
    moved = sum(v.size * v.dtype.itemsize for v in list(operands) + shapes)
    return pl.pallas_call(
        kernel,
        out_shape=shapes,
        in_specs=[SMEM] * len(at) + [VMEM] * len(operands),
        out_specs=[VMEM] * len(shapes),
        compiler_params=pltpu.CompilerParams(vmem_limit_bytes=16 * 2**20),
        cost_estimate=pl.CostEstimate(flops=flops, bytes_accessed=moved, transcendentals=0),
    )(*at, *operands)


def part(index, size):
    return pl.ds(pl.multiple_of(index * size, size), size)


def dot(a, b):
    return jnp.dot(a, b, preferred_element_type=F32)


def forward_kernel(at_ref, inverse_ref, *refs):
    blocks, out_ref = refs[:-1], refs[-1]
    rows = out_ref.shape[0]
    total = None
    for j, block in enumerate(blocks):
        term = dot(inverse_ref[:, part(at_ref[j], rows)], block[...])
        total = term if total is None else total + term
    out_ref[...] = total.astype(out_ref.dtype)


def update_kernel(at_ref, factor_ref, rhs_ref, *refs):
    blocks, out_ref = refs[:-1], refs[-1]
    rows = blocks[0].shape[0]

    @pl.loop(0, out_ref.shape[0] // rows)
    def _(i):
        here = part(i, rows)
        total = rhs_ref[here, :].astype(F32)
        for j, block in enumerate(blocks):
            total = total - dot(factor_ref[here, part(at_ref[j], rows)], block[...])
        out_ref[here, :] = total.astype(out_ref.dtype)


def split_kernel(at_ref, solved_ref, *outs):
    cols = outs[0].shape[0]
    for j, out_ref in enumerate(outs):
        out_ref[...] = solved_ref[:, part(at_ref[j], cols)].T


def hold_kernel(factor_ref, out_ref, sem):
    copy = pltpu.make_async_copy(factor_ref, out_ref, sem)
    copy.start()
    copy.wait()


def coupled_kernel(panel_blocks, row_blocks, at_ref, factor_ref, *refs):
    pieces, out_ref = refs[:-1], refs[-1]
    depth, width = pieces[0].shape[1], out_ref.shape[2]
    for j, b in enumerate(panel_blocks):
        cols = part(at_ref[b], width)
        total = None
        for k, piece in zip(row_blocks, pieces):
            term = dot(piece[...], factor_ref[part(at_ref[k], depth), cols])
            total = term if total is None else total + term
        out_ref[j] = total


def finish_kernel(panel_block, row_blocks, at_ref, factor_ref, begun_ref, *refs):
    pieces, out_ref = refs[:-1], refs[-1]
    depth, width = pieces[0].shape[1], out_ref.shape[1]
    total = begun_ref[panel_block]
    for k, piece in zip(row_blocks, pieces):
        total = total + dot(piece[...], factor_ref[part(at_ref[k], depth), part(at_ref[panel_block], width)])
    out_ref[...] = total.astype(out_ref.dtype)


def reduce_kernel(block, at_ref, forward_ref, kept_ref, core_ref, across_ref, inverse_ref, reduced_ref, send_ref):
    rows = reduced_ref.shape[1]
    coupled = kept_ref[...] + core_ref[...].astype(F32) + across_ref[...].astype(F32)
    reduced_ref[...] = (forward_ref[...].astype(F32).T - coupled).astype(reduced_ref.dtype)
    term = dot(reduced_ref[...], inverse_ref[:, part(at_ref[block], rows)])
    send_ref[...] = term.astype(send_ref.dtype)


def solve_kernel(block, at_ref, reduced_ref, inverse_ref, out_ref):
    term = dot(reduced_ref[...], inverse_ref[:, part(at_ref[block], out_ref.shape[1])])
    out_ref[...] = term.astype(out_ref.dtype)


def config_near_kernel(at_ref, axle_ref, *refs):
    shards, out_ref = refs[:-1], refs[-1]
    cols = shards[0].shape[0]
    total = None
    for j, shard in enumerate(shards):
        term = dot(axle_ref[:, part(at_ref[j], cols)], shard[...])
        total = term if total is None else total + term
    out_ref[...] = total


def config_far_kernel(at_ref, axle_ref, near_ref, c_ref, d_ref, cx_ref, dx_ref, out_ref):
    cols = c_ref.shape[0]
    middle = at_ref[8] == 1
    total = near_ref[...]
    for j, pair in ((6, (c_ref, d_ref)), (7, (cx_ref, dx_ref))):
        shard = jnp.where(middle, pair[0][...], pair[1][...])
        total = total + dot(axle_ref[:, part(at_ref[j], cols)], shard)
    out_ref[...] = total


def by_xor(value, axis, size, bits):
    return lax.ppermute(value, axis, [(i, i ^ bits) for i in range(size)])


def small_slice(b_panel, b_update, panel_inverse, update_factor, update_solution, axle_weights):
    factors, loads = 4, 8
    rows = panel_inverse.shape[0]
    updates, panel = update_factor.shape
    cols = b_panel.shape[1]
    f, at_load = lax.axis_index("factor"), lax.axis_index("load")
    at_factor = f ^ jnp.arange(factors, dtype=jnp.int32)

    spread = at_load ^ jnp.arange(loads, dtype=jnp.int32)

    depth = update_solution.shape[0]
    pieces = call(split_kernel, spread, [update_solution], [((cols, depth), BF16)] * loads, 0)
    *pieces, b_panel = lax.optimization_barrier((*pieces, b_panel))
    early, late = [pieces[0]], [by_xor(pieces[7], "load", loads, 7)]
    for k in (4, 5, 6):
        block, piece = lax.optimization_barrier((by_xor(pieces[k], "load", loads, k), pieces[k - 3]))
        early.append(block)
        late.append(by_xor(piece, "load", loads, k - 3))
    held = pl.pallas_call(
        hold_kernel,
        out_shape=jax.ShapeDtypeStruct((updates, panel), BF16),
        in_specs=[pl.BlockSpec(memory_space=pltpu.MemorySpace.HBM)],
        out_specs=VMEM,
        scratch_shapes=[pltpu.SemaphoreType.DMA],
        compiler_params=pltpu.CompilerParams(vmem_limit_bytes=16 * 2**20),
        cost_estimate=pl.CostEstimate(flops=0, bytes_accessed=2 * updates * panel, transcendentals=0),
    )(update_factor)

    b_across = lax.ppermute(b_panel, "factor", [(0, 2), (1, 3)])
    b_core = by_xor(b_panel, "factor", factors, 1)
    b_far = lax.ppermute(b_panel, "factor", [(0, 3), (1, 2)])
    (forward,) = call(
        forward_kernel,
        at_factor,
        [panel_inverse, b_panel, b_core, b_across, b_far],
        [((rows, cols), BF16)],
        2 * rows * panel * cols,
    )
    forward_across = by_xor(forward, "factor", factors, 2)
    late[3], forward_across = lax.optimization_barrier((late[3], forward_across))

    block = (cols, rows)
    at_coupled = jnp.concatenate([at_factor, spread])
    (begun,) = call(
        functools.partial(coupled_kernel, (0, 1, 2, 3), (4, 8, 9, 10)),
        at_coupled,
        [held] + early,
        [((factors,) + block, F32)],
        2 * cols * depth * 4 * panel,
    )

    def coupled(panel_block, kind):
        (out,) = call(
            functools.partial(finish_kernel, panel_block, (11, 5, 6, 7)),
            at_coupled,
            [held, begun] + late,
            [(block, kind)],
            2 * cols * depth * 4 * rows,
        )
        return out

    from_core = by_xor(coupled(3, BF16), "factor", factors, 1)
    send = (coupled(2, F32) + from_core.astype(F32)).astype(BF16)
    from_across = by_xor(send, "factor", factors, 2)
    from_core = by_xor(coupled(1, BF16), "factor", factors, 1)
    kept = coupled(0, F32)

    work = 2 * cols * rows * rows
    reduced, send = call(
        functools.partial(reduce_kernel, 3),
        at_factor,
        [forward, kept, from_core, from_across, panel_inverse],
        [(block, BF16), (block, BF16)],
        work,
    )

    def solved(panel_block, kind):
        (out,) = call(
            functools.partial(solve_kernel, panel_block),
            at_factor,
            [reduced, panel_inverse],
            [(block, kind)],
            work,
        )
        return out

    from_core = by_xor(send, "factor", factors, 1)
    send = (solved(2, F32) + from_core.astype(F32)).astype(BF16)
    from_across = lax.ppermute(send, "factor", [(2, 0), (3, 1)])
    from_core = by_xor(solved(1, BF16), "factor", factors, 1)
    kept = solved(0, F32)
    forward_core = by_xor(forward, "factor", factors, 1)
    forward_far = by_xor(forward_across, "factor", factors, 1)
    (update_rhs,) = call(
        update_kernel,
        at_factor,
        [held, b_update, forward, forward_core, forward_across, forward_far],
        [((updates, cols), BF16)],
        2 * updates * panel * cols,
    )
    from_across, update_rhs = lax.optimization_barrier((from_across, update_rhs))
    solution_t = (kept + from_core.astype(F32) + from_across.astype(F32)).astype(BF16)
    panel_solution = solution_t.T

    middle = (2, 3, 4, 5)
    own = solution_t
    own_x = by_xor(own, "load", loads, 1)
    a = by_xor(own, "load", loads, 2)
    b = by_xor(own, "load", loads, 6)
    own_x, a = lax.optimization_barrier((own_x, a))
    a_x = by_xor(a, "load", loads, 1)
    b, a_x = lax.optimization_barrier((b, a_x))
    c = lax.ppermute(a, "load", [(i, i ^ 6) for i in middle])
    d = lax.ppermute(b, "load", [(i, i ^ 2) for i in middle])
    b_x = by_xor(b, "load", loads, 1)
    c_x = lax.ppermute(c, "load", [(i, i ^ 1) for i in middle])
    d_x = lax.ppermute(d, "load", [(i, i ^ 1) for i in (0, 1, 6, 7)])

    in_middle = ((at_load >= 2) & (at_load < 6)).astype(jnp.int32)
    at_axle = jnp.concatenate([at_load ^ jnp.array([0, 1, 2, 3, 6, 7, 4, 5], jnp.int32), in_middle[None]])
    response = [((axle_weights.shape[0], rows), F32)]
    work = axle_weights.size * rows
    (begun,) = call(
        config_near_kernel, at_axle, [axle_weights, own, own_x, a, a_x, b, b_x], response, 3 * work // 2
    )
    (config_response,) = call(
        config_far_kernel, at_axle, [axle_weights, begun, c, d, c_x, d_x], response, work // 2
    )
    return (update_rhs, panel_solution, config_response)


def any_slice(b_panel, b_update, panel_inverse, update_factor, update_solution, axle_weights):
    b_all = lax.all_gather(b_panel, "factor", axis=0, tiled=True)
    forward = jnp.dot(panel_inverse, b_all, preferred_element_type=F32).astype(BF16)
    forward_all = lax.all_gather(forward, "factor", axis=0, tiled=True)
    lowered = jnp.dot(update_factor, forward_all, preferred_element_type=F32)
    update_rhs = (b_update.astype(F32) - lowered).astype(BF16)
    regrouped = lax.all_to_all(update_solution, "load", split_axis=1, concat_axis=0, tiled=True)
    over_rows = (((0,), (0,)), ((), ()))
    coupled = lax.psum_scatter(
        lax.dot_general(update_factor, regrouped, over_rows, preferred_element_type=F32),
        "factor",
        scatter_dimension=0,
        tiled=True,
    )
    reduced = (forward.astype(F32) - coupled).astype(BF16)
    panel_solution = lax.psum_scatter(
        lax.dot_general(panel_inverse, reduced, over_rows, preferred_element_type=F32),
        "factor",
        scatter_dimension=0,
        tiled=True,
    ).astype(BF16)
    config_response = lax.dot_general(
        axle_weights,
        lax.all_gather(panel_solution, "load", axis=1, tiled=True),
        (((1,), (1,)), ((), ())),
        preferred_element_type=F32,
    )
    return (update_rhs, panel_solution, config_response)


def solution(mesh):
    in_specs = (
        P("factor", "load"),
        P("factor", "load"),
        P("factor", None),
        P("factor", None),
        P(("factor", "load"), None),
        P("load", None),
    )
    out_specs = (P("factor", "load"), P("factor", "load"), P("load", "factor"))
    small = mesh.shape["factor"] == 4 and mesh.shape["load"] == 8
    local = small_slice if small else any_slice
    return jax.shard_map(local, mesh=mesh, in_specs=in_specs, out_specs=out_specs, check_vma=False)
```

```python
import functools

import jax
import jax.numpy as jnp
from jax import lax
from jax.experimental import pallas as pl
from jax.experimental.pallas import tpu as pltpu
from jax.sharding import PartitionSpec as P

BF16 = jnp.bfloat16
F32 = jnp.float32


VMEM = pl.BlockSpec(memory_space=pltpu.VMEM)
SMEM = pl.BlockSpec(memory_space=pltpu.SMEM)


def call(kernel, at, operands, outs, flops):
    at = [] if at is None else [at]
    shapes = [jax.ShapeDtypeStruct(shape, kind) for shape, kind in outs]
    moved = sum(v.size * v.dtype.itemsize for v in list(operands) + shapes)
    return pl.pallas_call(
        kernel,
        out_shape=shapes,
        in_specs=[SMEM] * len(at) + [VMEM] * len(operands),
        out_specs=[VMEM] * len(shapes),
        compiler_params=pltpu.CompilerParams(vmem_limit_bytes=16 * 2**20),
        cost_estimate=pl.CostEstimate(flops=flops, bytes_accessed=moved, transcendentals=0),
    )(*at, *operands)


def part(index, size):
    return pl.ds(pl.multiple_of(index * size, size), size)


def dot(a, b):
    return jnp.dot(a, b, preferred_element_type=F32)


def forward_kernel(at_ref, inverse_ref, *refs):
    blocks, out_ref = refs[:-1], refs[-1]
    rows = out_ref.shape[0]
    total = None
    for j, block in enumerate(blocks):
        term = dot(inverse_ref[:, part(at_ref[j], rows)], block[...])
        total = term if total is None else total + term
    out_ref[...] = total.astype(out_ref.dtype)


def update_kernel(at_ref, factor_ref, rhs_ref, *refs):
    blocks, out_ref = refs[:-1], refs[-1]
    rows = blocks[0].shape[0]

    @pl.loop(0, out_ref.shape[0] // rows)
    def _(i):
        here = part(i, rows)
        total = rhs_ref[here, :].astype(F32)
        for j, block in enumerate(blocks):
            total = total - dot(factor_ref[here, part(at_ref[j], rows)], block[...])
        out_ref[here, :] = total.astype(out_ref.dtype)


def split_kernel(at_ref, solved_ref, *outs):
    cols = outs[0].shape[0]
    for j, out_ref in enumerate(outs):
        out_ref[...] = solved_ref[:, part(at_ref[j], cols)].T


def hold_kernel(factor_ref, out_ref, sem):
    copy = pltpu.make_async_copy(factor_ref, out_ref, sem)
    copy.start()
    copy.wait()


def coupled_kernel(panel_blocks, row_blocks, at_ref, factor_ref, *refs):
    pieces, out_ref = refs[:-1], refs[-1]
    depth, width = pieces[0].shape[1], out_ref.shape[2]
    for j, b in enumerate(panel_blocks):
        cols = part(at_ref[b], width)
        total = None
        for k, piece in zip(row_blocks, pieces):
            term = dot(piece[...], factor_ref[part(at_ref[k], depth), cols])
            total = term if total is None else total + term
        out_ref[j] = total


def finish_kernel(panel_block, row_blocks, at_ref, factor_ref, begun_ref, *refs):
    pieces, out_ref = refs[:-1], refs[-1]
    depth, width = pieces[0].shape[1], out_ref.shape[1]
    total = begun_ref[panel_block]
    for k, piece in zip(row_blocks, pieces):
        total = total + dot(piece[...], factor_ref[part(at_ref[k], depth), part(at_ref[panel_block], width)])
    out_ref[...] = total.astype(out_ref.dtype)


def reduce_kernel(block, at_ref, forward_ref, kept_ref, core_ref, across_ref, inverse_ref, reduced_ref, send_ref):
    rows = reduced_ref.shape[1]
    coupled = kept_ref[...] + core_ref[...].astype(F32) + across_ref[...].astype(F32)
    reduced_ref[...] = (forward_ref[...].astype(F32).T - coupled).astype(reduced_ref.dtype)
    term = dot(reduced_ref[...], inverse_ref[:, part(at_ref[block], rows)])
    send_ref[...] = term.astype(send_ref.dtype)


def solve_kernel(block, at_ref, reduced_ref, inverse_ref, out_ref):
    term = dot(reduced_ref[...], inverse_ref[:, part(at_ref[block], out_ref.shape[1])])
    out_ref[...] = term.astype(out_ref.dtype)


def config_kernel(first, at_ref, axle_ref, *refs):
    out_ref = refs[-1]
    total, shards = (None, refs[:-1]) if first == 0 else (refs[0][...], refs[1:-1])
    cols = shards[0].shape[0]
    middle = at_ref[8] == 1
    singles = 4 if first == 0 else 0
    values = [shard[...] for shard in shards[:singles]]
    for inner, outer in zip(shards[singles::2], shards[singles + 1 :: 2]):
        values.append(jnp.where(middle, inner[...], outer[...]))
    for j, value in enumerate(values):
        term = dot(axle_ref[:, part(at_ref[first + j], cols)], value)
        total = term if total is None else total + term
    out_ref[...] = total


def by_xor(value, axis, size, bits):
    return lax.ppermute(value, axis, [(i, i ^ bits) for i in range(size)])


def small_slice(b_panel, b_update, panel_inverse, update_factor, update_solution, axle_weights):
    factors, loads = 4, 8
    rows = panel_inverse.shape[0]
    updates, panel = update_factor.shape
    cols = b_panel.shape[1]
    f, at_load = lax.axis_index("factor"), lax.axis_index("load")
    at_factor = f ^ jnp.arange(factors, dtype=jnp.int32)

    spread = at_load ^ jnp.arange(loads, dtype=jnp.int32)

    depth = update_solution.shape[0]
    pieces = call(split_kernel, spread, [update_solution], [((cols, depth), BF16)] * loads, 0)
    *pieces, b_panel = lax.optimization_barrier((*pieces, b_panel))
    far = [by_xor(pieces[k], "load", loads, k) for k in (4, 5, 6, 7)]
    far[0], pieces[1] = lax.optimization_barrier((far[0], pieces[1]))
    far[1], pieces[2] = lax.optimization_barrier((far[1], pieces[2]))
    far[2], far[3], pieces[3] = lax.optimization_barrier((far[2], far[3], pieces[3]))
    early = [pieces[0]] + far
    late = [by_xor(pieces[k], "load", loads, k) for k in (1, 2, 3)]
    held = pl.pallas_call(
        hold_kernel,
        out_shape=jax.ShapeDtypeStruct((updates, panel), BF16),
        in_specs=[pl.BlockSpec(memory_space=pltpu.MemorySpace.HBM)],
        out_specs=VMEM,
        scratch_shapes=[pltpu.SemaphoreType.DMA],
        compiler_params=pltpu.CompilerParams(vmem_limit_bytes=16 * 2**20),
        cost_estimate=pl.CostEstimate(flops=0, bytes_accessed=2 * updates * panel, transcendentals=0),
    )(update_factor)

    b_across = lax.ppermute(b_panel, "factor", [(0, 2), (1, 3)])
    b_core = by_xor(b_panel, "factor", factors, 1)
    b_far = lax.ppermute(b_panel, "factor", [(0, 3), (1, 2)])
    b_far, held = lax.optimization_barrier((b_far, held))
    (forward,) = call(
        forward_kernel,
        at_factor,
        [panel_inverse, b_panel, b_core, b_across, b_far],
        [((rows, cols), BF16)],
        2 * rows * panel * cols,
    )
    forward_across = by_xor(forward, "factor", factors, 2)
    late[2], forward_across = lax.optimization_barrier((late[2], forward_across))

    block = (cols, rows)
    at_coupled = jnp.concatenate([at_factor, spread])
    (begun,) = call(
        functools.partial(coupled_kernel, (0, 1, 2, 3), (4, 8, 9, 10, 11)),
        at_coupled,
        [held] + early,
        [((factors,) + block, F32)],
        2 * cols * depth * 5 * panel,
    )

    def coupled(panel_block, kind):
        (out,) = call(
            functools.partial(finish_kernel, panel_block, (5, 6, 7)),
            at_coupled,
            [held, begun] + late,
            [(block, kind)],
            2 * cols * depth * 3 * rows,
        )
        return out

    from_core = by_xor(coupled(3, BF16), "factor", factors, 1)
    send = (coupled(2, F32) + from_core.astype(F32)).astype(BF16)
    from_across = by_xor(send, "factor", factors, 2)
    from_core = by_xor(coupled(1, BF16), "factor", factors, 1)
    kept = coupled(0, F32)

    work = 2 * cols * rows * rows
    reduced, send = call(
        functools.partial(reduce_kernel, 3),
        at_factor,
        [forward, kept, from_core, from_across, panel_inverse],
        [(block, BF16), (block, BF16)],
        work,
    )

    def solved(panel_block, kind):
        (out,) = call(
            functools.partial(solve_kernel, panel_block),
            at_factor,
            [reduced, panel_inverse],
            [(block, kind)],
            work,
        )
        return out

    from_core = by_xor(send, "factor", factors, 1)
    send = (solved(2, F32) + from_core.astype(F32)).astype(BF16)
    from_across = lax.ppermute(send, "factor", [(2, 0), (3, 1)])
    from_core = by_xor(solved(1, BF16), "factor", factors, 1)
    kept = solved(0, F32)
    forward_core = by_xor(forward, "factor", factors, 1)
    forward_far = by_xor(forward_across, "factor", factors, 1)
    (update_rhs,) = call(
        update_kernel,
        at_factor,
        [held, b_update, forward, forward_core, forward_across, forward_far],
        [((updates, cols), BF16)],
        2 * updates * panel * cols,
    )
    from_across, update_rhs = lax.optimization_barrier((from_across, update_rhs))
    solution_t = (kept + from_core.astype(F32) + from_across.astype(F32)).astype(BF16)
    panel_solution = solution_t.T

    middle, ends = (2, 3, 4, 5), (0, 1, 6, 7)

    def hop(value, places, bits):
        return lax.ppermute(value, "load", [(i, i ^ bits) for i in places])

    own = solution_t
    b = hop(own, middle, 6)
    a = hop(own, middle + ends, 2)
    own_x = hop(own, middle + ends, 1)
    b, a, own_x = lax.optimization_barrier((b, a, own_x))
    c = hop(a, middle, 6)
    d = hop(b, middle, 2)
    a_x = hop(a, middle + ends, 1)
    b_x = hop(b, middle, 1)
    e = hop(own, ends, 6)
    c_x = hop(c, middle, 1)
    d_x = hop(d, ends, 1)
    e_x = hop(e, ends, 1)

    in_middle = ((at_load >= 2) & (at_load < 6)).astype(jnp.int32)
    at_axle = jnp.concatenate([at_load ^ jnp.array([0, 1, 2, 3, 4, 6, 5, 7], jnp.int32), in_middle[None]])
    response = [((axle_weights.shape[0], rows), F32)]
    work = axle_weights.size * rows // 4
    (begun,) = call(
        functools.partial(config_kernel, 0),
        at_axle,
        [axle_weights, own, own_x, a, a_x, c, d, b, e],
        response,
        6 * work,
    )
    (config_response,) = call(
        functools.partial(config_kernel, 6),
        at_axle,
        [axle_weights, begun, c_x, d_x, b_x, e_x],
        response,
        2 * work,
    )
    return (update_rhs, panel_solution, config_response)


def any_slice(b_panel, b_update, panel_inverse, update_factor, update_solution, axle_weights):
    b_all = lax.all_gather(b_panel, "factor", axis=0, tiled=True)
    forward = jnp.dot(panel_inverse, b_all, preferred_element_type=F32).astype(BF16)
    forward_all = lax.all_gather(forward, "factor", axis=0, tiled=True)
    lowered = jnp.dot(update_factor, forward_all, preferred_element_type=F32)
    update_rhs = (b_update.astype(F32) - lowered).astype(BF16)
    regrouped = lax.all_to_all(update_solution, "load", split_axis=1, concat_axis=0, tiled=True)
    over_rows = (((0,), (0,)), ((), ()))
    coupled = lax.psum_scatter(
        lax.dot_general(update_factor, regrouped, over_rows, preferred_element_type=F32),
        "factor",
        scatter_dimension=0,
        tiled=True,
    )
    reduced = (forward.astype(F32) - coupled).astype(BF16)
    panel_solution = lax.psum_scatter(
        lax.dot_general(panel_inverse, reduced, over_rows, preferred_element_type=F32),
        "factor",
        scatter_dimension=0,
        tiled=True,
    ).astype(BF16)
    config_response = lax.dot_general(
        axle_weights,
        lax.all_gather(panel_solution, "load", axis=1, tiled=True),
        (((1,), (1,)), ((), ())),
        preferred_element_type=F32,
    )
    return (update_rhs, panel_solution, config_response)


def solution(mesh):
    in_specs = (
        P("factor", "load"),
        P("factor", "load"),
        P("factor", None),
        P("factor", None),
        P(("factor", "load"), None),
        P("load", None),
    )
    out_specs = (P("factor", "load"), P("factor", "load"), P("load", "factor"))
    small = mesh.shape["factor"] == 4 and mesh.shape["load"] == 8
    local = small_slice if small else any_slice
    return jax.shard_map(local, mesh=mesh, in_specs=in_specs, out_specs=out_specs, check_vma=False)
```

```python
import functools

import jax
import jax.numpy as jnp
from jax import lax
from jax.experimental import pallas as pl
from jax.experimental.pallas import tpu as pltpu
from jax.sharding import PartitionSpec as P

BF16 = jnp.bfloat16
F32 = jnp.float32


VMEM = pl.BlockSpec(memory_space=pltpu.VMEM)
SMEM = pl.BlockSpec(memory_space=pltpu.SMEM)


def call(kernel, at, operands, outs, flops):
    at = [] if at is None else [at]
    shapes = [jax.ShapeDtypeStruct(shape, kind) for shape, kind in outs]
    moved = sum(v.size * v.dtype.itemsize for v in list(operands) + shapes)
    return pl.pallas_call(
        kernel,
        out_shape=shapes,
        in_specs=[SMEM] * len(at) + [VMEM] * len(operands),
        out_specs=[VMEM] * len(shapes),
        compiler_params=pltpu.CompilerParams(vmem_limit_bytes=16 * 2**20),
        cost_estimate=pl.CostEstimate(flops=flops, bytes_accessed=moved, transcendentals=0),
    )(*at, *operands)


def part(index, size):
    return pl.ds(pl.multiple_of(index * size, size), size)


def dot(a, b):
    return jnp.dot(a, b, preferred_element_type=F32)


def forward_kernel(at_ref, inverse_ref, *refs):
    blocks, out_ref = refs[:-1], refs[-1]
    rows = out_ref.shape[0]
    total = None
    for j, block in enumerate(blocks):
        term = dot(inverse_ref[:, part(at_ref[j], rows)], block[...])
        total = term if total is None else total + term
    out_ref[...] = total.astype(out_ref.dtype)


def update_kernel(at_ref, factor_ref, rhs_ref, *refs):
    blocks, out_ref = refs[:-1], refs[-1]
    rows = blocks[0].shape[0]

    @pl.loop(0, out_ref.shape[0] // rows)
    def _(i):
        here = part(i, rows)
        total = rhs_ref[here, :].astype(F32)
        for j, block in enumerate(blocks):
            total = total - dot(factor_ref[here, part(at_ref[j], rows)], block[...])
        out_ref[here, :] = total.astype(out_ref.dtype)


def split_kernel(at_ref, solved_ref, *outs):
    cols = outs[0].shape[0]
    for j, out_ref in enumerate(outs):
        out_ref[...] = solved_ref[:, part(at_ref[j], cols)].T


def hold_kernel(factor_ref, out_ref, sem):
    copy = pltpu.make_async_copy(factor_ref, out_ref, sem)
    copy.start()
    copy.wait()


def coupled_kernel(panel_blocks, row_blocks, at_ref, factor_ref, *refs):
    pieces, out_ref = refs[:-1], refs[-1]
    depth, width = pieces[0].shape[1], out_ref.shape[2]
    for j, b in enumerate(panel_blocks):
        cols = part(at_ref[b], width)
        total = None
        for k, piece in zip(row_blocks, pieces):
            term = dot(piece[...], factor_ref[part(at_ref[k], depth), cols])
            total = term if total is None else total + term
        out_ref[j] = total


def finish_kernel(panel_block, row_blocks, at_ref, factor_ref, begun_ref, *refs):
    pieces, out_ref = refs[:-1], refs[-1]
    depth, width = pieces[0].shape[1], out_ref.shape[1]
    total = begun_ref[panel_block]
    for k, piece in zip(row_blocks, pieces):
        total = total + dot(piece[...], factor_ref[part(at_ref[k], depth), part(at_ref[panel_block], width)])
    out_ref[...] = total.astype(out_ref.dtype)


def reduce_kernel(block, at_ref, forward_ref, kept_ref, core_ref, across_ref, inverse_ref, reduced_ref, send_ref):
    rows = reduced_ref.shape[1]
    coupled = kept_ref[...] + core_ref[...].astype(F32) + across_ref[...].astype(F32)
    reduced_ref[...] = (forward_ref[...].astype(F32).T - coupled).astype(reduced_ref.dtype)
    term = dot(reduced_ref[...], inverse_ref[:, part(at_ref[block], rows)])
    send_ref[...] = term.astype(send_ref.dtype)


def solve_kernel(block, at_ref, reduced_ref, inverse_ref, *outs):
    width = outs[0].shape[1]
    for k, out_ref in enumerate(outs):
        term = dot(reduced_ref[...], inverse_ref[:, part(at_ref[block] * len(outs) + k, width)])
        out_ref[...] = term.astype(out_ref.dtype)


def config_kernel(first, joined, at_ref, axle_ref, *refs):
    refs, out_ref = list(refs[:-1]), refs[-1]
    total = None if first == 0 else refs.pop(0)[...]
    if joined:
        half = refs.pop(0)
        out_ref[:, : half.shape[1]] = half[...]
    cols, width = refs[0].shape
    for j, shard in enumerate(refs):
        term = dot(axle_ref[:, part(at_ref[first + j], cols)], shard[...])
        total = term if total is None else total + term
    out_ref[:, out_ref.shape[1] - width :] = total


def by_xor(value, axis, size, bits):
    return lax.ppermute(value, axis, [(i, i ^ bits) for i in range(size)])


def small_slice(b_panel, b_update, panel_inverse, update_factor, update_solution, axle_weights):
    factors, loads = 4, 8
    rows = panel_inverse.shape[0]
    updates, panel = update_factor.shape
    cols = b_panel.shape[1]
    f, at_load = lax.axis_index("factor"), lax.axis_index("load")
    at_factor = f ^ jnp.arange(factors, dtype=jnp.int32)

    spread = at_load ^ jnp.arange(loads, dtype=jnp.int32)

    depth = update_solution.shape[0]
    pieces = call(split_kernel, spread, [update_solution], [((cols, depth), BF16)] * loads, 0)
    *pieces, b_panel = lax.optimization_barrier((*pieces, b_panel))
    early, late = [pieces[0]], [by_xor(pieces[7], "load", loads, 7)]
    for k in (4, 5, 6):
        block, piece = lax.optimization_barrier((by_xor(pieces[k], "load", loads, k), pieces[k - 3]))
        early.append(block)
        late.append(by_xor(piece, "load", loads, k - 3))
    held = pl.pallas_call(
        hold_kernel,
        out_shape=jax.ShapeDtypeStruct((updates, panel), BF16),
        in_specs=[pl.BlockSpec(memory_space=pltpu.MemorySpace.HBM)],
        out_specs=VMEM,
        scratch_shapes=[pltpu.SemaphoreType.DMA],
        compiler_params=pltpu.CompilerParams(vmem_limit_bytes=16 * 2**20),
        cost_estimate=pl.CostEstimate(flops=0, bytes_accessed=2 * updates * panel, transcendentals=0),
    )(update_factor)

    b_across = lax.ppermute(b_panel, "factor", [(0, 2), (1, 3)])
    b_core = by_xor(b_panel, "factor", factors, 1)
    b_far = lax.ppermute(b_panel, "factor", [(0, 3), (1, 2)])
    b_far, held = lax.optimization_barrier((b_far, held))
    (forward,) = call(
        forward_kernel,
        at_factor,
        [panel_inverse, b_panel, b_core, b_across, b_far],
        [((rows, cols), BF16)],
        2 * rows * panel * cols,
    )
    forward_across = by_xor(forward, "factor", factors, 2)
    late[3], forward_across = lax.optimization_barrier((late[3], forward_across))

    block = (cols, rows)
    at_coupled = jnp.concatenate([at_factor, spread])
    (begun,) = call(
        functools.partial(coupled_kernel, (0, 1, 2, 3), (4, 8, 9, 10)),
        at_coupled,
        [held] + early,
        [((factors,) + block, F32)],
        2 * cols * depth * 4 * panel,
    )

    def coupled(panel_block, kind):
        (out,) = call(
            functools.partial(finish_kernel, panel_block, (11, 5, 6, 7)),
            at_coupled,
            [held, begun] + late,
            [(block, kind)],
            2 * cols * depth * 4 * rows,
        )
        return out

    from_core = by_xor(coupled(3, BF16), "factor", factors, 1)
    send = (coupled(2, F32) + from_core.astype(F32)).astype(BF16)
    from_across = by_xor(send, "factor", factors, 2)
    from_core = by_xor(coupled(1, BF16), "factor", factors, 1)
    kept = coupled(0, F32)

    work = 2 * cols * rows * rows
    reduced, send = call(
        functools.partial(reduce_kernel, 3),
        at_factor,
        [forward, kept, from_core, from_across, panel_inverse],
        [(block, BF16), (block, BF16)],
        work,
    )

    halves = 2
    width = rows // halves

    def solved(panel_block, kind, pieces):
        return call(
            functools.partial(solve_kernel, panel_block),
            at_factor,
            [reduced, panel_inverse],
            [((cols, rows // pieces), kind)] * pieces,
            work,
        )

    def half(value, h):
        return value[:, h * width : (h + 1) * width].astype(F32)

    from_core = by_xor(send, "factor", factors, 1)
    kept = solved(2, F32, halves)
    from_across = [
        lax.ppermute((kept[h] + half(from_core, h)).astype(BF16), "factor", [(2, 0), (3, 1)]) for h in range(halves)
    ]
    (send,) = solved(1, BF16, 1)
    from_core = by_xor(send, "factor", factors, 1)
    kept = solved(0, F32, halves)
    forward_core = by_xor(forward, "factor", factors, 1)
    forward_far = by_xor(forward_across, "factor", factors, 1)
    (update_rhs,) = call(
        update_kernel,
        at_factor,
        [held, b_update, forward, forward_core, forward_across, forward_far],
        [((updates, cols), BF16)],
        2 * updates * panel * cols,
    )
    from_across[0], update_rhs = lax.optimization_barrier((from_across[0], update_rhs))

    def solution_half(h):
        return (kept[h] + half(from_core, h) + from_across[h].astype(F32)).astype(BF16)

    solution_t = [solution_half(0)]
    _, from_across[1] = lax.optimization_barrier((solution_t[0], from_across[1]))
    solution_t.append(solution_half(1))
    panel_solution = jnp.concatenate(solution_t, axis=1).T

    middle, ends = (2, 3, 4, 5), (0, 1, 6, 7)
    in_middle = (at_load >= 2) & (at_load < 6)

    def hop(value, places, bits):
        return lax.ppermute(value, "load", [(i, i ^ bits) for i in places])

    def gather(own, after):
        own_x = hop(own, middle + ends, 1)
        a = hop(own, middle + ends, 2)
        b = hop(own, middle + ends, 6)
        own_x, a = lax.optimization_barrier((own_x, a))
        a_x = hop(a, middle + ends, 1)
        b, a_x, after = lax.optimization_barrier((b, a_x, after))
        c = hop(a, middle, 6)
        d = hop(b, middle, 2)
        b_x = hop(b, middle + ends, 1)
        c = jnp.where(in_middle, c, d)
        return [own, own_x, a, a_x, b, b_x, c, hop(c, middle + ends, 1)], after

    at_axle = at_load ^ jnp.array([0, 1, 2, 3, 6, 7, 4, 5], jnp.int32)

    def config(first, joined, operands, width, blocks):
        (out,) = call(
            functools.partial(config_kernel, first, joined),
            at_axle,
            [axle_weights] + operands,
            [((axle_weights.shape[0], width), F32)],
            2 * axle_weights.shape[0] * cols * rows // halves * blocks,
        )
        return out

    shards, second = gather(*solution_t)
    last, _ = gather(second, second)
    before = config(0, False, shards, width, 8)
    begun = config(0, False, last[:6], width, 6)
    config_response = config(6, True, [begun, before] + last[6:], rows, 2)
    return (update_rhs, panel_solution, config_response)


def any_slice(b_panel, b_update, panel_inverse, update_factor, update_solution, axle_weights):
    b_all = lax.all_gather(b_panel, "factor", axis=0, tiled=True)
    forward = jnp.dot(panel_inverse, b_all, preferred_element_type=F32).astype(BF16)
    forward_all = lax.all_gather(forward, "factor", axis=0, tiled=True)
    lowered = jnp.dot(update_factor, forward_all, preferred_element_type=F32)
    update_rhs = (b_update.astype(F32) - lowered).astype(BF16)
    regrouped = lax.all_to_all(update_solution, "load", split_axis=1, concat_axis=0, tiled=True)
    over_rows = (((0,), (0,)), ((), ()))
    coupled = lax.psum_scatter(
        lax.dot_general(update_factor, regrouped, over_rows, preferred_element_type=F32),
        "factor",
        scatter_dimension=0,
        tiled=True,
    )
    reduced = (forward.astype(F32) - coupled).astype(BF16)
    panel_solution = lax.psum_scatter(
        lax.dot_general(panel_inverse, reduced, over_rows, preferred_element_type=F32),
        "factor",
        scatter_dimension=0,
        tiled=True,
    ).astype(BF16)
    config_response = lax.dot_general(
        axle_weights,
        lax.all_gather(panel_solution, "load", axis=1, tiled=True),
        (((1,), (1,)), ((), ())),
        preferred_element_type=F32,
    )
    return (update_rhs, panel_solution, config_response)


def solution(mesh):
    in_specs = (
        P("factor", "load"),
        P("factor", "load"),
        P("factor", None),
        P("factor", None),
        P(("factor", "load"), None),
        P("load", None),
    )
    out_specs = (P("factor", "load"), P("factor", "load"), P("load", "factor"))
    small = mesh.shape["factor"] == 4 and mesh.shape["load"] == 8
    local = small_slice if small else any_slice
    return jax.shard_map(local, mesh=mesh, in_specs=in_specs, out_specs=out_specs, check_vma=False)
```

```python
import functools

import jax
import jax.numpy as jnp
from jax import lax
from jax.experimental import pallas as pl
from jax.experimental.pallas import tpu as pltpu
from jax.sharding import PartitionSpec as P

BF16 = jnp.bfloat16
F32 = jnp.float32


VMEM = pl.BlockSpec(memory_space=pltpu.VMEM)
SMEM = pl.BlockSpec(memory_space=pltpu.SMEM)


def call(kernel, at, operands, outs, flops):
    at = [] if at is None else [at]
    shapes = [jax.ShapeDtypeStruct(shape, kind) for shape, kind in outs]
    moved = sum(v.size * v.dtype.itemsize for v in list(operands) + shapes)
    return pl.pallas_call(
        kernel,
        out_shape=shapes,
        in_specs=[SMEM] * len(at) + [VMEM] * len(operands),
        out_specs=[VMEM] * len(shapes),
        compiler_params=pltpu.CompilerParams(vmem_limit_bytes=16 * 2**20),
        cost_estimate=pl.CostEstimate(flops=flops, bytes_accessed=moved, transcendentals=0),
    )(*at, *operands)


def part(index, size):
    return pl.ds(pl.multiple_of(index * size, size), size)


def dot(a, b):
    return jnp.dot(a, b, preferred_element_type=F32)


def forward_kernel(at_ref, inverse_ref, *refs):
    blocks, out_ref = refs[:-1], refs[-1]
    rows = out_ref.shape[0]
    total = None
    for j, block in enumerate(blocks):
        term = dot(inverse_ref[:, part(at_ref[j], rows)], block[...])
        total = term if total is None else total + term
    out_ref[...] = total.astype(out_ref.dtype)


def update_kernel(at_ref, factor_ref, rhs_ref, *refs):
    blocks, out_ref = refs[:-1], refs[-1]
    rows = blocks[0].shape[0]

    @pl.loop(0, out_ref.shape[0] // rows)
    def _(i):
        here = part(i, rows)
        total = rhs_ref[here, :].astype(F32)
        for j, block in enumerate(blocks):
            total = total - dot(factor_ref[here, part(at_ref[j], rows)], block[...])
        out_ref[here, :] = total.astype(out_ref.dtype)


def turn_kernel(solved_ref, out_ref):
    cols = out_ref.shape[1]
    for j in range(out_ref.shape[0]):
        out_ref[j] = solved_ref[:, j * cols : (j + 1) * cols].T


def hold_kernel(factor_ref, out_ref, sem):
    copy = pltpu.make_async_copy(factor_ref, out_ref, sem)
    copy.start()
    copy.wait()


def coupled_kernel(panel_block, at_ref, factor_ref, solved_ref, out_ref):
    pieces, _, depth = solved_ref.shape
    cols = part(at_ref[panel_block], out_ref.shape[1])
    total = None
    for k in range(pieces):
        term = dot(solved_ref[k], factor_ref[k * depth : (k + 1) * depth, cols])
        total = term if total is None else total + term
    out_ref[...] = total.astype(out_ref.dtype)


def reduce_kernel(block, at_ref, forward_ref, kept_ref, core_ref, across_ref, inverse_ref, reduced_ref, send_ref):
    rows = reduced_ref.shape[1]
    coupled = kept_ref[...] + core_ref[...].astype(F32) + across_ref[...].astype(F32)
    reduced_ref[...] = (forward_ref[...].astype(F32).T - coupled).astype(reduced_ref.dtype)
    term = dot(reduced_ref[...], inverse_ref[:, part(at_ref[block], rows)])
    send_ref[...] = term.astype(send_ref.dtype)


def solve_kernel(block, at_ref, reduced_ref, inverse_ref, out_ref):
    term = dot(reduced_ref[...], inverse_ref[:, part(at_ref[block], out_ref.shape[1])])
    out_ref[...] = term.astype(out_ref.dtype)


def config_kernel(first, singles, at_ref, axle_ref, *refs):
    refs, out_ref = list(refs[:-1]), refs[-1]
    total = None if first == 0 else refs.pop(0)[...]
    cols = refs[0].shape[0]
    middle = at_ref[8] == 1
    shards = [ref[...] for ref in refs[:singles]]
    for inner, outer in zip(refs[singles::2], refs[singles + 1 :: 2]):
        shards.append(jnp.where(middle, inner[...], outer[...]))
    for j, shard in enumerate(shards):
        term = dot(axle_ref[:, part(at_ref[first + j], cols)], shard)
        total = term if total is None else total + term
    out_ref[...] = total


def by_xor(value, axis, size, bits):
    return lax.ppermute(value, axis, [(i, i ^ bits) for i in range(size)])


def small_slice(b_panel, b_update, panel_inverse, update_factor, update_solution, axle_weights):
    factors, loads = 4, 8
    rows = panel_inverse.shape[0]
    updates, panel = update_factor.shape
    cols = b_panel.shape[1]
    f, at_load = lax.axis_index("factor"), lax.axis_index("load")
    at_factor = f ^ jnp.arange(factors, dtype=jnp.int32)

    depth = update_solution.shape[0]
    (turned,) = call(turn_kernel, None, [update_solution], [((loads, cols, depth), BF16)], 0)
    turned, b_panel = lax.optimization_barrier((turned, b_panel))
    regrouped = lax.all_to_all(turned, "load", split_axis=0, concat_axis=0, tiled=True)
    held = pl.pallas_call(
        hold_kernel,
        out_shape=jax.ShapeDtypeStruct((updates, panel), BF16),
        in_specs=[pl.BlockSpec(memory_space=pltpu.MemorySpace.HBM)],
        out_specs=VMEM,
        scratch_shapes=[pltpu.SemaphoreType.DMA],
        compiler_params=pltpu.CompilerParams(vmem_limit_bytes=16 * 2**20),
        cost_estimate=pl.CostEstimate(flops=0, bytes_accessed=2 * updates * panel, transcendentals=0),
    )(update_factor)

    b_across = lax.ppermute(b_panel, "factor", [(0, 2), (1, 3)])
    b_core = by_xor(b_panel, "factor", factors, 1)
    b_far = lax.ppermute(b_panel, "factor", [(0, 3), (1, 2)])
    (forward,) = call(
        forward_kernel,
        at_factor,
        [panel_inverse, b_panel, b_core, b_across, b_far],
        [((rows, cols), BF16)],
        2 * rows * panel * cols,
    )
    forward_across = by_xor(forward, "factor", factors, 2)
    regrouped, held, forward_across = lax.optimization_barrier((regrouped, held, forward_across))

    block = (cols, rows)

    def coupled(panel_block, kind):
        (out,) = call(
            functools.partial(coupled_kernel, panel_block),
            at_factor,
            [held, regrouped],
            [(block, kind)],
            2 * updates * cols * rows,
        )
        return out

    from_core = by_xor(coupled(3, BF16), "factor", factors, 1)
    send = (coupled(2, F32) + from_core.astype(F32)).astype(BF16)
    from_across = by_xor(send, "factor", factors, 2)
    from_core = by_xor(coupled(1, BF16), "factor", factors, 1)
    kept = coupled(0, F32)

    work = 2 * cols * rows * rows
    reduced, send = call(
        functools.partial(reduce_kernel, 3),
        at_factor,
        [forward, kept, from_core, from_across, panel_inverse],
        [(block, BF16), (block, BF16)],
        work,
    )

    def solved(panel_block, kind):
        (out,) = call(
            functools.partial(solve_kernel, panel_block),
            at_factor,
            [reduced, panel_inverse],
            [(block, kind)],
            work,
        )
        return out

    from_core = by_xor(send, "factor", factors, 1)
    send = (solved(2, F32) + from_core.astype(F32)).astype(BF16)
    from_across = lax.ppermute(send, "factor", [(2, 0), (3, 1)])
    from_core = by_xor(solved(1, BF16), "factor", factors, 1)
    kept = solved(0, F32)
    forward_core = by_xor(forward, "factor", factors, 1)
    forward_far = by_xor(forward_across, "factor", factors, 1)
    (update_rhs,) = call(
        update_kernel,
        at_factor,
        [held, b_update, forward, forward_core, forward_across, forward_far],
        [((updates, cols), BF16)],
        2 * updates * panel * cols,
    )
    from_across, update_rhs = lax.optimization_barrier((from_across, update_rhs))
    solution_t = (kept + from_core.astype(F32) + from_across.astype(F32)).astype(BF16)
    panel_solution = solution_t.T

    middle = (2, 3, 4, 5)
    own = solution_t
    own_x = by_xor(own, "load", loads, 1)
    a = by_xor(own, "load", loads, 2)
    b = by_xor(own, "load", loads, 6)
    own_x, a = lax.optimization_barrier((own_x, a))
    a_x = by_xor(a, "load", loads, 1)
    b, a_x = lax.optimization_barrier((b, a_x))
    c = lax.ppermute(a, "load", [(i, i ^ 6) for i in middle])
    d = lax.ppermute(b, "load", [(i, i ^ 2) for i in middle])
    b_x = by_xor(b, "load", loads, 1)
    c_x = lax.ppermute(c, "load", [(i, i ^ 1) for i in middle])
    d_x = lax.ppermute(d, "load", [(i, i ^ 1) for i in (0, 1, 6, 7)])

    in_middle = ((at_load >= 2) & (at_load < 6)).astype(jnp.int32)
    at_axle = jnp.concatenate([at_load ^ jnp.array([0, 1, 2, 3, 6, 7, 4, 5], jnp.int32), in_middle[None]])
    response = [((axle_weights.shape[0], rows), F32)]
    work = axle_weights.size * rows // 4
    (begun,) = call(
        functools.partial(config_kernel, 0, 6),
        at_axle,
        [axle_weights, own, own_x, a, a_x, b, b_x, c, d],
        response,
        7 * work,
    )
    (config_response,) = call(
        functools.partial(config_kernel, 7, 0), at_axle, [axle_weights, begun, c_x, d_x], response, work
    )
    return (update_rhs, panel_solution, config_response)


def any_slice(b_panel, b_update, panel_inverse, update_factor, update_solution, axle_weights):
    b_all = lax.all_gather(b_panel, "factor", axis=0, tiled=True)
    forward = jnp.dot(panel_inverse, b_all, preferred_element_type=F32).astype(BF16)
    forward_all = lax.all_gather(forward, "factor", axis=0, tiled=True)
    lowered = jnp.dot(update_factor, forward_all, preferred_element_type=F32)
    update_rhs = (b_update.astype(F32) - lowered).astype(BF16)
    regrouped = lax.all_to_all(update_solution, "load", split_axis=1, concat_axis=0, tiled=True)
    over_rows = (((0,), (0,)), ((), ()))
    coupled = lax.psum_scatter(
        lax.dot_general(update_factor, regrouped, over_rows, preferred_element_type=F32),
        "factor",
        scatter_dimension=0,
        tiled=True,
    )
    reduced = (forward.astype(F32) - coupled).astype(BF16)
    panel_solution = lax.psum_scatter(
        lax.dot_general(panel_inverse, reduced, over_rows, preferred_element_type=F32),
        "factor",
        scatter_dimension=0,
        tiled=True,
    ).astype(BF16)
    config_response = lax.dot_general(
        axle_weights,
        lax.all_gather(panel_solution, "load", axis=1, tiled=True),
        (((1,), (1,)), ((), ())),
        preferred_element_type=F32,
    )
    return (update_rhs, panel_solution, config_response)


def solution(mesh):
    in_specs = (
        P("factor", "load"),
        P("factor", "load"),
        P("factor", None),
        P("factor", None),
        P(("factor", "load"), None),
        P("load", None),
    )
    out_specs = (P("factor", "load"), P("factor", "load"), P("load", "factor"))
    small = mesh.shape["factor"] == 4 and mesh.shape["load"] == 8
    local = small_slice if small else any_slice
    return jax.shard_map(local, mesh=mesh, in_specs=in_specs, out_specs=out_specs, check_vma=False)
```

```python
import functools

import jax
import jax.numpy as jnp
from jax import lax
from jax.experimental import pallas as pl
from jax.experimental.pallas import tpu as pltpu
from jax.sharding import PartitionSpec as P

BF16 = jnp.bfloat16
F32 = jnp.float32


VMEM = pl.BlockSpec(memory_space=pltpu.VMEM)
SMEM = pl.BlockSpec(memory_space=pltpu.SMEM)


def call(kernel, at, operands, outs, flops):
    at = [] if at is None else [at]
    shapes = [jax.ShapeDtypeStruct(shape, kind) for shape, kind in outs]
    moved = sum(v.size * v.dtype.itemsize for v in list(operands) + shapes)
    return pl.pallas_call(
        kernel,
        out_shape=shapes,
        in_specs=[SMEM] * len(at) + [VMEM] * len(operands),
        out_specs=[VMEM] * len(shapes),
        compiler_params=pltpu.CompilerParams(vmem_limit_bytes=16 * 2**20),
        cost_estimate=pl.CostEstimate(flops=flops, bytes_accessed=moved, transcendentals=0),
    )(*at, *operands)


def part(index, size):
    return pl.ds(pl.multiple_of(index * size, size), size)


def dot(a, b):
    return jnp.dot(a, b, preferred_element_type=F32)


def forward_kernel(at_ref, inverse_ref, *refs):
    blocks, out_ref = refs[:-1], refs[-1]
    rows = out_ref.shape[0]
    total = None
    for j, block in enumerate(blocks):
        term = dot(inverse_ref[:, part(at_ref[j], rows)], block[...])
        total = term if total is None else total + term
    out_ref[...] = total.astype(out_ref.dtype)


def update_kernel(at_ref, factor_ref, rhs_ref, *refs):
    blocks, out_ref = refs[:-1], refs[-1]
    rows = blocks[0].shape[0]

    @pl.loop(0, out_ref.shape[0] // rows)
    def _(i):
        here = part(i, rows)
        total = rhs_ref[here, :].astype(F32)
        for j, block in enumerate(blocks):
            total = total - dot(factor_ref[here, part(at_ref[j], rows)], block[...])
        out_ref[here, :] = total.astype(out_ref.dtype)


def turn_kernel(solved_ref, out_ref):
    cols = out_ref.shape[1]
    for j in range(out_ref.shape[0]):
        out_ref[j] = solved_ref[:, j * cols : (j + 1) * cols].T


def hold_kernel(factor_ref, out_ref, sem):
    copy = pltpu.make_async_copy(factor_ref, out_ref, sem)
    copy.start()
    copy.wait()


def coupled_kernel(panel_block, at_ref, factor_ref, solved_ref, out_ref):
    pieces, _, depth = solved_ref.shape
    cols = part(at_ref[panel_block], out_ref.shape[1])
    total = None
    for k in range(pieces):
        term = dot(solved_ref[k], factor_ref[k * depth : (k + 1) * depth, cols])
        total = term if total is None else total + term
    out_ref[...] = total.astype(out_ref.dtype)


def reduce_kernel(block, at_ref, forward_ref, kept_ref, core_ref, across_ref, inverse_ref, reduced_ref, send_ref):
    rows = reduced_ref.shape[1]
    coupled = kept_ref[...] + core_ref[...].astype(F32) + across_ref[...].astype(F32)
    reduced_ref[...] = (forward_ref[...].astype(F32).T - coupled).astype(reduced_ref.dtype)
    term = dot(reduced_ref[...], inverse_ref[:, part(at_ref[block], rows)])
    send_ref[...] = term.astype(send_ref.dtype)


def solve_kernel(block, at_ref, reduced_ref, inverse_ref, out_ref):
    term = dot(reduced_ref[...], inverse_ref[:, part(at_ref[block], out_ref.shape[1])])
    out_ref[...] = term.astype(out_ref.dtype)


def config_kernel(first, singles, at_ref, axle_ref, *refs):
    refs, out_ref = list(refs[:-1]), refs[-1]
    total = None if first == 0 else refs.pop(0)[...]
    cols = refs[0].shape[0]
    middle = at_ref[8] == 1
    shards = [ref[...] for ref in refs[:singles]]
    for inner, outer in zip(refs[singles::2], refs[singles + 1 :: 2]):
        shards.append(jnp.where(middle, inner[...], outer[...]))
    for j, shard in enumerate(shards):
        term = dot(axle_ref[:, part(at_ref[first + j], cols)], shard)
        total = term if total is None else total + term
    out_ref[...] = total


def by_xor(value, axis, size, bits):
    return lax.ppermute(value, axis, [(i, i ^ bits) for i in range(size)])


def small_slice(b_panel, b_update, panel_inverse, update_factor, update_solution, axle_weights):
    factors, loads = 4, 8
    rows = panel_inverse.shape[0]
    updates, panel = update_factor.shape
    cols = b_panel.shape[1]
    f, at_load = lax.axis_index("factor"), lax.axis_index("load")
    at_factor = f ^ jnp.arange(factors, dtype=jnp.int32)

    depth = update_solution.shape[0]
    (turned,) = call(turn_kernel, None, [update_solution], [((loads, cols, depth), BF16)], 0)
    turned, b_panel = lax.optimization_barrier((turned, b_panel))
    regrouped = lax.all_to_all(turned, "load", split_axis=0, concat_axis=0, tiled=True)
    held = pl.pallas_call(
        hold_kernel,
        out_shape=jax.ShapeDtypeStruct((updates, panel), BF16),
        in_specs=[pl.BlockSpec(memory_space=pltpu.MemorySpace.HBM)],
        out_specs=VMEM,
        scratch_shapes=[pltpu.SemaphoreType.DMA],
        compiler_params=pltpu.CompilerParams(vmem_limit_bytes=16 * 2**20),
        cost_estimate=pl.CostEstimate(flops=0, bytes_accessed=2 * updates * panel, transcendentals=0),
    )(update_factor)

    b_across = lax.ppermute(b_panel, "factor", [(0, 2), (1, 3)])
    b_core = by_xor(b_panel, "factor", factors, 1)
    b_far = lax.ppermute(b_across, "factor", [(2, 3), (3, 2)])
    b_far, held = lax.optimization_barrier((b_far, held))
    (forward,) = call(
        forward_kernel,
        at_factor,
        [panel_inverse, b_panel, b_core, b_across, b_far],
        [((rows, cols), BF16)],
        2 * rows * panel * cols,
    )
    forward_across = by_xor(forward, "factor", factors, 2)
    regrouped, forward_across = lax.optimization_barrier((regrouped, forward_across))

    block = (cols, rows)

    def coupled(panel_block, kind):
        (out,) = call(
            functools.partial(coupled_kernel, panel_block),
            at_factor,
            [held, regrouped],
            [(block, kind)],
            2 * updates * cols * rows,
        )
        return out

    from_core = by_xor(coupled(3, BF16), "factor", factors, 1)
    send = (coupled(2, F32) + from_core.astype(F32)).astype(BF16)
    from_across = by_xor(send, "factor", factors, 2)
    from_core = by_xor(coupled(1, BF16), "factor", factors, 1)
    kept = coupled(0, F32)

    work = 2 * cols * rows * rows
    reduced, send = call(
        functools.partial(reduce_kernel, 3),
        at_factor,
        [forward, kept, from_core, from_across, panel_inverse],
        [(block, BF16), (block, BF16)],
        work,
    )

    def solved(panel_block, kind):
        (out,) = call(
            functools.partial(solve_kernel, panel_block),
            at_factor,
            [reduced, panel_inverse],
            [(block, kind)],
            work,
        )
        return out

    from_core = by_xor(send, "factor", factors, 1)
    send = (solved(2, F32) + from_core.astype(F32)).astype(BF16)
    from_across = lax.ppermute(send, "factor", [(2, 0), (3, 1)])
    from_core = by_xor(solved(1, BF16), "factor", factors, 1)
    kept = solved(0, F32)
    forward_core = by_xor(forward, "factor", factors, 1)
    forward_far = by_xor(forward_across, "factor", factors, 1)
    (update_rhs,) = call(
        update_kernel,
        at_factor,
        [held, b_update, forward, forward_core, forward_across, forward_far],
        [((updates, cols), BF16)],
        2 * updates * panel * cols,
    )
    from_across, update_rhs = lax.optimization_barrier((from_across, update_rhs))
    solution_t = (kept + from_core.astype(F32) + from_across.astype(F32)).astype(BF16)
    panel_solution = solution_t.T

    middle = (2, 3, 4, 5)
    own = solution_t
    own_x = by_xor(own, "load", loads, 1)
    a = by_xor(own, "load", loads, 2)
    b = by_xor(own, "load", loads, 6)
    own_x, a = lax.optimization_barrier((own_x, a))
    a_x = by_xor(a, "load", loads, 1)
    b, a_x = lax.optimization_barrier((b, a_x))
    c = lax.ppermute(a, "load", [(i, i ^ 6) for i in middle])
    d = lax.ppermute(b, "load", [(i, i ^ 2) for i in middle])
    b_x = by_xor(b, "load", loads, 1)
    c_x = lax.ppermute(c, "load", [(i, i ^ 1) for i in middle])
    d_x = lax.ppermute(d, "load", [(i, i ^ 1) for i in (0, 1, 6, 7)])

    in_middle = ((at_load >= 2) & (at_load < 6)).astype(jnp.int32)
    at_axle = jnp.concatenate([at_load ^ jnp.array([0, 1, 2, 3, 6, 7, 4, 5], jnp.int32), in_middle[None]])
    response = [((axle_weights.shape[0], rows), F32)]
    work = axle_weights.size * rows // 4
    (begun,) = call(
        functools.partial(config_kernel, 0, 6),
        at_axle,
        [axle_weights, own, own_x, a, a_x, b, b_x, c, d],
        response,
        7 * work,
    )
    (config_response,) = call(
        functools.partial(config_kernel, 7, 0), at_axle, [axle_weights, begun, c_x, d_x], response, work
    )
    return (update_rhs, panel_solution, config_response)


def any_slice(b_panel, b_update, panel_inverse, update_factor, update_solution, axle_weights):
    b_all = lax.all_gather(b_panel, "factor", axis=0, tiled=True)
    forward = jnp.dot(panel_inverse, b_all, preferred_element_type=F32).astype(BF16)
    forward_all = lax.all_gather(forward, "factor", axis=0, tiled=True)
    lowered = jnp.dot(update_factor, forward_all, preferred_element_type=F32)
    update_rhs = (b_update.astype(F32) - lowered).astype(BF16)
    regrouped = lax.all_to_all(update_solution, "load", split_axis=1, concat_axis=0, tiled=True)
    over_rows = (((0,), (0,)), ((), ()))
    coupled = lax.psum_scatter(
        lax.dot_general(update_factor, regrouped, over_rows, preferred_element_type=F32),
        "factor",
        scatter_dimension=0,
        tiled=True,
    )
    reduced = (forward.astype(F32) - coupled).astype(BF16)
    panel_solution = lax.psum_scatter(
        lax.dot_general(panel_inverse, reduced, over_rows, preferred_element_type=F32),
        "factor",
        scatter_dimension=0,
        tiled=True,
    ).astype(BF16)
    config_response = lax.dot_general(
        axle_weights,
        lax.all_gather(panel_solution, "load", axis=1, tiled=True),
        (((1,), (1,)), ((), ())),
        preferred_element_type=F32,
    )
    return (update_rhs, panel_solution, config_response)


def solution(mesh):
    in_specs = (
        P("factor", "load"),
        P("factor", "load"),
        P("factor", None),
        P("factor", None),
        P(("factor", "load"), None),
        P("load", None),
    )
    out_specs = (P("factor", "load"), P("factor", "load"), P("load", "factor"))
    small = mesh.shape["factor"] == 4 and mesh.shape["load"] == 8
    local = small_slice if small else any_slice
    return jax.shard_map(local, mesh=mesh, in_specs=in_specs, out_specs=out_specs, check_vma=False)
```

```python
import functools

import jax
import jax.numpy as jnp
from jax import lax
from jax.experimental import pallas as pl
from jax.experimental.pallas import tpu as pltpu
from jax.sharding import PartitionSpec as P

BF16 = jnp.bfloat16
F32 = jnp.float32


VMEM = pl.BlockSpec(memory_space=pltpu.VMEM)
SMEM = pl.BlockSpec(memory_space=pltpu.SMEM)


def call(kernel, at, operands, outs, flops):
    at = [] if at is None else [at]
    shapes = [jax.ShapeDtypeStruct(shape, kind) for shape, kind in outs]
    moved = sum(v.size * v.dtype.itemsize for v in list(operands) + shapes)
    return pl.pallas_call(
        kernel,
        out_shape=shapes,
        in_specs=[SMEM] * len(at) + [VMEM] * len(operands),
        out_specs=[VMEM] * len(shapes),
        compiler_params=pltpu.CompilerParams(vmem_limit_bytes=16 * 2**20),
        cost_estimate=pl.CostEstimate(flops=flops, bytes_accessed=moved, transcendentals=0),
    )(*at, *operands)


def part(index, size):
    return pl.ds(pl.multiple_of(index * size, size), size)


def dot(a, b):
    return jnp.dot(a, b, preferred_element_type=F32)


def forward_kernel(at_ref, inverse_ref, *refs):
    blocks, out_ref = refs[:-1], refs[-1]
    rows = out_ref.shape[0]
    total = None
    for j, block in enumerate(blocks):
        term = dot(inverse_ref[:, part(at_ref[j], rows)], block[...])
        total = term if total is None else total + term
    out_ref[...] = total.astype(out_ref.dtype)


def update_kernel(at_ref, factor_ref, rhs_ref, *refs):
    blocks, out_ref = refs[:-1], refs[-1]
    total = rhs_ref[...].astype(F32)
    for j, block in enumerate(blocks):
        total = total - dot(factor_ref[:, part(at_ref[j], block.shape[0])], block[...])
    out_ref[...] = total.astype(out_ref.dtype)


def update_of(at, factor, rhs, blocks):
    (updates, panel), cols = factor.shape, rhs.shape[1]
    rows = blocks[0].shape[0]

    def here(i, at):
        return (i, 0)

    return pl.pallas_call(
        update_kernel,
        out_shape=jax.ShapeDtypeStruct((updates, cols), BF16),
        grid_spec=pltpu.PrefetchScalarGridSpec(
            num_scalar_prefetch=1,
            grid=(updates // rows,),
            in_specs=[pl.BlockSpec((rows, panel), here), pl.BlockSpec((rows, cols), here)]
            + [pl.BlockSpec((rows, cols), lambda i, at: (0, 0))] * len(blocks),
            out_specs=pl.BlockSpec((rows, cols), here),
        ),
        compiler_params=pltpu.CompilerParams(vmem_limit_bytes=57 * 2**20),
        cost_estimate=pl.CostEstimate(
            flops=2 * updates * panel * cols,
            bytes_accessed=2 * (updates * (panel + 2 * cols) + panel * cols),
            transcendentals=0,
        ),
    )(at, factor, rhs, *blocks)


def turn_kernel(solved_ref, out_ref):
    cols = out_ref.shape[1]
    for j in range(out_ref.shape[0]):
        out_ref[j] = solved_ref[:, j * cols : (j + 1) * cols].T


def coupled_kernel(at_ref, factor_ref, solved_ref, out_ref, total_ref):
    step = pl.program_id(0)
    depth = solved_ref.shape[2]
    pieces = factor_ref.shape[0] // depth
    total = jnp.where(step == 0, 0.0, total_ref[...])
    for k in range(pieces):
        total = total + dot(solved_ref[step * pieces + k], factor_ref[k * depth : (k + 1) * depth, :])
    total_ref[...] = total

    @pl.when(step == pl.num_programs(0) - 1)
    def _():
        out_ref[...] = total.astype(out_ref.dtype)


def coupled_of(panel_block, at, factor, solved, rows, kind):
    pieces, cols, depth = solved.shape
    together = 2
    return pl.pallas_call(
        coupled_kernel,
        out_shape=jax.ShapeDtypeStruct((cols, rows), kind),
        grid_spec=pltpu.PrefetchScalarGridSpec(
            num_scalar_prefetch=1,
            grid=(pieces // together,),
            in_specs=[
                pl.BlockSpec((together * depth, rows), lambda k, at: (k, at[panel_block])),
                pl.BlockSpec((pieces, cols, depth), lambda k, at: (0, 0, 0)),
            ],
            out_specs=pl.BlockSpec((cols, rows), lambda k, at: (0, 0)),
            scratch_shapes=[pltpu.VMEM((cols, rows), F32)],
        ),
        compiler_params=pltpu.CompilerParams(vmem_limit_bytes=57 * 2**20),
        cost_estimate=pl.CostEstimate(
            flops=2 * pieces * depth * cols * rows,
            bytes_accessed=2 * pieces * depth * (cols + rows) + 4 * cols * rows,
            transcendentals=0,
        ),
    )(at, factor, solved)


def reduce_kernel(block, at_ref, forward_ref, kept_ref, core_ref, across_ref, inverse_ref, reduced_ref, send_ref):
    rows = reduced_ref.shape[1]
    coupled = kept_ref[...] + core_ref[...].astype(F32) + across_ref[...].astype(F32)
    reduced_ref[...] = (forward_ref[...].astype(F32).T - coupled).astype(reduced_ref.dtype)
    term = dot(reduced_ref[...], inverse_ref[:, part(at_ref[block], rows)])
    send_ref[...] = term.astype(send_ref.dtype)


def solve_kernel(block, at_ref, reduced_ref, inverse_ref, out_ref):
    term = dot(reduced_ref[...], inverse_ref[:, part(at_ref[block], out_ref.shape[1])])
    out_ref[...] = term.astype(out_ref.dtype)


def config_kernel(first, singles, at_ref, axle_ref, *refs):
    refs, out_ref = list(refs[:-1]), refs[-1]
    total = None if first == 0 else refs.pop(0)[...]
    cols = refs[0].shape[0]
    middle = at_ref[8] == 1
    shards = [ref[...] for ref in refs[:singles]]
    for inner, outer in zip(refs[singles::2], refs[singles + 1 :: 2]):
        shards.append(jnp.where(middle, inner[...], outer[...]))
    for j, shard in enumerate(shards):
        term = dot(axle_ref[:, part(at_ref[first + j], cols)], shard)
        total = term if total is None else total + term
    out_ref[...] = total


def by_xor(value, axis, size, bits):
    return lax.ppermute(value, axis, [(i, i ^ bits) for i in range(size)])


def small_slice(b_panel, b_update, panel_inverse, update_factor, update_solution, axle_weights):
    factors, loads = 4, 8
    rows = panel_inverse.shape[0]
    updates, panel = update_factor.shape
    cols = b_panel.shape[1]
    f, at_load = lax.axis_index("factor"), lax.axis_index("load")
    at_factor = f ^ jnp.arange(factors, dtype=jnp.int32)

    depth = update_solution.shape[0]
    (turned,) = call(turn_kernel, None, [update_solution], [((loads, cols, depth), BF16)], 0)
    turned, b_panel = lax.optimization_barrier((turned, b_panel))
    regrouped = lax.all_to_all(turned, "load", split_axis=0, concat_axis=0, tiled=True)
    b_across = lax.ppermute(b_panel, "factor", [(0, 2), (1, 3)])
    b_core = by_xor(b_panel, "factor", factors, 1)
    b_far = lax.ppermute(b_across, "factor", [(2, 3), (3, 2)])
    (forward,) = call(
        forward_kernel,
        at_factor,
        [panel_inverse, b_panel, b_core, b_across, b_far],
        [((rows, cols), BF16)],
        2 * rows * panel * cols,
    )
    forward_across = by_xor(forward, "factor", factors, 2)
    regrouped, forward_across = lax.optimization_barrier((regrouped, forward_across))

    block = (cols, rows)

    def coupled(panel_block, kind):
        return coupled_of(panel_block, at_factor, update_factor, regrouped, rows, kind)

    from_core = by_xor(coupled(3, BF16), "factor", factors, 1)
    send = (coupled(2, F32) + from_core.astype(F32)).astype(BF16)
    from_across = by_xor(send, "factor", factors, 2)
    from_core = by_xor(coupled(1, BF16), "factor", factors, 1)
    kept = coupled(0, F32)

    work = 2 * cols * rows * rows
    reduced, send = call(
        functools.partial(reduce_kernel, 3),
        at_factor,
        [forward, kept, from_core, from_across, panel_inverse],
        [(block, BF16), (block, BF16)],
        work,
    )

    def solved(panel_block, kind):
        (out,) = call(
            functools.partial(solve_kernel, panel_block),
            at_factor,
            [reduced, panel_inverse],
            [(block, kind)],
            work,
        )
        return out

    from_core = by_xor(send, "factor", factors, 1)
    send = (solved(2, F32) + from_core.astype(F32)).astype(BF16)
    from_across = lax.ppermute(send, "factor", [(2, 0), (3, 1)])
    from_core = by_xor(solved(1, BF16), "factor", factors, 1)
    kept = solved(0, F32)
    forward_core = by_xor(forward, "factor", factors, 1)
    forward_far = by_xor(forward_across, "factor", factors, 1)
    update_rhs = update_of(
        at_factor, update_factor, b_update, [forward, forward_core, forward_across, forward_far]
    )
    from_across, update_rhs = lax.optimization_barrier((from_across, update_rhs))
    solution_t = (kept + from_core.astype(F32) + from_across.astype(F32)).astype(BF16)
    panel_solution = solution_t.T

    middle = (2, 3, 4, 5)
    own = solution_t
    own_x = by_xor(own, "load", loads, 1)
    a = by_xor(own, "load", loads, 2)
    b = by_xor(own, "load", loads, 6)
    own_x, a = lax.optimization_barrier((own_x, a))
    a_x = by_xor(a, "load", loads, 1)
    b, a_x = lax.optimization_barrier((b, a_x))
    c = lax.ppermute(a, "load", [(i, i ^ 6) for i in middle])
    d = lax.ppermute(b, "load", [(i, i ^ 2) for i in middle])
    b_x = by_xor(b, "load", loads, 1)
    c_x = lax.ppermute(c, "load", [(i, i ^ 1) for i in middle])
    d_x = lax.ppermute(d, "load", [(i, i ^ 1) for i in (0, 1, 6, 7)])

    in_middle = ((at_load >= 2) & (at_load < 6)).astype(jnp.int32)
    at_axle = jnp.concatenate([at_load ^ jnp.array([0, 1, 2, 3, 6, 7, 4, 5], jnp.int32), in_middle[None]])
    response = [((axle_weights.shape[0], rows), F32)]
    work = axle_weights.size * rows // 4
    (begun,) = call(
        functools.partial(config_kernel, 0, 6),
        at_axle,
        [axle_weights, own, own_x, a, a_x, b, b_x, c, d],
        response,
        7 * work,
    )
    (config_response,) = call(
        functools.partial(config_kernel, 7, 0), at_axle, [axle_weights, begun, c_x, d_x], response, work
    )
    return (update_rhs, panel_solution, config_response)


def any_slice(b_panel, b_update, panel_inverse, update_factor, update_solution, axle_weights):
    b_all = lax.all_gather(b_panel, "factor", axis=0, tiled=True)
    forward = jnp.dot(panel_inverse, b_all, preferred_element_type=F32).astype(BF16)
    forward_all = lax.all_gather(forward, "factor", axis=0, tiled=True)
    lowered = jnp.dot(update_factor, forward_all, preferred_element_type=F32)
    update_rhs = (b_update.astype(F32) - lowered).astype(BF16)
    regrouped = lax.all_to_all(update_solution, "load", split_axis=1, concat_axis=0, tiled=True)
    over_rows = (((0,), (0,)), ((), ()))
    coupled = lax.psum_scatter(
        lax.dot_general(update_factor, regrouped, over_rows, preferred_element_type=F32),
        "factor",
        scatter_dimension=0,
        tiled=True,
    )
    reduced = (forward.astype(F32) - coupled).astype(BF16)
    panel_solution = lax.psum_scatter(
        lax.dot_general(panel_inverse, reduced, over_rows, preferred_element_type=F32),
        "factor",
        scatter_dimension=0,
        tiled=True,
    ).astype(BF16)
    config_response = lax.dot_general(
        axle_weights,
        lax.all_gather(panel_solution, "load", axis=1, tiled=True),
        (((1,), (1,)), ((), ())),
        preferred_element_type=F32,
    )
    return (update_rhs, panel_solution, config_response)


def solution(mesh):
    in_specs = (
        P("factor", "load"),
        P("factor", "load"),
        P("factor", None),
        P("factor", None),
        P(("factor", "load"), None),
        P("load", None),
    )
    out_specs = (P("factor", "load"), P("factor", "load"), P("load", "factor"))
    small = mesh.shape["factor"] == 4 and mesh.shape["load"] == 8
    local = small_slice if small else any_slice
    return jax.shard_map(local, mesh=mesh, in_specs=in_specs, out_specs=out_specs, check_vma=False)
```

```python
import functools

import jax
import jax.numpy as jnp
from jax import lax
from jax.experimental import pallas as pl
from jax.experimental.pallas import tpu as pltpu
from jax.sharding import PartitionSpec as P

BF16 = jnp.bfloat16
F32 = jnp.float32


VMEM = pl.BlockSpec(memory_space=pltpu.VMEM)
SMEM = pl.BlockSpec(memory_space=pltpu.SMEM)


def call(kernel, at, operands, outs, flops):
    at = [] if at is None else [at]
    shapes = [jax.ShapeDtypeStruct(shape, kind) for shape, kind in outs]
    moved = sum(v.size * v.dtype.itemsize for v in list(operands) + shapes)
    return pl.pallas_call(
        kernel,
        out_shape=shapes,
        in_specs=[SMEM] * len(at) + [VMEM] * len(operands),
        out_specs=[VMEM] * len(shapes),
        compiler_params=pltpu.CompilerParams(vmem_limit_bytes=16 * 2**20),
        cost_estimate=pl.CostEstimate(flops=flops, bytes_accessed=moved, transcendentals=0),
    )(*at, *operands)


def part(index, size):
    return pl.ds(pl.multiple_of(index * size, size), size)


def dot(a, b):
    return jnp.dot(a, b, preferred_element_type=F32)


def forward_kernel(at_ref, inverse_ref, *refs):
    blocks, out_ref = refs[:-1], refs[-1]
    rows = out_ref.shape[0]
    total = None
    for j, block in enumerate(blocks):
        term = dot(inverse_ref[:, part(at_ref[j], rows)], block[...])
        total = term if total is None else total + term
    out_ref[...] = total.astype(out_ref.dtype)


def update_kernel(at_ref, factor_ref, rhs_ref, *refs):
    blocks, out_ref = refs[:-1], refs[-1]
    rows = blocks[0].shape[0]

    @pl.loop(0, out_ref.shape[0] // rows)
    def _(i):
        here = part(i, rows)
        total = rhs_ref[here, :].astype(F32)
        for j, block in enumerate(blocks):
            total = total - dot(factor_ref[here, part(at_ref[j], rows)], block[...])
        out_ref[here, :] = total.astype(out_ref.dtype)


def turn_kernel(solved_ref, out_ref):
    cols = out_ref.shape[1]
    for j in range(out_ref.shape[0]):
        out_ref[j] = solved_ref[:, j * cols : (j + 1) * cols].T


def coupled_kernel(at_ref, factor_ref, solved_ref, send_ref, kept_ref, held_ref, total_ref, sems):
    pieces, _, depth = solved_ref.shape
    parts, width = sems.shape[0], send_ref.shape[2]
    rows = held_ref.shape[0] // parts
    copies = []
    for k in range(parts):
        here = pl.ds(k * rows, rows)
        copies.append(pltpu.make_async_copy(factor_ref.at[here], held_ref.at[here], sems.at[k]))
        copies[k].start()
    each = pieces // parts
    for k in range(parts):
        copies[k].wait()
        for j in range(4):
            cols = part(at_ref[j], width)
            total = None if k == 0 else total_ref[j]
            for i in range(k * each, (k + 1) * each):
                term = dot(solved_ref[i], held_ref[i * depth : (i + 1) * depth, cols])
                total = term if total is None else total + term
            if k < parts - 1:
                total_ref[j] = total
            elif j % 2 == 1:
                send_ref[j // 2] = total.astype(send_ref.dtype)
            else:
                kept_ref[j // 2] = total


def coupled_of(at, factor, solved, rows):
    (updates, panel), cols = factor.shape, solved.shape[1]
    parts = 4
    return pl.pallas_call(
        coupled_kernel,
        out_shape=[jax.ShapeDtypeStruct((2, cols, rows), BF16), jax.ShapeDtypeStruct((2, cols, rows), F32)],
        in_specs=[SMEM, pl.BlockSpec(memory_space=pl.ANY), VMEM],
        out_specs=[VMEM, VMEM],
        scratch_shapes=[
            pltpu.VMEM((updates, panel), BF16),
            pltpu.VMEM((4, cols, rows), F32),
            pltpu.SemaphoreType.DMA((parts,)),
        ],
        compiler_params=pltpu.CompilerParams(vmem_limit_bytes=57 * 2**20),
        cost_estimate=pl.CostEstimate(
            flops=2 * updates * panel * cols,
            bytes_accessed=2 * updates * (panel + cols) + 6 * panel * cols,
            transcendentals=0,
        ),
    )(at, factor, solved)


def reduce_kernel(block, at_ref, forward_ref, kept_ref, core_ref, across_ref, inverse_ref, reduced_ref, send_ref):
    rows = reduced_ref.shape[1]
    coupled = kept_ref[0] + core_ref[0].astype(F32) + across_ref[...].astype(F32)
    reduced_ref[...] = (forward_ref[...].astype(F32).T - coupled).astype(reduced_ref.dtype)
    term = dot(reduced_ref[...], inverse_ref[:, part(at_ref[block], rows)])
    send_ref[...] = term.astype(send_ref.dtype)


def solve_kernel(block, at_ref, reduced_ref, inverse_ref, out_ref):
    term = dot(reduced_ref[...], inverse_ref[:, part(at_ref[block], out_ref.shape[1])])
    out_ref[...] = term.astype(out_ref.dtype)


def config_kernel(first, singles, at_ref, axle_ref, *refs):
    refs, out_ref = list(refs[:-1]), refs[-1]
    total = None if first == 0 else refs.pop(0)[...]
    cols = refs[0].shape[0]
    middle = at_ref[8] == 1
    shards = [ref[...] for ref in refs[:singles]]
    for inner, outer in zip(refs[singles::2], refs[singles + 1 :: 2]):
        shards.append(jnp.where(middle, inner[...], outer[...]))
    for j, shard in enumerate(shards):
        term = dot(axle_ref[:, part(at_ref[first + j], cols)], shard)
        total = term if total is None else total + term
    out_ref[...] = total


def by_xor(value, axis, size, bits):
    return lax.ppermute(value, axis, [(i, i ^ bits) for i in range(size)])


def small_slice(b_panel, b_update, panel_inverse, update_factor, update_solution, axle_weights):
    factors, loads = 4, 8
    rows = panel_inverse.shape[0]
    updates, panel = update_factor.shape
    cols = b_panel.shape[1]
    f, at_load = lax.axis_index("factor"), lax.axis_index("load")
    at_factor = f ^ jnp.arange(factors, dtype=jnp.int32)

    depth = update_solution.shape[0]
    (turned,) = call(turn_kernel, None, [update_solution], [((loads, cols, depth), BF16)], 0)
    turned, b_panel = lax.optimization_barrier((turned, b_panel))
    regrouped = lax.all_to_all(turned, "load", split_axis=0, concat_axis=0, tiled=True)
    b_across = lax.ppermute(b_panel, "factor", [(0, 2), (1, 3)])
    b_core = by_xor(b_panel, "factor", factors, 1)
    b_far = lax.ppermute(b_across, "factor", [(2, 3), (3, 2)])
    (forward,) = call(
        forward_kernel,
        at_factor,
        [panel_inverse, b_panel, b_core, b_across, b_far],
        [((rows, cols), BF16)],
        2 * rows * panel * cols,
    )
    forward_across = by_xor(forward, "factor", factors, 2)
    regrouped, forward_across = lax.optimization_barrier((regrouped, forward_across))

    block = (cols, rows)

    send, kept = coupled_of(at_factor, update_factor, regrouped, rows)
    from_core = by_xor(send, "factor", factors, 1)
    send = (kept[1] + from_core[1].astype(F32)).astype(BF16)
    from_across = by_xor(send, "factor", factors, 2)

    work = 2 * cols * rows * rows
    reduced, send = call(
        functools.partial(reduce_kernel, 3),
        at_factor,
        [forward, kept, from_core, from_across, panel_inverse],
        [(block, BF16), (block, BF16)],
        work,
    )

    def solved(panel_block, kind):
        (out,) = call(
            functools.partial(solve_kernel, panel_block),
            at_factor,
            [reduced, panel_inverse],
            [(block, kind)],
            work,
        )
        return out

    from_core = by_xor(send, "factor", factors, 1)
    send = (solved(2, F32) + from_core.astype(F32)).astype(BF16)
    from_across = lax.ppermute(send, "factor", [(2, 0), (3, 1)])
    from_core = by_xor(solved(1, BF16), "factor", factors, 1)
    kept = solved(0, F32)
    forward_core = by_xor(forward, "factor", factors, 1)
    forward_far = by_xor(forward_across, "factor", factors, 1)
    (update_rhs,) = call(
        update_kernel,
        at_factor,
        [update_factor, b_update, forward, forward_core, forward_across, forward_far],
        [((updates, cols), BF16)],
        2 * updates * panel * cols,
    )
    from_across, update_rhs = lax.optimization_barrier((from_across, update_rhs))
    solution_t = (kept + from_core.astype(F32) + from_across.astype(F32)).astype(BF16)
    panel_solution = solution_t.T

    middle = (2, 3, 4, 5)
    own = solution_t
    a = by_xor(own, "load", loads, 2)
    b = by_xor(own, "load", loads, 6)
    a, mine = lax.optimization_barrier((a, own))
    a_x = by_xor(a, "load", loads, 1)
    own_x = by_xor(mine, "load", loads, 1)
    b, a_x, own_x = lax.optimization_barrier((b, a_x, own_x))
    c = lax.ppermute(a, "load", [(i, i ^ 6) for i in middle])
    d = lax.ppermute(b, "load", [(i, i ^ 2) for i in middle])
    b_x = by_xor(b, "load", loads, 1)
    c_x = lax.ppermute(c, "load", [(i, i ^ 1) for i in middle])
    d_x = lax.ppermute(d, "load", [(i, i ^ 1) for i in (0, 1, 6, 7)])

    in_middle = ((at_load >= 2) & (at_load < 6)).astype(jnp.int32)
    at_axle = jnp.concatenate([at_load ^ jnp.array([0, 1, 2, 3, 6, 7, 4, 5], jnp.int32), in_middle[None]])
    response = [((axle_weights.shape[0], rows), F32)]
    work = axle_weights.size * rows // 4
    (begun,) = call(
        functools.partial(config_kernel, 0, 6),
        at_axle,
        [axle_weights, own, own_x, a, a_x, b, b_x, c, d],
        response,
        7 * work,
    )
    (config_response,) = call(
        functools.partial(config_kernel, 7, 0), at_axle, [axle_weights, begun, c_x, d_x], response, work
    )
    return (update_rhs, panel_solution, config_response)


def any_slice(b_panel, b_update, panel_inverse, update_factor, update_solution, axle_weights):
    b_all = lax.all_gather(b_panel, "factor", axis=0, tiled=True)
    forward = jnp.dot(panel_inverse, b_all, preferred_element_type=F32).astype(BF16)
    forward_all = lax.all_gather(forward, "factor", axis=0, tiled=True)
    lowered = jnp.dot(update_factor, forward_all, preferred_element_type=F32)
    update_rhs = (b_update.astype(F32) - lowered).astype(BF16)
    regrouped = lax.all_to_all(update_solution, "load", split_axis=1, concat_axis=0, tiled=True)
    over_rows = (((0,), (0,)), ((), ()))
    coupled = lax.psum_scatter(
        lax.dot_general(update_factor, regrouped, over_rows, preferred_element_type=F32),
        "factor",
        scatter_dimension=0,
        tiled=True,
    )
    reduced = (forward.astype(F32) - coupled).astype(BF16)
    panel_solution = lax.psum_scatter(
        lax.dot_general(panel_inverse, reduced, over_rows, preferred_element_type=F32),
        "factor",
        scatter_dimension=0,
        tiled=True,
    ).astype(BF16)
    config_response = lax.dot_general(
        axle_weights,
        lax.all_gather(panel_solution, "load", axis=1, tiled=True),
        (((1,), (1,)), ((), ())),
        preferred_element_type=F32,
    )
    return (update_rhs, panel_solution, config_response)


def solution(mesh):
    in_specs = (
        P("factor", "load"),
        P("factor", "load"),
        P("factor", None),
        P("factor", None),
        P(("factor", "load"), None),
        P("load", None),
    )
    out_specs = (P("factor", "load"), P("factor", "load"), P("load", "factor"))
    small = mesh.shape["factor"] == 4 and mesh.shape["load"] == 8
    local = small_slice if small else any_slice
    return jax.shard_map(local, mesh=mesh, in_specs=in_specs, out_specs=out_specs, check_vma=False)
```

```python
import functools

import jax
import jax.numpy as jnp
from jax import lax
from jax.experimental import pallas as pl
from jax.experimental.pallas import tpu as pltpu
from jax.sharding import PartitionSpec as P

BF16 = jnp.bfloat16
F32 = jnp.float32


VMEM = pl.BlockSpec(memory_space=pltpu.VMEM)
SMEM = pl.BlockSpec(memory_space=pltpu.SMEM)


def call(kernel, at, operands, outs, flops):
    at = [] if at is None else [at]
    shapes = [jax.ShapeDtypeStruct(shape, kind) for shape, kind in outs]
    moved = sum(v.size * v.dtype.itemsize for v in list(operands) + shapes)
    return pl.pallas_call(
        kernel,
        out_shape=shapes,
        in_specs=[SMEM] * len(at) + [VMEM] * len(operands),
        out_specs=[VMEM] * len(shapes),
        compiler_params=pltpu.CompilerParams(vmem_limit_bytes=16 * 2**20),
        cost_estimate=pl.CostEstimate(flops=flops, bytes_accessed=moved, transcendentals=0),
    )(*at, *operands)


def part(index, size):
    return pl.ds(pl.multiple_of(index * size, size), size)


def dot(a, b):
    return jnp.dot(a, b, preferred_element_type=F32)


def forward_kernel(at_ref, inverse_ref, *refs):
    blocks, out_ref = refs[:-1], refs[-1]
    rows = out_ref.shape[0]
    total = None
    for j, block in enumerate(blocks):
        term = dot(inverse_ref[:, part(at_ref[j], rows)], block[...])
        total = term if total is None else total + term
    out_ref[...] = total.astype(out_ref.dtype)


def update_kernel(at_ref, factor_ref, rhs_ref, *refs):
    blocks, out_ref = refs[:-1], refs[-1]
    rows = blocks[0].shape[0]

    @pl.loop(0, out_ref.shape[0] // rows)
    def _(i):
        here = part(i, rows)
        total = rhs_ref[here, :].astype(F32)
        for j, block in enumerate(blocks):
            total = total - dot(factor_ref[here, part(at_ref[j], rows)], block[...])
        out_ref[here, :] = total.astype(out_ref.dtype)


def split_kernel(at_ref, solved_ref, *outs):
    cols = outs[0].shape[0]
    for j, out_ref in enumerate(outs):
        out_ref[...] = solved_ref[:, part(at_ref[j], cols)].T


def hold_kernel(factor_ref, out_ref, sem):
    copy = pltpu.make_async_copy(factor_ref, out_ref, sem)
    copy.start()
    copy.wait()


def coupled_kernel(panel_blocks, row_blocks, at_ref, factor_ref, *refs):
    pieces, out_ref = refs[:-1], refs[-1]
    depth, width = pieces[0].shape[1], out_ref.shape[2]
    for j, b in enumerate(panel_blocks):
        cols = part(at_ref[b], width)
        total = None
        for k, piece in zip(row_blocks, pieces):
            term = dot(piece[...], factor_ref[part(at_ref[k], depth), cols])
            total = term if total is None else total + term
        out_ref[j] = total


def finish_kernel(panel_block, row_blocks, at_ref, factor_ref, begun_ref, *refs):
    pieces, out_ref = refs[:-1], refs[-1]
    depth, width = pieces[0].shape[1], out_ref.shape[1]
    total = begun_ref[panel_block]
    for k, piece in zip(row_blocks, pieces):
        total = total + dot(piece[...], factor_ref[part(at_ref[k], depth), part(at_ref[panel_block], width)])
    out_ref[...] = total.astype(out_ref.dtype)


def reduce_kernel(block, at_ref, forward_ref, kept_ref, core_ref, across_ref, inverse_ref, reduced_ref, send_ref):
    rows = reduced_ref.shape[1]
    coupled = kept_ref[...] + core_ref[...].astype(F32) + across_ref[...].astype(F32)
    reduced_ref[...] = (forward_ref[...].astype(F32).T - coupled).astype(reduced_ref.dtype)
    term = dot(reduced_ref[...], inverse_ref[:, part(at_ref[block], rows)])
    send_ref[...] = term.astype(send_ref.dtype)


def solve_kernel(block, at_ref, reduced_ref, inverse_ref, out_ref):
    term = dot(reduced_ref[...], inverse_ref[:, part(at_ref[block], out_ref.shape[1])])
    out_ref[...] = term.astype(out_ref.dtype)


def config_kernel(first, singles, at_ref, axle_ref, *refs):
    refs, out_ref = list(refs[:-1]), refs[-1]
    total = None if first == 0 else refs.pop(0)[...]
    cols = refs[0].shape[0]
    middle = at_ref[8] == 1
    shards = [ref[...] for ref in refs[:singles]]
    for inner, outer in zip(refs[singles::2], refs[singles + 1 :: 2]):
        shards.append(jnp.where(middle, inner[...], outer[...]))
    for j, shard in enumerate(shards):
        term = dot(axle_ref[:, part(at_ref[first + j], cols)], shard)
        total = term if total is None else total + term
    out_ref[...] = total


def by_xor(value, axis, size, bits):
    return lax.ppermute(value, axis, [(i, i ^ bits) for i in range(size)])


def small_slice(b_panel, b_update, panel_inverse, update_factor, update_solution, axle_weights):
    factors, loads = 4, 8
    rows = panel_inverse.shape[0]
    updates, panel = update_factor.shape
    cols = b_panel.shape[1]
    f, at_load = lax.axis_index("factor"), lax.axis_index("load")
    at_factor = f ^ jnp.arange(factors, dtype=jnp.int32)

    spread = at_load ^ jnp.arange(loads, dtype=jnp.int32)

    depth = update_solution.shape[0]
    pieces = call(split_kernel, spread, [update_solution], [((cols, depth), BF16)] * loads, 0)
    *pieces, b_panel = lax.optimization_barrier((*pieces, b_panel))
    early = [pieces[0]] + [by_xor(pieces[k], "load", loads, k) for k in (4, 5, 6)]
    late = [by_xor(pieces[7], "load", loads, 7)]
    early[1], *pieces[1:4] = lax.optimization_barrier((early[1], *pieces[1:4]))
    late += [by_xor(pieces[k], "load", loads, k) for k in (1, 2, 3)]
    held = pl.pallas_call(
        hold_kernel,
        out_shape=jax.ShapeDtypeStruct((updates, panel), BF16),
        in_specs=[pl.BlockSpec(memory_space=pltpu.MemorySpace.HBM)],
        out_specs=VMEM,
        scratch_shapes=[pltpu.SemaphoreType.DMA],
        compiler_params=pltpu.CompilerParams(vmem_limit_bytes=16 * 2**20),
        cost_estimate=pl.CostEstimate(flops=0, bytes_accessed=2 * updates * panel, transcendentals=0),
    )(update_factor)

    b_across = lax.ppermute(b_panel, "factor", [(0, 2), (1, 3)])
    b_core = by_xor(b_panel, "factor", factors, 1)
    b_far = lax.ppermute(b_panel, "factor", [(0, 3), (1, 2)])
    (forward,) = call(
        forward_kernel,
        at_factor,
        [panel_inverse, b_panel, b_core, b_across, b_far],
        [((rows, cols), BF16)],
        2 * rows * panel * cols,
    )
    forward_across = by_xor(forward, "factor", factors, 2)
    late[3], forward_across = lax.optimization_barrier((late[3], forward_across))

    block = (cols, rows)
    at_coupled = jnp.concatenate([at_factor, spread])
    (begun,) = call(
        functools.partial(coupled_kernel, (0, 1, 2, 3), (4, 8, 9, 10)),
        at_coupled,
        [held] + early,
        [((factors,) + block, F32)],
        2 * cols * depth * 4 * panel,
    )

    def coupled(panel_block, kind):
        (out,) = call(
            functools.partial(finish_kernel, panel_block, (11, 5, 6, 7)),
            at_coupled,
            [held, begun] + late,
            [(block, kind)],
            2 * cols * depth * 4 * rows,
        )
        return out

    from_core = by_xor(coupled(3, BF16), "factor", factors, 1)
    send = (coupled(2, F32) + from_core.astype(F32)).astype(BF16)
    send, late[0] = lax.optimization_barrier((send, late[0]))
    from_across = by_xor(send, "factor", factors, 2)
    from_core = by_xor(coupled(1, BF16), "factor", factors, 1)
    kept = coupled(0, F32)

    work = 2 * cols * rows * rows
    reduced, send = call(
        functools.partial(reduce_kernel, 3),
        at_factor,
        [forward, kept, from_core, from_across, panel_inverse],
        [(block, BF16), (block, BF16)],
        work,
    )

    def solved(panel_block, kind):
        (out,) = call(
            functools.partial(solve_kernel, panel_block),
            at_factor,
            [reduced, panel_inverse],
            [(block, kind)],
            work,
        )
        return out

    from_core = by_xor(send, "factor", factors, 1)
    send = (solved(2, F32) + from_core.astype(F32)).astype(BF16)
    from_across = lax.ppermute(send, "factor", [(2, 0), (3, 1)])
    from_core = by_xor(solved(1, BF16), "factor", factors, 1)
    kept = solved(0, F32)
    forward_core = by_xor(forward, "factor", factors, 1)
    forward_far = by_xor(forward_across, "factor", factors, 1)
    (update_rhs,) = call(
        update_kernel,
        at_factor,
        [held, b_update, forward, forward_core, forward_across, forward_far],
        [((updates, cols), BF16)],
        2 * updates * panel * cols,
    )
    from_across, update_rhs = lax.optimization_barrier((from_across, update_rhs))
    solution_t = (kept + from_core.astype(F32) + from_across.astype(F32)).astype(BF16)
    panel_solution = solution_t.T

    middle = (2, 3, 4, 5)
    own = solution_t
    own_x = by_xor(own, "load", loads, 1)
    a = by_xor(own, "load", loads, 2)
    b = by_xor(own, "load", loads, 6)
    own_x, a = lax.optimization_barrier((own_x, a))
    a_x = by_xor(a, "load", loads, 1)
    b, a_x = lax.optimization_barrier((b, a_x))
    c = lax.ppermute(a, "load", [(i, i ^ 6) for i in middle])
    d = lax.ppermute(b, "load", [(i, i ^ 2) for i in middle])
    b_x = by_xor(b, "load", loads, 1)
    c_x = lax.ppermute(c, "load", [(i, i ^ 1) for i in middle])
    d_x = lax.ppermute(d, "load", [(i, i ^ 1) for i in (0, 1, 6, 7)])

    in_middle = ((at_load >= 2) & (at_load < 6)).astype(jnp.int32)
    at_axle = jnp.concatenate([at_load ^ jnp.array([0, 1, 2, 3, 6, 7, 4, 5], jnp.int32), in_middle[None]])
    response = [((axle_weights.shape[0], rows), F32)]
    work = axle_weights.size * rows // 4
    (begun,) = call(
        functools.partial(config_kernel, 0, 6),
        at_axle,
        [axle_weights, own, own_x, a, a_x, b, b_x, c, d],
        response,
        7 * work,
    )
    (config_response,) = call(
        functools.partial(config_kernel, 7, 0), at_axle, [axle_weights, begun, c_x, d_x], response, work
    )
    return (update_rhs, panel_solution, config_response)


def any_slice(b_panel, b_update, panel_inverse, update_factor, update_solution, axle_weights):
    b_all = lax.all_gather(b_panel, "factor", axis=0, tiled=True)
    forward = jnp.dot(panel_inverse, b_all, preferred_element_type=F32).astype(BF16)
    forward_all = lax.all_gather(forward, "factor", axis=0, tiled=True)
    lowered = jnp.dot(update_factor, forward_all, preferred_element_type=F32)
    update_rhs = (b_update.astype(F32) - lowered).astype(BF16)
    regrouped = lax.all_to_all(update_solution, "load", split_axis=1, concat_axis=0, tiled=True)
    over_rows = (((0,), (0,)), ((), ()))
    coupled = lax.psum_scatter(
        lax.dot_general(update_factor, regrouped, over_rows, preferred_element_type=F32),
        "factor",
        scatter_dimension=0,
        tiled=True,
    )
    reduced = (forward.astype(F32) - coupled).astype(BF16)
    panel_solution = lax.psum_scatter(
        lax.dot_general(panel_inverse, reduced, over_rows, preferred_element_type=F32),
        "factor",
        scatter_dimension=0,
        tiled=True,
    ).astype(BF16)
    config_response = lax.dot_general(
        axle_weights,
        lax.all_gather(panel_solution, "load", axis=1, tiled=True),
        (((1,), (1,)), ((), ())),
        preferred_element_type=F32,
    )
    return (update_rhs, panel_solution, config_response)


def solution(mesh):
    in_specs = (
        P("factor", "load"),
        P("factor", "load"),
        P("factor", None),
        P("factor", None),
        P(("factor", "load"), None),
        P("load", None),
    )
    out_specs = (P("factor", "load"), P("factor", "load"), P("load", "factor"))
    small = mesh.shape["factor"] == 4 and mesh.shape["load"] == 8
    local = small_slice if small else any_slice
    return jax.shard_map(local, mesh=mesh, in_specs=in_specs, out_specs=out_specs, check_vma=False)
```

```python
import functools

import jax
import jax.numpy as jnp
from jax import lax
from jax.experimental import pallas as pl
from jax.experimental.pallas import tpu as pltpu
from jax.sharding import PartitionSpec as P

BF16 = jnp.bfloat16
F32 = jnp.float32


VMEM = pl.BlockSpec(memory_space=pltpu.VMEM)
SMEM = pl.BlockSpec(memory_space=pltpu.SMEM)


def call(kernel, at, operands, outs, flops):
    at = [] if at is None else [at]
    shapes = [jax.ShapeDtypeStruct(shape, kind) for shape, kind in outs]
    moved = sum(v.size * v.dtype.itemsize for v in list(operands) + shapes)
    return pl.pallas_call(
        kernel,
        out_shape=shapes,
        in_specs=[SMEM] * len(at) + [VMEM] * len(operands),
        out_specs=[VMEM] * len(shapes),
        compiler_params=pltpu.CompilerParams(vmem_limit_bytes=16 * 2**20),
        cost_estimate=pl.CostEstimate(flops=flops, bytes_accessed=moved, transcendentals=0),
    )(*at, *operands)


def part(index, size):
    return pl.ds(pl.multiple_of(index * size, size), size)


def dot(a, b):
    return jnp.dot(a, b, preferred_element_type=F32)


def forward_kernel(at_ref, inverse_ref, *refs):
    blocks, out_ref = refs[:-1], refs[-1]
    rows = out_ref.shape[0]
    total = None
    for j, block in enumerate(blocks):
        term = dot(inverse_ref[:, part(at_ref[j], rows)], block[...])
        total = term if total is None else total + term
    out_ref[...] = total.astype(out_ref.dtype)


def update_kernel(at_ref, factor_ref, rhs_ref, *refs):
    blocks, out_ref = refs[:-1], refs[-1]
    rows = blocks[0].shape[0]

    @pl.loop(0, out_ref.shape[0] // rows)
    def _(i):
        here = part(i, rows)
        total = rhs_ref[here, :].astype(F32)
        for j, block in enumerate(blocks):
            total = total - dot(factor_ref[here, part(at_ref[j], rows)], block[...])
        out_ref[here, :] = total.astype(out_ref.dtype)


def split_kernel(at_ref, solved_ref, *outs):
    cols = outs[0].shape[0]
    for j, out_ref in enumerate(outs):
        out_ref[...] = solved_ref[:, part(at_ref[j], cols)].T


def hold_kernel(factor_ref, out_ref, sem):
    copy = pltpu.make_async_copy(factor_ref, out_ref, sem)
    copy.start()
    copy.wait()


def coupled_kernel(panel_blocks, row_blocks, at_ref, factor_ref, *refs):
    pieces, out_ref = refs[:-1], refs[-1]
    depth, width = pieces[0].shape[1], out_ref.shape[2]
    for j, b in enumerate(panel_blocks):
        cols = part(at_ref[b], width)
        total = None
        for k, piece in zip(row_blocks, pieces):
            term = dot(piece[...], factor_ref[part(at_ref[k], depth), cols])
            total = term if total is None else total + term
        out_ref[j] = total


def finish_kernel(panel_block, row_blocks, at_ref, factor_ref, begun_ref, *refs):
    pieces, out_ref = refs[:-1], refs[-1]
    depth, width = pieces[0].shape[1], out_ref.shape[1]
    total = begun_ref[panel_block]
    for k, piece in zip(row_blocks, pieces):
        total = total + dot(piece[...], factor_ref[part(at_ref[k], depth), part(at_ref[panel_block], width)])
    out_ref[...] = total.astype(out_ref.dtype)


def reduce_kernel(block, at_ref, forward_ref, kept_ref, core_ref, across_ref, inverse_ref, reduced_ref, send_ref):
    rows = reduced_ref.shape[1]
    coupled = kept_ref[...] + core_ref[...].astype(F32) + across_ref[...].astype(F32)
    reduced_ref[...] = (forward_ref[...].astype(F32).T - coupled).astype(reduced_ref.dtype)
    term = dot(reduced_ref[...], inverse_ref[:, part(at_ref[block], rows)])
    send_ref[...] = term.astype(send_ref.dtype)


def solve_kernel(block, at_ref, reduced_ref, inverse_ref, out_ref):
    term = dot(reduced_ref[...], inverse_ref[:, part(at_ref[block], out_ref.shape[1])])
    out_ref[...] = term.astype(out_ref.dtype)


def config_kernel(first, singles, at_ref, axle_ref, *refs):
    refs, out_ref = list(refs[:-1]), refs[-1]
    total = None if first == 0 else refs.pop(0)[...]
    cols = refs[0].shape[0]
    middle = at_ref[8] == 1
    shards = [ref[...] for ref in refs[:singles]]
    for inner, outer in zip(refs[singles::2], refs[singles + 1 :: 2]):
        shards.append(jnp.where(middle, inner[...], outer[...]))
    for j, shard in enumerate(shards):
        term = dot(axle_ref[:, part(at_ref[first + j], cols)], shard)
        total = term if total is None else total + term
    out_ref[...] = total


def by_xor(value, axis, size, bits):
    return lax.ppermute(value, axis, [(i, i ^ bits) for i in range(size)])


def small_slice(b_panel, b_update, panel_inverse, update_factor, update_solution, axle_weights):
    factors, loads = 4, 8
    rows = panel_inverse.shape[0]
    updates, panel = update_factor.shape
    cols = b_panel.shape[1]
    f, at_load = lax.axis_index("factor"), lax.axis_index("load")
    at_factor = f ^ jnp.arange(factors, dtype=jnp.int32)

    spread = at_load ^ jnp.arange(loads, dtype=jnp.int32)

    depth = update_solution.shape[0]
    pieces = call(split_kernel, spread, [update_solution], [((cols, depth), BF16)] * loads, 0)
    *pieces, b_panel = lax.optimization_barrier((*pieces, b_panel))
    early = [pieces[0]] + [by_xor(pieces[k], "load", loads, k) for k in (4, 5, 6)]
    late = [by_xor(pieces[7], "load", loads, 7)]
    early[1], *pieces[1:4] = lax.optimization_barrier((early[1], *pieces[1:4]))
    late += [by_xor(pieces[k], "load", loads, k) for k in (1, 2, 3)]
    held = pl.pallas_call(
        hold_kernel,
        out_shape=jax.ShapeDtypeStruct((updates, panel), BF16),
        in_specs=[pl.BlockSpec(memory_space=pltpu.MemorySpace.HBM)],
        out_specs=VMEM,
        scratch_shapes=[pltpu.SemaphoreType.DMA],
        compiler_params=pltpu.CompilerParams(vmem_limit_bytes=16 * 2**20),
        cost_estimate=pl.CostEstimate(flops=0, bytes_accessed=2 * updates * panel, transcendentals=0),
    )(update_factor)

    b_across = lax.ppermute(b_panel, "factor", [(0, 2), (1, 3)])
    b_core = by_xor(b_panel, "factor", factors, 1)
    b_far = lax.ppermute(b_across, "factor", [(2, 3), (3, 2)])
    (forward,) = call(
        forward_kernel,
        at_factor,
        [panel_inverse, b_panel, b_core, b_across, b_far],
        [((rows, cols), BF16)],
        2 * rows * panel * cols,
    )
    forward_across = by_xor(forward, "factor", factors, 2)
    late[3], forward_across = lax.optimization_barrier((late[3], forward_across))

    block = (cols, rows)
    at_coupled = jnp.concatenate([at_factor, spread])
    (begun,) = call(
        functools.partial(coupled_kernel, (0, 1, 2, 3), (4, 8, 9, 10)),
        at_coupled,
        [held] + early,
        [((factors,) + block, F32)],
        2 * cols * depth * 4 * panel,
    )

    def coupled(panel_block, kind):
        (out,) = call(
            functools.partial(finish_kernel, panel_block, (11, 5, 6, 7)),
            at_coupled,
            [held, begun] + late,
            [(block, kind)],
            2 * cols * depth * 4 * rows,
        )
        return out

    from_core = by_xor(coupled(3, BF16), "factor", factors, 1)
    send = (coupled(2, F32) + from_core.astype(F32)).astype(BF16)
    send, late[0] = lax.optimization_barrier((send, late[0]))
    from_across = by_xor(send, "factor", factors, 2)
    from_core = by_xor(coupled(1, BF16), "factor", factors, 1)
    kept = coupled(0, F32)

    work = 2 * cols * rows * rows
    reduced, send = call(
        functools.partial(reduce_kernel, 3),
        at_factor,
        [forward, kept, from_core, from_across, panel_inverse],
        [(block, BF16), (block, BF16)],
        work,
    )

    def solved(panel_block, kind):
        (out,) = call(
            functools.partial(solve_kernel, panel_block),
            at_factor,
            [reduced, panel_inverse],
            [(block, kind)],
            work,
        )
        return out

    from_core = by_xor(send, "factor", factors, 1)
    send = (solved(2, F32) + from_core.astype(F32)).astype(BF16)
    from_across = lax.ppermute(send, "factor", [(2, 0), (3, 1)])
    from_core = by_xor(solved(1, BF16), "factor", factors, 1)
    kept = solved(0, F32)
    forward_core = by_xor(forward, "factor", factors, 1)
    forward_far = by_xor(forward_across, "factor", factors, 1)
    (update_rhs,) = call(
        update_kernel,
        at_factor,
        [held, b_update, forward, forward_core, forward_across, forward_far],
        [((updates, cols), BF16)],
        2 * updates * panel * cols,
    )
    from_across, update_rhs = lax.optimization_barrier((from_across, update_rhs))
    solution_t = (kept + from_core.astype(F32) + from_across.astype(F32)).astype(BF16)
    panel_solution = solution_t.T

    middle = (2, 3, 4, 5)
    own = solution_t
    own_x = by_xor(own, "load", loads, 1)
    a = by_xor(own, "load", loads, 2)
    b = by_xor(own, "load", loads, 6)
    own_x, a = lax.optimization_barrier((own_x, a))
    a_x = by_xor(a, "load", loads, 1)
    b, a_x = lax.optimization_barrier((b, a_x))
    c = lax.ppermute(a, "load", [(i, i ^ 6) for i in middle])
    d = lax.ppermute(b, "load", [(i, i ^ 2) for i in middle])
    b_x = by_xor(b, "load", loads, 1)
    c_x = lax.ppermute(c, "load", [(i, i ^ 1) for i in middle])
    d_x = lax.ppermute(d, "load", [(i, i ^ 1) for i in (0, 1, 6, 7)])

    in_middle = ((at_load >= 2) & (at_load < 6)).astype(jnp.int32)
    at_axle = jnp.concatenate([at_load ^ jnp.array([0, 1, 2, 3, 6, 7, 4, 5], jnp.int32), in_middle[None]])
    response = [((axle_weights.shape[0], rows), F32)]
    work = axle_weights.size * rows // 4
    (begun,) = call(
        functools.partial(config_kernel, 0, 6),
        at_axle,
        [axle_weights, own, own_x, a, a_x, b, b_x, c, d],
        response,
        7 * work,
    )
    (config_response,) = call(
        functools.partial(config_kernel, 7, 0), at_axle, [axle_weights, begun, c_x, d_x], response, work
    )
    return (update_rhs, panel_solution, config_response)


def any_slice(b_panel, b_update, panel_inverse, update_factor, update_solution, axle_weights):
    b_all = lax.all_gather(b_panel, "factor", axis=0, tiled=True)
    forward = jnp.dot(panel_inverse, b_all, preferred_element_type=F32).astype(BF16)
    forward_all = lax.all_gather(forward, "factor", axis=0, tiled=True)
    lowered = jnp.dot(update_factor, forward_all, preferred_element_type=F32)
    update_rhs = (b_update.astype(F32) - lowered).astype(BF16)
    regrouped = lax.all_to_all(update_solution, "load", split_axis=1, concat_axis=0, tiled=True)
    over_rows = (((0,), (0,)), ((), ()))
    coupled = lax.psum_scatter(
        lax.dot_general(update_factor, regrouped, over_rows, preferred_element_type=F32),
        "factor",
        scatter_dimension=0,
        tiled=True,
    )
    reduced = (forward.astype(F32) - coupled).astype(BF16)
    panel_solution = lax.psum_scatter(
        lax.dot_general(panel_inverse, reduced, over_rows, preferred_element_type=F32),
        "factor",
        scatter_dimension=0,
        tiled=True,
    ).astype(BF16)
    config_response = lax.dot_general(
        axle_weights,
        lax.all_gather(panel_solution, "load", axis=1, tiled=True),
        (((1,), (1,)), ((), ())),
        preferred_element_type=F32,
    )
    return (update_rhs, panel_solution, config_response)


def solution(mesh):
    in_specs = (
        P("factor", "load"),
        P("factor", "load"),
        P("factor", None),
        P("factor", None),
        P(("factor", "load"), None),
        P("load", None),
    )
    out_specs = (P("factor", "load"), P("factor", "load"), P("load", "factor"))
    small = mesh.shape["factor"] == 4 and mesh.shape["load"] == 8
    local = small_slice if small else any_slice
    return jax.shard_map(local, mesh=mesh, in_specs=in_specs, out_specs=out_specs, check_vma=False)
```

```python
import functools

import jax
import jax.numpy as jnp
from jax import lax
from jax.experimental import pallas as pl
from jax.experimental.pallas import tpu as pltpu
from jax.sharding import PartitionSpec as P

BF16 = jnp.bfloat16
F32 = jnp.float32


VMEM = pl.BlockSpec(memory_space=pltpu.VMEM)
SMEM = pl.BlockSpec(memory_space=pltpu.SMEM)


def call(kernel, at, operands, outs, flops):
    at = [] if at is None else [at]
    shapes = [jax.ShapeDtypeStruct(shape, kind) for shape, kind in outs]
    moved = sum(v.size * v.dtype.itemsize for v in list(operands) + shapes)
    return pl.pallas_call(
        kernel,
        out_shape=shapes,
        in_specs=[SMEM] * len(at) + [VMEM] * len(operands),
        out_specs=[VMEM] * len(shapes),
        compiler_params=pltpu.CompilerParams(vmem_limit_bytes=16 * 2**20),
        cost_estimate=pl.CostEstimate(flops=flops, bytes_accessed=moved, transcendentals=0),
    )(*at, *operands)


def part(index, size):
    return pl.ds(pl.multiple_of(index * size, size), size)


def dot(a, b):
    return jnp.dot(a, b, preferred_element_type=F32)


def forward_kernel(at_ref, inverse_ref, *refs):
    blocks, out_ref = refs[:-1], refs[-1]
    rows = out_ref.shape[0]
    total = None
    for j, block in enumerate(blocks):
        term = dot(inverse_ref[:, part(at_ref[j], rows)], block[...])
        total = term if total is None else total + term
    out_ref[...] = total.astype(out_ref.dtype)


def update_kernel(at_ref, factor_ref, rhs_ref, *refs):
    blocks, out_ref = refs[:-1], refs[-1]
    rows = blocks[0].shape[0]

    @pl.loop(0, out_ref.shape[0] // rows)
    def _(i):
        here = part(i, rows)
        total = rhs_ref[here, :].astype(F32)
        for j, block in enumerate(blocks):
            total = total - dot(factor_ref[here, part(at_ref[j], rows)], block[...])
        out_ref[here, :] = total.astype(out_ref.dtype)


def split_kernel(at_ref, solved_ref, *outs):
    cols = outs[0].shape[0]
    for j, out_ref in enumerate(outs):
        out_ref[...] = solved_ref[:, part(at_ref[j], cols)].T


def hold_kernel(factor_ref, out_ref, sem):
    copy = pltpu.make_async_copy(factor_ref, out_ref, sem)
    copy.start()
    copy.wait()


def coupled_kernel(panel_blocks, row_blocks, at_ref, factor_ref, *refs):
    pieces, out_ref = refs[:-1], refs[-1]
    depth, width = pieces[0].shape[1], out_ref.shape[2]
    for j, b in enumerate(panel_blocks):
        cols = part(at_ref[b], width)
        total = None
        for k, piece in zip(row_blocks, pieces):
            term = dot(piece[...], factor_ref[part(at_ref[k], depth), cols])
            total = term if total is None else total + term
        out_ref[j] = total


def finish_kernel(panel_blocks, row_blocks, at_ref, factor_ref, begun_ref, *refs):
    pieces, out_ref = refs[:-1], refs[-1]
    depth, width = pieces[0].shape[1], out_ref.shape[2]
    for j, b in enumerate(panel_blocks):
        total = begun_ref[b]
        for k, piece in zip(row_blocks, pieces):
            total = total + dot(piece[...], factor_ref[part(at_ref[k], depth), part(at_ref[b], width)])
        out_ref[j] = total.astype(out_ref.dtype)


def reduce_kernel(block, at_ref, forward_ref, kept_ref, core_ref, across_ref, inverse_ref, reduced_ref, send_ref):
    rows = reduced_ref.shape[1]
    coupled = kept_ref[0] + core_ref[0].astype(F32) + across_ref[...].astype(F32)
    reduced_ref[...] = (forward_ref[...].astype(F32).T - coupled).astype(reduced_ref.dtype)
    term = dot(reduced_ref[...], inverse_ref[:, part(at_ref[block], rows)])
    send_ref[...] = term.astype(send_ref.dtype)


def solve_kernel(block, at_ref, reduced_ref, inverse_ref, out_ref):
    term = dot(reduced_ref[...], inverse_ref[:, part(at_ref[block], out_ref.shape[1])])
    out_ref[...] = term.astype(out_ref.dtype)


def config_kernel(first, singles, at_ref, axle_ref, *refs):
    refs, out_ref = list(refs[:-1]), refs[-1]
    total = None if first == 0 else refs.pop(0)[...]
    cols = refs[0].shape[0]
    middle = at_ref[8] == 1
    shards = [ref[...] for ref in refs[:singles]]
    for inner, outer in zip(refs[singles::2], refs[singles + 1 :: 2]):
        shards.append(jnp.where(middle, inner[...], outer[...]))
    for j, shard in enumerate(shards):
        term = dot(axle_ref[:, part(at_ref[first + j], cols)], shard)
        total = term if total is None else total + term
    out_ref[...] = total


def by_xor(value, axis, size, bits):
    return lax.ppermute(value, axis, [(i, i ^ bits) for i in range(size)])


def small_slice(b_panel, b_update, panel_inverse, update_factor, update_solution, axle_weights):
    factors, loads = 4, 8
    rows = panel_inverse.shape[0]
    updates, panel = update_factor.shape
    cols = b_panel.shape[1]
    f, at_load = lax.axis_index("factor"), lax.axis_index("load")
    at_factor = f ^ jnp.arange(factors, dtype=jnp.int32)

    spread = at_load ^ jnp.arange(loads, dtype=jnp.int32)

    depth = update_solution.shape[0]
    pieces = call(split_kernel, spread, [update_solution], [((cols, depth), BF16)] * loads, 0)
    *pieces, b_panel = lax.optimization_barrier((*pieces, b_panel))
    early = [pieces[0]] + [by_xor(pieces[k], "load", loads, k) for k in (4, 5, 6)]
    late = [by_xor(pieces[7], "load", loads, 7)]
    early[1], *pieces[1:4] = lax.optimization_barrier((early[1], *pieces[1:4]))
    late += [by_xor(pieces[k], "load", loads, k) for k in (1, 2, 3)]
    held = pl.pallas_call(
        hold_kernel,
        out_shape=jax.ShapeDtypeStruct((updates, panel), BF16),
        in_specs=[pl.BlockSpec(memory_space=pltpu.MemorySpace.HBM)],
        out_specs=VMEM,
        scratch_shapes=[pltpu.SemaphoreType.DMA],
        compiler_params=pltpu.CompilerParams(vmem_limit_bytes=16 * 2**20),
        cost_estimate=pl.CostEstimate(flops=0, bytes_accessed=2 * updates * panel, transcendentals=0),
    )(update_factor)

    b_across = lax.ppermute(b_panel, "factor", [(0, 2), (1, 3)])
    b_core = by_xor(b_panel, "factor", factors, 1)
    b_far = lax.ppermute(b_panel, "factor", [(0, 3), (1, 2)])
    (forward,) = call(
        forward_kernel,
        at_factor,
        [panel_inverse, b_panel, b_core, b_across, b_far],
        [((rows, cols), BF16)],
        2 * rows * panel * cols,
    )
    forward_across = by_xor(forward, "factor", factors, 2)
    late[3], forward_across = lax.optimization_barrier((late[3], forward_across))

    block = (cols, rows)
    at_coupled = jnp.concatenate([at_factor, spread])
    (begun,) = call(
        functools.partial(coupled_kernel, (0, 1, 2, 3), (4, 8, 9, 10)),
        at_coupled,
        [held] + early,
        [((factors,) + block, F32)],
        2 * cols * depth * 4 * panel,
    )

    def coupled(panel_blocks, kind):
        (out,) = call(
            functools.partial(finish_kernel, panel_blocks, (11, 5, 6, 7)),
            at_coupled,
            [held, begun] + late,
            [((len(panel_blocks),) + block, kind)],
            2 * cols * depth * 4 * rows * len(panel_blocks),
        )
        return out

    from_core = by_xor(coupled((1, 3), BF16), "factor", factors, 1)
    kept = coupled((0, 2), F32)
    from_across = by_xor((kept[1] + from_core[1].astype(F32)).astype(BF16), "factor", factors, 2)

    work = 2 * cols * rows * rows
    reduced, send = call(
        functools.partial(reduce_kernel, 3),
        at_factor,
        [forward, kept, from_core, from_across, panel_inverse],
        [(block, BF16), (block, BF16)],
        work,
    )

    def solved(panel_block, kind):
        (out,) = call(
            functools.partial(solve_kernel, panel_block),
            at_factor,
            [reduced, panel_inverse],
            [(block, kind)],
            work,
        )
        return out

    from_core = by_xor(send, "factor", factors, 1)
    send = (solved(2, F32) + from_core.astype(F32)).astype(BF16)
    from_across = lax.ppermute(send, "factor", [(2, 0), (3, 1)])
    from_core = by_xor(solved(1, BF16), "factor", factors, 1)
    kept = solved(0, F32)
    forward_core = by_xor(forward, "factor", factors, 1)
    forward_far = by_xor(forward_across, "factor", factors, 1)
    (update_rhs,) = call(
        update_kernel,
        at_factor,
        [held, b_update, forward, forward_core, forward_across, forward_far],
        [((updates, cols), BF16)],
        2 * updates * panel * cols,
    )
    from_across, update_rhs = lax.optimization_barrier((from_across, update_rhs))
    solution_t = (kept + from_core.astype(F32) + from_across.astype(F32)).astype(BF16)
    panel_solution = solution_t.T

    middle = (2, 3, 4, 5)
    own = solution_t
    own_x = by_xor(own, "load", loads, 1)
    a = by_xor(own, "load", loads, 2)
    b = by_xor(own, "load", loads, 6)
    own_x, a = lax.optimization_barrier((own_x, a))
    a_x = by_xor(a, "load", loads, 1)
    b, a_x = lax.optimization_barrier((b, a_x))
    c = lax.ppermute(a, "load", [(i, i ^ 6) for i in middle])
    d = lax.ppermute(b, "load", [(i, i ^ 2) for i in middle])
    b_x = by_xor(b, "load", loads, 1)
    c_x = lax.ppermute(c, "load", [(i, i ^ 1) for i in middle])
    d_x = lax.ppermute(d, "load", [(i, i ^ 1) for i in (0, 1, 6, 7)])

    in_middle = ((at_load >= 2) & (at_load < 6)).astype(jnp.int32)
    at_axle = jnp.concatenate([at_load ^ jnp.array([0, 1, 2, 3, 6, 7, 4, 5], jnp.int32), in_middle[None]])
    response = [((axle_weights.shape[0], rows), F32)]
    work = axle_weights.size * rows // 4
    (begun,) = call(
        functools.partial(config_kernel, 0, 6),
        at_axle,
        [axle_weights, own, own_x, a, a_x, b, b_x, c, d],
        response,
        7 * work,
    )
    (config_response,) = call(
        functools.partial(config_kernel, 7, 0), at_axle, [axle_weights, begun, c_x, d_x], response, work
    )
    return (update_rhs, panel_solution, config_response)


def any_slice(b_panel, b_update, panel_inverse, update_factor, update_solution, axle_weights):
    b_all = lax.all_gather(b_panel, "factor", axis=0, tiled=True)
    forward = jnp.dot(panel_inverse, b_all, preferred_element_type=F32).astype(BF16)
    forward_all = lax.all_gather(forward, "factor", axis=0, tiled=True)
    lowered = jnp.dot(update_factor, forward_all, preferred_element_type=F32)
    update_rhs = (b_update.astype(F32) - lowered).astype(BF16)
    regrouped = lax.all_to_all(update_solution, "load", split_axis=1, concat_axis=0, tiled=True)
    over_rows = (((0,), (0,)), ((), ()))
    coupled = lax.psum_scatter(
        lax.dot_general(update_factor, regrouped, over_rows, preferred_element_type=F32),
        "factor",
        scatter_dimension=0,
        tiled=True,
    )
    reduced = (forward.astype(F32) - coupled).astype(BF16)
    panel_solution = lax.psum_scatter(
        lax.dot_general(panel_inverse, reduced, over_rows, preferred_element_type=F32),
        "factor",
        scatter_dimension=0,
        tiled=True,
    ).astype(BF16)
    config_response = lax.dot_general(
        axle_weights,
        lax.all_gather(panel_solution, "load", axis=1, tiled=True),
        (((1,), (1,)), ((), ())),
        preferred_element_type=F32,
    )
    return (update_rhs, panel_solution, config_response)


def solution(mesh):
    in_specs = (
        P("factor", "load"),
        P("factor", "load"),
        P("factor", None),
        P("factor", None),
        P(("factor", "load"), None),
        P("load", None),
    )
    out_specs = (P("factor", "load"), P("factor", "load"), P("load", "factor"))
    small = mesh.shape["factor"] == 4 and mesh.shape["load"] == 8
    local = small_slice if small else any_slice
    return jax.shard_map(local, mesh=mesh, in_specs=in_specs, out_specs=out_specs, check_vma=False)
```

```python
import functools

import jax
import jax.numpy as jnp
from jax import lax
from jax.experimental import pallas as pl
from jax.experimental.pallas import tpu as pltpu
from jax.sharding import PartitionSpec as P

BF16 = jnp.bfloat16
F32 = jnp.float32


VMEM = pl.BlockSpec(memory_space=pltpu.VMEM)
SMEM = pl.BlockSpec(memory_space=pltpu.SMEM)


def call(kernel, at, operands, outs, flops):
    at = [] if at is None else [at]
    shapes = [jax.ShapeDtypeStruct(shape, kind) for shape, kind in outs]
    moved = sum(v.size * v.dtype.itemsize for v in list(operands) + shapes)
    return pl.pallas_call(
        kernel,
        out_shape=shapes,
        in_specs=[SMEM] * len(at) + [VMEM] * len(operands),
        out_specs=[VMEM] * len(shapes),
        compiler_params=pltpu.CompilerParams(vmem_limit_bytes=16 * 2**20),
        cost_estimate=pl.CostEstimate(flops=flops, bytes_accessed=moved, transcendentals=0),
    )(*at, *operands)


def part(index, size):
    return pl.ds(pl.multiple_of(index * size, size), size)


def dot(a, b):
    return jnp.dot(a, b, preferred_element_type=F32)


def forward_kernel(first, at_ref, inverse_ref, *refs):
    refs, out_ref = list(refs[:-1]), refs[-1]
    rows = out_ref.shape[0]
    total = None if first == 0 else refs.pop(0)[...]
    for j, block in enumerate(refs):
        term = dot(inverse_ref[:, part(at_ref[first + j], rows)], block[...])
        total = term if total is None else total + term
    out_ref[...] = total.astype(out_ref.dtype)


def update_kernel(at_ref, factor_ref, rhs_ref, *refs):
    blocks, out_ref = refs[:-1], refs[-1]
    rows = blocks[0].shape[0]

    @pl.loop(0, out_ref.shape[0] // rows)
    def _(i):
        here = part(i, rows)
        total = rhs_ref[here, :].astype(F32)
        for j, block in enumerate(blocks):
            total = total - dot(factor_ref[here, part(at_ref[j], rows)], block[...])
        out_ref[here, :] = total.astype(out_ref.dtype)


def split_kernel(at_ref, solved_ref, *outs):
    cols = outs[0].shape[0]
    for j, out_ref in enumerate(outs):
        out_ref[...] = solved_ref[:, part(at_ref[j], cols)].T


def hold_kernel(factor_ref, out_ref, sem):
    copy = pltpu.make_async_copy(factor_ref, out_ref, sem)
    copy.start()
    copy.wait()


def coupled_kernel(panel_blocks, row_blocks, at_ref, factor_ref, *refs):
    pieces, out_ref = refs[:-1], refs[-1]
    depth, width = pieces[0].shape[1], out_ref.shape[2]
    for j, b in enumerate(panel_blocks):
        cols = part(at_ref[b], width)
        total = None
        for k, piece in zip(row_blocks, pieces):
            term = dot(piece[...], factor_ref[part(at_ref[k], depth), cols])
            total = term if total is None else total + term
        out_ref[j] = total


def finish_kernel(panel_blocks, row_blocks, at_ref, factor_ref, begun_ref, *refs):
    pieces, out_ref = refs[:-1], refs[-1]
    depth, width = pieces[0].shape[1], out_ref.shape[2]
    for j, b in enumerate(panel_blocks):
        total = begun_ref[b]
        for k, piece in zip(row_blocks, pieces):
            total = total + dot(piece[...], factor_ref[part(at_ref[k], depth), part(at_ref[b], width)])
        out_ref[j] = total.astype(out_ref.dtype)


def reduce_kernel(block, at_ref, forward_ref, kept_ref, core_ref, across_ref, inverse_ref, reduced_ref, send_ref):
    rows = reduced_ref.shape[1]
    coupled = kept_ref[0] + core_ref[0].astype(F32) + across_ref[...].astype(F32)
    reduced_ref[...] = (forward_ref[...].astype(F32).T - coupled).astype(reduced_ref.dtype)
    term = dot(reduced_ref[...], inverse_ref[:, part(at_ref[block], rows)])
    send_ref[...] = term.astype(send_ref.dtype)


def solve_kernel(block, at_ref, reduced_ref, inverse_ref, out_ref):
    term = dot(reduced_ref[...], inverse_ref[:, part(at_ref[block], out_ref.shape[1])])
    out_ref[...] = term.astype(out_ref.dtype)


def config_kernel(first, singles, at_ref, axle_ref, *refs):
    refs, out_ref = list(refs[:-1]), refs[-1]
    total = None if first == 0 else refs.pop(0)[...]
    cols = refs[0].shape[0]
    middle = at_ref[8] == 1
    shards = [ref[...] for ref in refs[:singles]]
    for inner, outer in zip(refs[singles::2], refs[singles + 1 :: 2]):
        shards.append(jnp.where(middle, inner[...], outer[...]))
    for j, shard in enumerate(shards):
        term = dot(axle_ref[:, part(at_ref[first + j], cols)], shard)
        total = term if total is None else total + term
    out_ref[...] = total


def by_xor(value, axis, size, bits):
    return lax.ppermute(value, axis, [(i, i ^ bits) for i in range(size)])


def small_slice(b_panel, b_update, panel_inverse, update_factor, update_solution, axle_weights):
    factors, loads = 4, 8
    rows = panel_inverse.shape[0]
    updates, panel = update_factor.shape
    cols = b_panel.shape[1]
    f, at_load = lax.axis_index("factor"), lax.axis_index("load")
    at_factor = f ^ jnp.arange(factors, dtype=jnp.int32)

    spread = at_load ^ jnp.arange(loads, dtype=jnp.int32)

    depth = update_solution.shape[0]
    pieces = call(split_kernel, spread, [update_solution], [((cols, depth), BF16)] * loads, 0)
    *pieces, b_panel = lax.optimization_barrier((*pieces, b_panel))
    early = [pieces[0]] + [by_xor(pieces[k], "load", loads, k) for k in (4, 5, 6)]
    late = [by_xor(pieces[7], "load", loads, 7)]
    early[1], *pieces[1:4] = lax.optimization_barrier((early[1], *pieces[1:4]))
    late += [by_xor(pieces[k], "load", loads, k) for k in (1, 2, 3)]
    held = pl.pallas_call(
        hold_kernel,
        out_shape=jax.ShapeDtypeStruct((updates, panel), BF16),
        in_specs=[pl.BlockSpec(memory_space=pltpu.MemorySpace.HBM)],
        out_specs=VMEM,
        scratch_shapes=[pltpu.SemaphoreType.DMA],
        compiler_params=pltpu.CompilerParams(vmem_limit_bytes=16 * 2**20),
        cost_estimate=pl.CostEstimate(flops=0, bytes_accessed=2 * updates * panel, transcendentals=0),
    )(update_factor)

    b_across = lax.ppermute(b_panel, "factor", [(0, 2), (1, 3)])
    b_core = by_xor(b_panel, "factor", factors, 1)
    b_far = lax.ppermute(b_panel, "factor", [(0, 3), (1, 2)])
    work = rows * panel * cols
    (begun,) = call(
        functools.partial(forward_kernel, 0),
        at_factor,
        [panel_inverse, b_panel, b_core],
        [((rows, cols), F32)],
        work,
    )
    (forward,) = call(
        functools.partial(forward_kernel, 2),
        at_factor,
        [panel_inverse, begun, b_across, b_far],
        [((rows, cols), BF16)],
        work,
    )
    forward_across = by_xor(forward, "factor", factors, 2)
    late[3], forward_across = lax.optimization_barrier((late[3], forward_across))

    block = (cols, rows)
    at_coupled = jnp.concatenate([at_factor, spread])
    (begun,) = call(
        functools.partial(coupled_kernel, (0, 1, 2, 3), (4, 8, 9, 10)),
        at_coupled,
        [held] + early,
        [((factors,) + block, F32)],
        2 * cols * depth * 4 * panel,
    )

    def coupled(panel_blocks, kind):
        (out,) = call(
            functools.partial(finish_kernel, panel_blocks, (11, 5, 6, 7)),
            at_coupled,
            [held, begun] + late,
            [((len(panel_blocks),) + block, kind)],
            2 * cols * depth * 4 * rows * len(panel_blocks),
        )
        return out

    from_core = by_xor(coupled((1, 3), BF16), "factor", factors, 1)
    kept = coupled((0, 2), F32)
    from_across = by_xor((kept[1] + from_core[1].astype(F32)).astype(BF16), "factor", factors, 2)

    work = 2 * cols * rows * rows
    reduced, send = call(
        functools.partial(reduce_kernel, 3),
        at_factor,
        [forward, kept, from_core, from_across, panel_inverse],
        [(block, BF16), (block, BF16)],
        work,
    )

    def solved(panel_block, kind):
        (out,) = call(
            functools.partial(solve_kernel, panel_block),
            at_factor,
            [reduced, panel_inverse],
            [(block, kind)],
            work,
        )
        return out

    from_core = by_xor(send, "factor", factors, 1)
    send = (solved(2, F32) + from_core.astype(F32)).astype(BF16)
    from_across = lax.ppermute(send, "factor", [(2, 0), (3, 1)])
    from_core = by_xor(solved(1, BF16), "factor", factors, 1)
    kept = solved(0, F32)
    forward_core = by_xor(forward, "factor", factors, 1)
    forward_far = by_xor(forward_across, "factor", factors, 1)
    (update_rhs,) = call(
        update_kernel,
        at_factor,
        [held, b_update, forward, forward_core, forward_across, forward_far],
        [((updates, cols), BF16)],
        2 * updates * panel * cols,
    )
    from_across, update_rhs = lax.optimization_barrier((from_across, update_rhs))
    solution_t = (kept + from_core.astype(F32) + from_across.astype(F32)).astype(BF16)
    panel_solution = solution_t.T

    middle = (2, 3, 4, 5)
    own = solution_t
    own_x = by_xor(own, "load", loads, 1)
    a = by_xor(own, "load", loads, 2)
    b = by_xor(own, "load", loads, 6)
    own_x, a = lax.optimization_barrier((own_x, a))
    a_x = by_xor(a, "load", loads, 1)
    b, a_x = lax.optimization_barrier((b, a_x))
    c = lax.ppermute(a, "load", [(i, i ^ 6) for i in middle])
    d = lax.ppermute(b, "load", [(i, i ^ 2) for i in middle])
    b_x = by_xor(b, "load", loads, 1)
    c_x = lax.ppermute(c, "load", [(i, i ^ 1) for i in middle])
    d_x = lax.ppermute(d, "load", [(i, i ^ 1) for i in (0, 1, 6, 7)])

    in_middle = ((at_load >= 2) & (at_load < 6)).astype(jnp.int32)
    at_axle = jnp.concatenate([at_load ^ jnp.array([0, 1, 2, 3, 6, 7, 4, 5], jnp.int32), in_middle[None]])
    response = [((axle_weights.shape[0], rows), F32)]
    work = axle_weights.size * rows // 4
    (begun,) = call(
        functools.partial(config_kernel, 0, 6),
        at_axle,
        [axle_weights, own, own_x, a, a_x, b, b_x, c, d],
        response,
        7 * work,
    )
    (config_response,) = call(
        functools.partial(config_kernel, 7, 0), at_axle, [axle_weights, begun, c_x, d_x], response, work
    )
    return (update_rhs, panel_solution, config_response)


def any_slice(b_panel, b_update, panel_inverse, update_factor, update_solution, axle_weights):
    b_all = lax.all_gather(b_panel, "factor", axis=0, tiled=True)
    forward = jnp.dot(panel_inverse, b_all, preferred_element_type=F32).astype(BF16)
    forward_all = lax.all_gather(forward, "factor", axis=0, tiled=True)
    lowered = jnp.dot(update_factor, forward_all, preferred_element_type=F32)
    update_rhs = (b_update.astype(F32) - lowered).astype(BF16)
    regrouped = lax.all_to_all(update_solution, "load", split_axis=1, concat_axis=0, tiled=True)
    over_rows = (((0,), (0,)), ((), ()))
    coupled = lax.psum_scatter(
        lax.dot_general(update_factor, regrouped, over_rows, preferred_element_type=F32),
        "factor",
        scatter_dimension=0,
        tiled=True,
    )
    reduced = (forward.astype(F32) - coupled).astype(BF16)
    panel_solution = lax.psum_scatter(
        lax.dot_general(panel_inverse, reduced, over_rows, preferred_element_type=F32),
        "factor",
        scatter_dimension=0,
        tiled=True,
    ).astype(BF16)
    config_response = lax.dot_general(
        axle_weights,
        lax.all_gather(panel_solution, "load", axis=1, tiled=True),
        (((1,), (1,)), ((), ())),
        preferred_element_type=F32,
    )
    return (update_rhs, panel_solution, config_response)


def solution(mesh):
    in_specs = (
        P("factor", "load"),
        P("factor", "load"),
        P("factor", None),
        P("factor", None),
        P(("factor", "load"), None),
        P("load", None),
    )
    out_specs = (P("factor", "load"), P("factor", "load"), P("load", "factor"))
    small = mesh.shape["factor"] == 4 and mesh.shape["load"] == 8
    local = small_slice if small else any_slice
    return jax.shard_map(local, mesh=mesh, in_specs=in_specs, out_specs=out_specs, check_vma=False)
```

```python
import functools

import jax
import jax.numpy as jnp
from jax import lax
from jax.experimental import pallas as pl
from jax.experimental.pallas import tpu as pltpu
from jax.sharding import PartitionSpec as P

BF16 = jnp.bfloat16
F32 = jnp.float32


VMEM = pl.BlockSpec(memory_space=pltpu.VMEM)
SMEM = pl.BlockSpec(memory_space=pltpu.SMEM)


def call(kernel, at, operands, outs, flops):
    at = [] if at is None else [at]
    shapes = [jax.ShapeDtypeStruct(shape, kind) for shape, kind in outs]
    moved = sum(v.size * v.dtype.itemsize for v in list(operands) + shapes)
    return pl.pallas_call(
        kernel,
        out_shape=shapes,
        in_specs=[SMEM] * len(at) + [VMEM] * len(operands),
        out_specs=[VMEM] * len(shapes),
        compiler_params=pltpu.CompilerParams(vmem_limit_bytes=16 * 2**20),
        cost_estimate=pl.CostEstimate(flops=flops, bytes_accessed=moved, transcendentals=0),
    )(*at, *operands)


def part(index, size):
    return pl.ds(pl.multiple_of(index * size, size), size)


def dot(a, b):
    return jnp.dot(a, b, preferred_element_type=F32)


def forward_kernel(first, at_ref, inverse_ref, *refs):
    refs, out_ref = list(refs[:-1]), refs[-1]
    rows = out_ref.shape[0]
    total = None if first == 0 else refs.pop(0)[...]
    for j, block in enumerate(refs):
        term = dot(inverse_ref[:, part(at_ref[first + j], rows)], block[...])
        total = term if total is None else total + term
    out_ref[...] = total.astype(out_ref.dtype)


def update_kernel(at_ref, factor_ref, rhs_ref, *refs):
    blocks, out_ref = refs[:-1], refs[-1]
    rows = blocks[0].shape[0]

    @pl.loop(0, out_ref.shape[0] // rows)
    def _(i):
        here = part(i, rows)
        total = rhs_ref[here, :].astype(F32)
        for j, block in enumerate(blocks):
            total = total - dot(factor_ref[here, part(at_ref[j], rows)], block[...])
        out_ref[here, :] = total.astype(out_ref.dtype)


def split_kernel(at_ref, solved_ref, *outs):
    cols = outs[0].shape[0]
    for j, out_ref in enumerate(outs):
        out_ref[...] = solved_ref[:, part(at_ref[j], cols)].T


def hold_kernel(factor_ref, out_ref, sem):
    copy = pltpu.make_async_copy(factor_ref, out_ref, sem)
    copy.start()
    copy.wait()


def coupled_kernel(panel_blocks, row_blocks, at_ref, factor_ref, *refs):
    pieces, out_ref = refs[:-1], refs[-1]
    depth, width = pieces[0].shape[1], out_ref.shape[2]
    for j, b in enumerate(panel_blocks):
        cols = part(at_ref[b], width)
        total = None
        for k, piece in zip(row_blocks, pieces):
            term = dot(piece[...], factor_ref[part(at_ref[k], depth), cols])
            total = term if total is None else total + term
        out_ref[j] = total


def finish_kernel(panel_blocks, row_blocks, at_ref, factor_ref, begun_ref, *refs):
    pieces, out_ref = refs[:-1], refs[-1]
    depth, width = pieces[0].shape[1], out_ref.shape[2]
    for j, b in enumerate(panel_blocks):
        total = begun_ref[b]
        for k, piece in zip(row_blocks, pieces):
            total = total + dot(piece[...], factor_ref[part(at_ref[k], depth), part(at_ref[b], width)])
        out_ref[j] = total.astype(out_ref.dtype)


def reduce_kernel(block, at_ref, forward_ref, kept_ref, core_ref, across_ref, inverse_ref, reduced_ref, send_ref):
    rows = reduced_ref.shape[1]
    coupled = kept_ref[0] + core_ref[0].astype(F32) + across_ref[...].astype(F32)
    reduced_ref[...] = (forward_ref[...].astype(F32).T - coupled).astype(reduced_ref.dtype)
    term = dot(reduced_ref[...], inverse_ref[:, part(at_ref[block], rows)])
    send_ref[...] = term.astype(send_ref.dtype)


def solve_kernel(block, at_ref, reduced_ref, inverse_ref, out_ref):
    term = dot(reduced_ref[...], inverse_ref[:, part(at_ref[block], out_ref.shape[1])])
    out_ref[...] = term.astype(out_ref.dtype)


def config_kernel(first, singles, at_ref, axle_ref, *refs):
    refs, out_ref = list(refs[:-1]), refs[-1]
    total = None if first == 0 else refs.pop(0)[...]
    cols = refs[0].shape[0]
    middle = at_ref[8] == 1
    shards = [ref[...] for ref in refs[:singles]]
    for inner, outer in zip(refs[singles::2], refs[singles + 1 :: 2]):
        shards.append(jnp.where(middle, inner[...], outer[...]))
    for j, shard in enumerate(shards):
        term = dot(axle_ref[:, part(at_ref[first + j], cols)], shard)
        total = term if total is None else total + term
    out_ref[...] = total


def by_xor(value, axis, size, bits):
    return lax.ppermute(value, axis, [(i, i ^ bits) for i in range(size)])


def small_slice(b_panel, b_update, panel_inverse, update_factor, update_solution, axle_weights):
    factors, loads = 4, 8
    rows = panel_inverse.shape[0]
    updates, panel = update_factor.shape
    cols = b_panel.shape[1]
    f, at_load = lax.axis_index("factor"), lax.axis_index("load")
    at_factor = f ^ jnp.arange(factors, dtype=jnp.int32)

    spread = at_load ^ jnp.arange(loads, dtype=jnp.int32)

    depth = update_solution.shape[0]
    pieces = call(split_kernel, spread, [update_solution], [((cols, depth), BF16)] * loads, 0)
    *pieces, b_panel = lax.optimization_barrier((*pieces, b_panel))
    early = [pieces[0]] + [by_xor(pieces[k], "load", loads, k) for k in (4, 5, 6)]
    late = [by_xor(pieces[7], "load", loads, 7)]
    held = pl.pallas_call(
        hold_kernel,
        out_shape=jax.ShapeDtypeStruct((updates, panel), BF16),
        in_specs=[pl.BlockSpec(memory_space=pltpu.MemorySpace.HBM)],
        out_specs=VMEM,
        scratch_shapes=[pltpu.SemaphoreType.DMA],
        compiler_params=pltpu.CompilerParams(vmem_limit_bytes=16 * 2**20),
        cost_estimate=pl.CostEstimate(flops=0, bytes_accessed=2 * updates * panel, transcendentals=0),
    )(update_factor)
    early[1], *pieces[1:4] = lax.optimization_barrier((early[1], *pieces[1:4]))
    pieces[3], held = lax.optimization_barrier((pieces[3], held))
    late += [by_xor(pieces[k], "load", loads, k) for k in (1, 2, 3)]

    b_across = lax.ppermute(b_panel, "factor", [(0, 2), (1, 3)])
    b_core = by_xor(b_panel, "factor", factors, 1)
    b_far = lax.ppermute(b_panel, "factor", [(0, 3), (1, 2)])
    work = rows * panel * cols
    (begun,) = call(
        functools.partial(forward_kernel, 0),
        at_factor,
        [panel_inverse, b_panel, b_core],
        [((rows, cols), F32)],
        work,
    )
    (forward,) = call(
        functools.partial(forward_kernel, 2),
        at_factor,
        [panel_inverse, begun, b_across, b_far],
        [((rows, cols), BF16)],
        work,
    )
    forward_across = by_xor(forward, "factor", factors, 2)
    late[3], forward_across = lax.optimization_barrier((late[3], forward_across))

    block = (cols, rows)
    at_coupled = jnp.concatenate([at_factor, spread])
    (begun,) = call(
        functools.partial(coupled_kernel, (0, 1, 2, 3), (4, 8, 9, 10)),
        at_coupled,
        [held] + early,
        [((factors,) + block, F32)],
        2 * cols * depth * 4 * panel,
    )

    def coupled(panel_blocks, kind):
        (out,) = call(
            functools.partial(finish_kernel, panel_blocks, (11, 5, 6, 7)),
            at_coupled,
            [held, begun] + late,
            [((len(panel_blocks),) + block, kind)],
            2 * cols * depth * 4 * rows * len(panel_blocks),
        )
        return out

    from_core = by_xor(coupled((1, 3), BF16), "factor", factors, 1)
    kept = coupled((0, 2), F32)
    from_across = by_xor((kept[1] + from_core[1].astype(F32)).astype(BF16), "factor", factors, 2)

    work = 2 * cols * rows * rows
    reduced, send = call(
        functools.partial(reduce_kernel, 3),
        at_factor,
        [forward, kept, from_core, from_across, panel_inverse],
        [(block, BF16), (block, BF16)],
        work,
    )

    def solved(panel_block, kind):
        (out,) = call(
            functools.partial(solve_kernel, panel_block),
            at_factor,
            [reduced, panel_inverse],
            [(block, kind)],
            work,
        )
        return out

    from_core = by_xor(send, "factor", factors, 1)
    send = (solved(2, F32) + from_core.astype(F32)).astype(BF16)
    from_across = lax.ppermute(send, "factor", [(2, 0), (3, 1)])
    from_core = by_xor(solved(1, BF16), "factor", factors, 1)
    kept = solved(0, F32)
    forward_core = by_xor(forward, "factor", factors, 1)
    forward_far = by_xor(forward_across, "factor", factors, 1)
    (update_rhs,) = call(
        update_kernel,
        at_factor,
        [held, b_update, forward, forward_core, forward_across, forward_far],
        [((updates, cols), BF16)],
        2 * updates * panel * cols,
    )
    from_across, update_rhs = lax.optimization_barrier((from_across, update_rhs))
    solution_t = (kept + from_core.astype(F32) + from_across.astype(F32)).astype(BF16)
    panel_solution = solution_t.T

    middle = (2, 3, 4, 5)
    own = solution_t
    own_x = by_xor(own, "load", loads, 1)
    a = by_xor(own, "load", loads, 2)
    b = by_xor(own, "load", loads, 6)
    own_x, a = lax.optimization_barrier((own_x, a))
    a_x = by_xor(a, "load", loads, 1)
    b, a_x = lax.optimization_barrier((b, a_x))
    c = lax.ppermute(a, "load", [(i, i ^ 6) for i in middle])
    d = lax.ppermute(b, "load", [(i, i ^ 2) for i in middle])
    b_x = by_xor(b, "load", loads, 1)
    c_x = lax.ppermute(c, "load", [(i, i ^ 1) for i in middle])
    d_x = lax.ppermute(d, "load", [(i, i ^ 1) for i in (0, 1, 6, 7)])

    in_middle = ((at_load >= 2) & (at_load < 6)).astype(jnp.int32)
    at_axle = jnp.concatenate([at_load ^ jnp.array([0, 1, 2, 3, 6, 7, 4, 5], jnp.int32), in_middle[None]])
    response = [((axle_weights.shape[0], rows), F32)]
    work = axle_weights.size * rows // 4
    (begun,) = call(
        functools.partial(config_kernel, 0, 6),
        at_axle,
        [axle_weights, own, own_x, a, a_x, b, b_x, c, d],
        response,
        7 * work,
    )
    (config_response,) = call(
        functools.partial(config_kernel, 7, 0), at_axle, [axle_weights, begun, c_x, d_x], response, work
    )
    return (update_rhs, panel_solution, config_response)


def any_slice(b_panel, b_update, panel_inverse, update_factor, update_solution, axle_weights):
    b_all = lax.all_gather(b_panel, "factor", axis=0, tiled=True)
    forward = jnp.dot(panel_inverse, b_all, preferred_element_type=F32).astype(BF16)
    forward_all = lax.all_gather(forward, "factor", axis=0, tiled=True)
    lowered = jnp.dot(update_factor, forward_all, preferred_element_type=F32)
    update_rhs = (b_update.astype(F32) - lowered).astype(BF16)
    regrouped = lax.all_to_all(update_solution, "load", split_axis=1, concat_axis=0, tiled=True)
    over_rows = (((0,), (0,)), ((), ()))
    coupled = lax.psum_scatter(
        lax.dot_general(update_factor, regrouped, over_rows, preferred_element_type=F32),
        "factor",
        scatter_dimension=0,
        tiled=True,
    )
    reduced = (forward.astype(F32) - coupled).astype(BF16)
    panel_solution = lax.psum_scatter(
        lax.dot_general(panel_inverse, reduced, over_rows, preferred_element_type=F32),
        "factor",
        scatter_dimension=0,
        tiled=True,
    ).astype(BF16)
    config_response = lax.dot_general(
        axle_weights,
        lax.all_gather(panel_solution, "load", axis=1, tiled=True),
        (((1,), (1,)), ((), ())),
        preferred_element_type=F32,
    )
    return (update_rhs, panel_solution, config_response)


def solution(mesh):
    in_specs = (
        P("factor", "load"),
        P("factor", "load"),
        P("factor", None),
        P("factor", None),
        P(("factor", "load"), None),
        P("load", None),
    )
    out_specs = (P("factor", "load"), P("factor", "load"), P("load", "factor"))
    small = mesh.shape["factor"] == 4 and mesh.shape["load"] == 8
    local = small_slice if small else any_slice
    return jax.shard_map(local, mesh=mesh, in_specs=in_specs, out_specs=out_specs, check_vma=False)
```
